32 devices in a mesh: row: 16 (over z, y, core), ch: 2 (over x).
Axes of the slice: x: 2, y: 2, z: 4, core: 2. Of those that a mesh axis runs over, the one named last changes fastest.
Arguments:
- pair_act: bfloat16 [256, 256, 128], P('row', 'ch'), may hold values from -240 to 240
- cotangent: bfloat16 [256, 256, 128], P('row', 'ch'), may hold values from -6 to 6
- in_gain: float32 [128], replicated, may hold values from 0.25 to 1.75
- in_bias: float32 [128], replicated, may hold values from -3 to 3
- proj_weight: bfloat16 [128, 640], replicated, may hold values from -0.5 to 0.5
- out_gain: float32 [128], replicated, may hold values from 0.25 to 1.75
- out_bias: float32 [128], replicated, may hold values from -3 to 3
- out_weight: bfloat16 [128, 128], replicated, may hold values from -0.5 to 0.5
Outputs:
- grad_pair: bfloat16 [256, 256, 128], P('row', 'ch')
The draws below stay inside these ranges and needn't reach their ends.
All inputs are finite; a program needn't handle non-finite values.
Results may differ from the reference program's by a relative error of at most 0.0072.
Values may be sent and summed in bfloat16 or wider, within the bound.
No kernel may reach another device: no remote copies, remote signals or barrier semaphores. Data moves between devices by JAX's collectives and lax.ppermute only.
A program may use at most 64 MiB of HBM per device.

```python
import math
import jax
import jax.numpy as jnp
from jax import lax

C = 128
N = 256


def draw_pair_act(key, part):
    key = jax.random.fold_in(key, 7)
    noise_key, pair_key, chan_key = jax.random.split(key, 3)
    pair_scale = jnp.exp(jax.random.uniform(pair_key, (N, N, 1), jnp.float32) * math.log(10.0))
    chan_scale = jnp.exp(jax.random.uniform(chan_key, (1, 1, C), jnp.float32) * math.log(4.0))
    noise_field = jnp.clip(jax.random.normal(noise_key, (N, N, C), jnp.float32), -6.0, 6.0)
    return (noise_field * pair_scale * chan_scale).astype(jnp.bfloat16)


def block_levels(rng, dims, cuts, low, high):
    loudness = 1.0
    for position, shards_of in cuts:
        heights = jax.random.uniform(jax.random.fold_in(jax.random.fold_in(rng, 6), position), (shards_of,), jnp.float32, low / len(cuts), high / len(cuts))
        loudness = loudness * jnp.repeat(jnp.exp(heights), dims[position] // shards_of).reshape((-1,) + (1,) * (len(dims) - 1 - position))
    return loudness


def normal_values(key, shape, width, most, pieces=(), kind=jnp.bfloat16):
    drawn = jax.random.normal(key, shape, jnp.float32) * width
    if len(pieces) > 0:
        drawn = block_levels(key, shape, pieces, -0.22, 0.18) * drawn
    return jnp.clip(drawn, min=-most, max=most).astype(kind)


def setup_inputs(seed: int = 0) -> dict:
    arg_keys = jax.random.split(jax.random.key(seed), 9)
    return {
        "pair_act": draw_pair_act(jax.random.fold_in(arg_keys[8], 71), 0),
        "cotangent": normal_values(arg_keys[1], (N, N, C), 1.0, 6.0, ((0, 16), (1, 2))),
        "in_gain": jnp.clip(1.0 + 0.15 * jax.random.normal(arg_keys[2], (C,), jnp.float32), 0.25, 1.75),
        "in_bias": normal_values(arg_keys[3], (C,), 0.5, 3.0, (), jnp.float32),
        "proj_weight": normal_values(arg_keys[4], (C, 5 * C), C ** -0.5, 0.5),
        "out_gain": jnp.clip(1.0 + 0.15 * jax.random.normal(arg_keys[5], (C,), jnp.float32), 0.25, 1.75),
        "out_bias": normal_values(arg_keys[6], (C,), 0.5, 3.0, (), jnp.float32),
        "out_weight": normal_values(arg_keys[7], (C, C), C ** -0.5, 0.5),
    }


EPSILON = 1e-05

def to_half(values):
    return lax.optimization_barrier(values.astype(jnp.bfloat16))

def normalize(values):
    center = lax.optimization_barrier(jnp.mean(values, axis=-1, keepdims=True))
    shifted = values - center
    scale_inv = lax.rsqrt(lax.optimization_barrier(jnp.mean(shifted * shifted, axis=-1, keepdims=True)) + EPSILON)
    return (shifted * scale_inv, scale_inv)

def norm_back(grad_hat, normed, scale_inv):
    first = lax.optimization_barrier(jnp.mean(grad_hat, axis=-1, keepdims=True))
    second = lax.optimization_barrier(jnp.mean(grad_hat * normed, axis=-1, keepdims=True))
    return scale_inv * (grad_hat - first - normed * second)

def reference(pair_act, cotangent, in_gain, in_bias, proj_weight, out_gain, out_bias, out_weight):
    flat = pair_act.astype(jnp.float32).reshape(N * N, C)
    normed, scale_inv = normalize(flat)
    normal_in = (normed * in_gain + in_bias).astype(jnp.bfloat16)
    projected = jnp.dot(normal_in, proj_weight, preferred_element_type=jnp.float32)
    left_val, left_gate, right_val, right_gate, out_logit = jnp.split(projected, 5, axis=-1)
    left_sig = jax.nn.sigmoid(left_gate)
    right_sig = jax.nn.sigmoid(right_gate)
    left_fac = to_half(left_sig * left_val).astype(jnp.float32).reshape(N, N, C)
    right_fac = to_half(right_sig * right_val).astype(jnp.float32).reshape(N, N, C)
    product = jnp.einsum('ikc,jkc->ijc', left_fac, right_fac, precision=lax.Precision.HIGHEST)
    tri_flat = to_half(product).astype(jnp.float32).reshape(N * N, C)
    tri_hat, tri_inv = normalize(tri_flat)
    normal_out = (tri_hat * out_gain + out_bias).astype(jnp.bfloat16)
    mixed = jnp.dot(normal_out, out_weight, preferred_element_type=jnp.float32)
    out_gate = jax.nn.sigmoid(out_logit)
    grad_out = cotangent.astype(jnp.float32).reshape(N * N, C)
    grad_mixed = (grad_out * out_gate).astype(jnp.bfloat16)
    grad_logit = grad_out * mixed * out_gate * (1.0 - out_gate)
    grad_normal = jnp.dot(grad_mixed, out_weight.T, preferred_element_type=jnp.float32)
    grad_tri = to_half(norm_back(grad_normal * out_gain, tri_hat, tri_inv)).astype(jnp.float32).reshape(N, N, C)
    left_sum = jnp.einsum('ijc,jkc->ikc', grad_tri, right_fac, precision=lax.Precision.HIGHEST)
    right_sum = jnp.einsum('ijc,ikc->jkc', grad_tri, left_fac, precision=lax.Precision.HIGHEST)
    grad_left = to_half(left_sum).astype(jnp.float32).reshape(N * N, C)
    grad_right = to_half(right_sum).astype(jnp.float32).reshape(N * N, C)
    grad_proj = jnp.concatenate([grad_left * left_sig, grad_left * left_val * left_sig * (1.0 - left_sig), grad_right * right_sig, grad_right * right_val * right_sig * (1.0 - right_sig), grad_logit], axis=-1).astype(jnp.bfloat16)
    grad_in = jnp.dot(grad_proj, proj_weight.T, preferred_element_type=jnp.float32)
    grad_pair = norm_back(grad_in * in_gain, normed, scale_inv)
    return grad_pair.astype(jnp.bfloat16).reshape(N, N, C)
```

```python
import functools
import math

import jax
import jax.numpy as jnp
from jax import lax
from jax.experimental import pallas as pl
from jax.experimental.pallas import tpu as pltpu
from jax.sharding import PartitionSpec as P

EPSILON = 1e-05
F32 = jnp.float32
BF16 = jnp.bfloat16
UNROLL = 4
BLOCK = 256
PARTS = 4


def dot(a, b, da, db):
    return lax.dot_general(a, b, (((da,), (db,)), ((), ())), preferred_element_type=F32)


def sigmoid(values):
    return 0.5 * jnp.tanh(0.5 * values) + 0.5


def normalize(values, axis):
    center = jnp.mean(values, axis=axis, keepdims=True)
    shifted = values - center
    scale_inv = lax.rsqrt(jnp.mean(shifted * shifted, axis=axis, keepdims=True) + EPSILON)
    return (shifted * scale_inv, scale_inv)


def norm_back(grad_hat, normed, scale_inv, axis):
    first = jnp.mean(grad_hat, axis=axis, keepdims=True)
    second = jnp.mean(grad_hat * normed, axis=axis, keepdims=True)
    return scale_inv * (grad_hat - first - normed * second)


def column(row, width):
    return jnp.broadcast_to(row, (width, row.shape[-1])).T


def call(kernel, outs, scratch, *args, hbm=0, limit=16):
    single = not isinstance(outs, (list, tuple))
    args = [pltpu.with_memory_space_constraint(a, pltpu.HBM) if n < hbm else a for n, a in enumerate(args)]
    specs = [pl.BlockSpec(memory_space=pltpu.HBM if n < hbm else pltpu.VMEM) for n in range(len(args))]
    out_specs = [
        pl.BlockSpec(memory_space=getattr(out, "memory_space", pltpu.VMEM))
        for out in ([outs] if single else outs)
    ]
    return pl.pallas_call(
        kernel,
        out_shape=outs if single else tuple(outs),
        in_specs=specs,
        out_specs=out_specs[0] if single else tuple(out_specs),
        scratch_shapes=scratch,
        compiler_params=pltpu.CompilerParams(vmem_limit_bytes=limit * 1024 * 1024),
    )(*args)


def permutation(outer, inner):
    to = lax.broadcasted_iota(jnp.int32, (BLOCK, BLOCK), 0)
    start = lax.broadcasted_iota(jnp.int32, (BLOCK, BLOCK), 1)
    return (start == to % inner * outer + to // inner).astype(F32).astype(BF16)


def identity(size):
    first = lax.broadcasted_iota(jnp.int32, (size, size), 0)
    return (first == lax.broadcasted_iota(jnp.int32, (size, size), 1)).astype(F32).astype(BF16)


def swapped(swap, blocks):
    cols = blocks[0].shape[-1]
    wide = jnp.concatenate([block.reshape(BLOCK, cols) for block in blocks], axis=1)
    wide = dot(swap, wide, 1, 0).astype(BF16)
    return [wide[:, n * cols : (n + 1) * cols] for n in range(len(blocks))]


def fetched(sources, targets, sems):
    copies = [
        pltpu.make_async_copy(source, target, sems.at[n])
        for n, (source, target) in enumerate(zip(sources, targets))
    ]
    for copy in copies:
        copy.start()
    for copy in copies:
        copy.wait()


def weight_copies(w_hbm, w_ref, first, sems):
    width = w_hbm.shape[0]
    return [
        pltpu.make_async_copy(
            w_hbm.at[:, (first + n) * width : (first + n + 1) * width],
            w_ref.at[:, n * width : (n + 1) * width],
            sems.at[n],
        )
        for n in range(2)
    ]


def right_kernel(
    lay, x_hbm, gain_hbm, bias_hbm, w_hbm, r_hbm, n_ref, x_ref, gain_ref, bias_ref, w_ref, wt_ref, r_ref, right_ref, sems, out_sems
):
    rows, cols, width = x_ref.shape
    mine = width // lay.half
    parts = sems.shape[0] - 4
    size = rows // parts

    def fetch(p):
        here = pl.ds(p * size, size)
        return pltpu.make_async_copy(x_hbm.at[here], x_ref.at[here], sems.at[4 + p])

    small = [
        pltpu.make_async_copy(gain_hbm, gain_ref, sems.at[2]),
        pltpu.make_async_copy(bias_hbm, bias_ref, sems.at[3]),
    ]
    weights = weight_copies(w_hbm, w_ref, 2, sems)
    fetch(0).start()
    for copy in small + weights:
        copy.start()
    for p in range(1, parts):
        fetch(p).start()
    group = BLOCK // rows
    swap = permutation(group, rows)

    def normal(p):
        fetch(p).wait()
        for n in range(0, size, 2):
            i = p * size + n
            x = dot(eye, x_ref[pl.ds(i, 2)].reshape(2 * cols, width), 1, 1)
            normed, _s = normalize(x, 0)
            n_ref[p * size // 2 + n // 2] = (normed * gain + bias).astype(BF16)

    def project(p):
        for n in range(0, size, 2):
            i = p * size + n
            proj = dot(wt_ref[...], n_ref[p * size // 2 + n // 2], 1, 0)
            right = (sigmoid(proj[width:]) * proj[:width]).astype(BF16)
            for m in range(2):
                r_ref[i + m] = right[:, m * cols : (m + 1) * cols]

    def body(p, _):
        normal(p)
        project(p - 1)
        return 0

    eye = identity(width)
    for copy in small:
        copy.wait()
    gain = column(gain_ref[...], 2 * cols)
    bias = column(bias_ref[...], 2 * cols)
    normal(0)
    for copy in weights:
        copy.wait()
    wt_ref[...] = w_ref[...].astype(F32).T.astype(BF16)
    lax.fori_loop(1, parts, body, 0)
    project(parts - 1)
    out = []
    blocks = places(width, mine, rows)
    for k in range(0, len(blocks), 2):
        pair = blocks[k : k + 2]
        for (to, _here), right in zip(pair, swapped(swap, [r_ref[:, here] for _to, here in pair])):
            right_ref[to] = right.reshape(group // mine, mine, rows, cols)
            for share in range(to.start, to.stop):
                for n, device in enumerate(lay.order):
                    if lay.inside.index(device % lay.half) == share:
                        out.append(pltpu.make_async_copy(right_ref.at[share], r_hbm.at[n], out_sems.at[n]))
                        out[-1].start()
    for copy in out:
        copy.wait()


def left_kernel(lay, w_hbm, n_ref, mine_out, mate_out, w_ref, wt_ref, l_ref, left_ref, sems):
    rows, width, cols = l_ref.shape
    mine = width // lay.half
    group = BLOCK // rows
    weights = weight_copies(w_hbm, w_ref, 0, sems)
    for copy in weights:
        copy.start()
    for copy in weights:
        copy.wait()
    wt_ref[...] = w_ref[...].astype(F32).T.astype(BF16)
    swap = permutation(group, rows)

    def body(n, _):
        proj = dot(wt_ref[...], n_ref[n], 1, 0)
        left = (sigmoid(proj[width:]) * proj[:width]).astype(BF16)
        for m in range(2):
            l_ref[2 * n + m] = left[:, m * cols : (m + 1) * cols]
        return 0

    lax.fori_loop(0, rows // 2, body, 0, unroll=2)
    blocks = places(width, mine, rows)
    for k in range(0, len(blocks), 2):
        pair = blocks[k : k + 2]
        for (to, _here), left in zip(pair, swapped(swap, [l_ref[:, here] for _to, here in pair])):
            left_ref[to] = left.reshape(group // mine, mine, rows, cols)
    for n, s in enumerate(lay.hops):
        mine_out[n] = left_ref[lay.share(s)]
        mate_out[n] = left_ref[lay.share(s ^ lay.mate)]


def gate_kernel(*refs):
    sources, (h_ref, fac_hbm, fac_ref, wt_ref), targets, (sems, out_sems) = (
        refs[:7],
        refs[7:11],
        refs[11:18],
        refs[18:],
    )
    x_ref, cot_ref, gain_ref, bias_ref, w_ref, ogain_ref, ow_ref = targets
    rows, cols, width = x_ref.shape
    fetched(sources, targets, sems)
    wt_ref[...] = w_ref[:, : 4 * width].astype(F32).T.astype(BF16)
    ogain = column(ogain_ref[...], cols)

    def body(i, _):
        normed, _s = normalize(x_ref[i].astype(F32), -1)
        normal_in = (normed * gain_ref[...] + bias_ref[...]).astype(BF16)
        proj = dot(wt_ref[...], normal_in, 1, 1)
        for side in range(2):
            val = proj[2 * side * width : (2 * side + 1) * width]
            sig = sigmoid(proj[(2 * side + 1) * width : (2 * side + 2) * width])
            fac_ref[i, 2 * side * width : (2 * side + 1) * width] = sig.astype(BF16)
            fac_ref[i, (2 * side + 1) * width : (2 * side + 2) * width] = (
                val * sig * (1.0 - sig)
            ).astype(BF16)
        out_gate = sigmoid(dot(normal_in, w_ref[:, 4 * width :], 1, 0))
        grad_mixed = (cot_ref[i].astype(F32) * out_gate).astype(BF16)
        h_ref[i] = dot(ow_ref[...], grad_mixed, 1, 1) * ogain
        return 0

    size = rows // PARTS

    def send(p):
        here = pl.ds(p * size, size)
        return pltpu.make_async_copy(fac_ref.at[here], fac_hbm.at[here], out_sems.at[p])

    def part(p, _):
        for n in range(size):
            body(p * size + n, 0)
        send(p).start()
        return 0

    lax.fori_loop(0, PARTS, part, 0)
    for p in range(PARTS):
        send(p).wait()


def places(n_channels, mine, rows):
    group = BLOCK // rows
    return [
        (slice(c // mine, (c + group) // mine), slice(c, c + group)) for c in range(0, n_channels, group)
    ]


def to_rows(t_ref, ts_ref):
    rows, width, cols = ts_ref.shape
    mine = t_ref.shape[1]
    group = BLOCK // rows
    swap = permutation(rows, group)
    blocks = places(width, mine, rows)
    for n in range(0, len(blocks), 2):
        pair = blocks[n : n + 2]
        for (_to, here), block in zip(pair, swapped(swap, [t_ref[to] for to, _here in pair])):
            ts_ref[:, here] = block.reshape(rows, group, cols)


def tri_back_kernel(t_ref, h_ref, gt_ref, t_hbm, ts_ref, gs_ref, sem):
    rows, width, cols = h_ref.shape
    mine = t_ref.shape[1]
    group = BLOCK // rows
    copy = pltpu.make_async_copy(t_ref, t_hbm, sem)
    copy.start()
    back = permutation(group, rows)
    to_rows(t_ref, ts_ref)

    def body(i, _):
        tri, h = ts_ref[i].astype(F32), h_ref[i]
        shifted = tri - jnp.mean(tri, axis=0, keepdims=True)
        first = jnp.mean(h, axis=0, keepdims=True)
        both = jnp.mean(h * shifted, axis=0, keepdims=True)
        tri_inv = lax.rsqrt(jnp.mean(shifted * shifted, axis=0, keepdims=True) + EPSILON)
        gs_ref[i] = (tri_inv * (h - first - shifted * (both * tri_inv * tri_inv))).astype(BF16)
        return 0

    lax.fori_loop(0, rows, body, 0, unroll=UNROLL)
    blocks = places(width, mine, rows)
    for n in range(0, len(blocks), 2):
        pair = blocks[n : n + 2]
        for (to, _here), block in zip(pair, swapped(back, [gs_ref[:, here] for _to, here in pair])):
            gt_ref[to] = block.reshape(group // mine, mine, rows, cols)
    copy.wait()


def logit_kernel(*refs):
    (fac_hbm, *sources), refs = refs[:10], refs[10:]
    (gin0_ref, nt0_ref, fac0_ref, gin_hbm, nt_hbm, s_ref), refs = refs[:6], refs[6:]
    (ts_ref, gin_ref, nt_ref, out_sems), targets, sems = refs[:4], refs[4:13], refs[13]
    t_ref, x_ref, cot_ref, gain_ref, bias_ref, w_ref, ogain_ref, obias_ref, ow_ref = targets
    rows, cols, width = x_ref.shape
    first = pl.ds(0, nt0_ref.shape[0])
    fetched([*sources, fac_hbm.at[first]], [*targets, fac0_ref], sems)
    to_rows(t_ref, ts_ref)
    ogain = column(ogain_ref[...], cols)
    obias = column(obias_ref[...], cols)

    def body(i, _):
        normed, scale_inv = normalize(x_ref[i].astype(F32), -1)
        normal_in = (normed * gain_ref[...] + bias_ref[...]).astype(BF16)
        out_gate = sigmoid(dot(normal_in, w_ref[:, 4 * width :], 1, 0))
        tri_hat, _s = normalize(ts_ref[i].astype(F32), 0)
        normal_out = (tri_hat * ogain + obias).astype(BF16)
        mixed = dot(normal_out, ow_ref[...], 0, 0)
        grad_logit = cot_ref[i].astype(F32) * mixed * out_gate * (1.0 - out_gate)
        gin_ref[i] = dot(w_ref[:, 4 * width :], grad_logit.astype(BF16), 1, 1)
        nt_ref[i] = normed.T.astype(BF16)
        s_ref[pl.ds(i, 1), :] = jnp.broadcast_to(scale_inv, (cols, width)).T[:1]
        return 0

    lax.fori_loop(0, rows, body, 0, unroll=UNROLL)
    gin0_ref[...] = gin_ref[first]
    nt0_ref[...] = nt_ref[first]
    copies = [
        pltpu.make_async_copy(gin_ref, gin_hbm, out_sems.at[0]),
        pltpu.make_async_copy(nt_ref, nt_hbm, out_sems.at[1]),
    ]
    for copy in copies:
        copy.start()
    for copy in copies:
        copy.wait()


def pair_kernel(
    lay, fac_hbm, nt_hbm, gin_hbm, fac0_ref, nt0_ref, gin0_ref, r_ref, s_ref, gain_ref, w_ref, *refs
):
    l_refs, refs = refs[: lay.n_hops], refs[lay.n_hops :]
    out_hbm, l_ref, ls_ref, rs_ref, fac_ref, nt_ref, gin_ref, out_ref, sems = refs
    rows, cols, width = out_ref.shape
    mine = width // lay.half
    parts = sems.shape[1]
    size = rows // parts

    def fetch(p):
        here = pl.ds(p * size, size)
        return [
            pltpu.make_async_copy(fac_hbm.at[here], fac_ref.at[here], sems.at[0, p]),
            pltpu.make_async_copy(nt_hbm.at[here], nt_ref.at[here], sems.at[1, p]),
            pltpu.make_async_copy(gin_hbm.at[here], gin_ref.at[here], sems.at[2, p]),
        ]

    def send(p):
        here = pl.ds(p * size, size)
        return pltpu.make_async_copy(out_ref.at[here], out_hbm.at[here], sems.at[3, p])

    for p in range(1, parts):
        for copy in fetch(p):
            copy.start()
    gain = column(gain_ref[...], cols)
    eye = identity(cols)
    group = BLOCK // rows
    swap = permutation(rows, group)
    for s, source in lay.received(l_refs):
        l_ref[lay.share(s)] = source[...]
    for to, here in places(width, mine, rows):
        sums = []
        for share in range(to.start, to.stop):
            one, two = (
                r_ref[n].astype(F32)
                for n, device in enumerate(lay.order)
                if lay.inside.index(device % lay.half) == share
            )
            sums.append((one + two).astype(BF16))
        left, right = swapped(swap, [l_ref[to], jnp.stack(sums)])
        ls_ref[:, here] = left.reshape(rows, group, cols)
        rs_ref[:, here] = right.reshape(rows, group, cols)

    def part(p, fac_here, nt_here, gin_here):
        for n in range(0, size, 2):
            i = p * size + n
            blocks = []
            for m in range(2):
                left, right, fac = ls_ref[i + m], rs_ref[i + m], fac_here[i + m]
                blocks.append(
                    jnp.concatenate(
                        [
                            left * fac[:width],
                            left * fac[width : 2 * width],
                            right * fac[2 * width : 3 * width],
                            right * fac[3 * width :],
                        ],
                        axis=0,
                    )
                )
            grad_in = dot(w_ref[:, : 4 * width], jnp.concatenate(blocks, axis=1), 1, 0)
            for m in range(2):
                grad = (grad_in[:, m * cols : (m + 1) * cols] + gin_here[i + m]) * gain
                scale_inv = s_ref[pl.ds(i + m, 1), :]
                normed = nt_here[i + m].astype(F32)
                result = norm_back(grad, normed, scale_inv, 0).astype(BF16)
                out_ref[i + m] = dot(eye, result, 1, 1).astype(BF16)

    def body(p, _):
        for copy in fetch(p):
            copy.wait()
        part(p, fac_ref, nt_ref, gin_ref)
        send(p).start()
        return 0

    part(0, fac0_ref, nt0_ref, gin0_ref)
    send(0).start()
    lax.fori_loop(1, parts, body, 0)
    for p in range(parts):
        send(p).wait()


class Layout:
    def __init__(self, n_row, n_ch):
        self.n_row, self.n_ch = n_row, n_ch
        self.devices = n_row * n_ch
        self.half = self.devices // 2
        outer = math.isqrt(n_row)
        self.inner = self.devices // outer
        self.order = [o * self.inner + n for n in range(self.inner) for o in range(outer)]
        self.inside = [o * self.inner + n for n in range(self.inner) for o in range(outer // 2)]
        self.mate = n_ch
        self.hops = [s for s in range(self.half) if s & self.mate == 0]
        self.hops[1:] = self.hops[:0:-1]
        self.n_hops = len(self.hops) + 1
        self.all_place = self.place(self.order, n_row)
        self.half_place = self.place(self.inside, n_row // 2)
        self.near_place = self.place(list(range(self.half)), n_row // 2)

    def place(self, order, n_row):
        return [[order.index(r * self.n_ch + b) for b in range(self.n_ch)] for r in range(n_row)]

    def other(self, s):
        me = lax.axis_index("row") * self.n_ch + lax.axis_index("ch")
        return jnp.bitwise_xor(lax.rem(me, self.half), s)

    def share(self, s):
        other = self.other(s)
        return lax.rem(other, self.inner) * (self.half // self.inner) + lax.div(other, self.inner)

    def exchange_all(self, blocks):
        return lax.all_to_all(
            blocks, ("row", "ch"), split_axis=0, concat_axis=0, tiled=True, axis_index_groups=[self.order]
        )

    def exchange_half(self, blocks):
        groups = [[first + n for n in self.inside] for first in (0, self.half)]
        return lax.all_to_all(
            blocks, ("row", "ch"), split_axis=0, concat_axis=0, tiled=True, axis_index_groups=groups
        )

    def swap(self, block, s):
        return lax.ppermute(block, ("row", "ch"), [(n, n ^ s) for n in range(self.devices)])

    def permute(self, mine, mates):
        mates = self.swap(mates, self.mate)
        shape = jax.ShapeDtypeStruct((2,) + mine.shape[1:], mine.dtype)
        pairs = call(merge_kernel, [shape] * (len(self.hops) - 1), [], mine, mates)
        return [mine, mates] + [self.swap(pair, s) for pair, s in zip(pairs, self.hops[1:])]

    def received(self, refs):
        mine, mates, *pairs = refs
        found = [(0, mine.at[0]), (self.mate, mates.at[0])]
        for s, pair in zip(self.hops[1:], pairs):
            found += [(s, pair.at[0]), (s ^ self.mate, pair.at[1])]
        return found


def merge_kernel(mine_ref, mates_ref, *outs):
    for n, out_ref in enumerate(outs, 1):
        out_ref[0] = mine_ref[n]
        out_ref[1] = mates_ref[n]


def plane(ref, place, c):
    return jnp.concatenate(
        [
            jnp.concatenate([ref[n, c] for n in column_of], axis=0)
            for column_of in zip(*place)
        ],
        axis=1,
    )


def store_plane(ref, place, c, value):
    rows, cols = ref.shape[-2:]
    for r, row_of in enumerate(place):
        for b, n in enumerate(row_of):
            ref[n, c] = value[r * rows : (r + 1) * rows, b * cols : (b + 1) * cols]


def tri_kernel(lay, r_ref, *refs):
    l_refs, (t_ref, l_ref) = refs[: lay.n_hops], refs[lay.n_hops :]
    for s, source in lay.received(l_refs):
        l_ref[lay.other(s)] = source[...]
    for c in range(t_ref.shape[1]):
        tri = dot(plane(l_ref, lay.near_place, c), plane(r_ref, lay.all_place, c), 1, 1)
        store_plane(t_ref, lay.half_place, c, tri.astype(BF16))


def factor_back_kernel(lay, gt_ref, l_ref, r_ref, gr_hbm, *refs):
    mine_out, mate_out, gl_ref, gr_ref, sems = refs
    copies = []
    for c in range(gt_ref.shape[1]):
        right = dot(plane(gt_ref, lay.half_place, c), plane(l_ref, lay.near_place, c), 0, 0)
        store_plane(gr_ref, lay.all_place, c, right.astype(BF16))
        here = (slice(None), c)
        copies.append(pltpu.make_async_copy(gr_ref.at[here], gr_hbm.at[here], sems.at[c]))
        copies[-1].start()
    for c in range(gt_ref.shape[1]):
        left = dot(plane(gt_ref, lay.half_place, c), plane(r_ref, lay.all_place, c), 1, 0)
        store_plane(gl_ref, lay.near_place, c, left.astype(BF16))
    for n, s in enumerate(lay.hops):
        mine_out[n] = gl_ref[lay.other(s)]
        mate_out[n] = gl_ref[lay.other(s ^ lay.mate)]
    for copy in copies:
        copy.wait()


def by_channel(
    n_row, n_ch, pair_act, cotangent, in_gain, in_bias, proj_weight, out_gain, out_bias, out_weight
):
    lay = Layout(n_row, n_ch)
    rows, cols, width = pair_act.shape
    mine = width // lay.half
    struct = jax.ShapeDtypeStruct
    half = pltpu.VMEM((rows, width, cols), BF16)
    weight_t = pltpu.VMEM((4 * width, width), BF16)
    in_gain, in_bias, out_gain, out_bias = (
        v.reshape(1, width) for v in (in_gain, in_bias, out_gain, out_bias)
    )

    some = struct((len(lay.hops), mine, rows, cols), BF16)
    one = struct((lay.half, mine, rows, cols), BF16)
    one_here = pltpu.VMEM(one.shape, BF16)
    two_shape = (lay.devices, mine, rows, cols)
    row = pltpu.VMEM((1, width), F32)
    weight = pltpu.VMEM(proj_weight.shape, BF16)
    out_weight_here = pltpu.VMEM((width, width), BF16)
    both_weights = pltpu.VMEM((width, 2 * width), BF16)
    both_turned = pltpu.VMEM((2 * width, width), BF16)
    right, normal_in = call(
        functools.partial(right_kernel, lay),
        [pltpu.HBM(two_shape, BF16), struct((rows // 2, width, 2 * cols), BF16)],
        [
            half,
            row,
            row,
            both_weights,
            both_turned,
            half,
            one_here,
            pltpu.SemaphoreType.DMA((4 + PARTS,)),
            pltpu.SemaphoreType.DMA((lay.devices,)),
        ],
        pair_act,
        in_gain,
        in_bias,
        proj_weight,
        hbm=4,
    )
    left = call(
        functools.partial(left_kernel, lay),
        [some, some],
        [both_weights, both_turned, half, one_here, pltpu.SemaphoreType.DMA((2,))],
        proj_weight,
        normal_in,
        hbm=1,
    )
    right = lay.exchange_all(right)
    left = lay.permute(*left)
    h, fac = call(
        gate_kernel,
        [pltpu.VMEM((rows, width, cols), F32), pltpu.HBM((rows, 4 * width, cols), BF16)],
        [
            pltpu.VMEM((rows, 4 * width, cols), BF16),
            weight_t,
            half,
            half,
            row,
            row,
            weight,
            row,
            out_weight_here,
            pltpu.SemaphoreType.DMA((7,)),
            pltpu.SemaphoreType.DMA((PARTS,)),
        ],
        pair_act,
        cotangent,
        in_gain,
        in_bias,
        proj_weight,
        out_gain,
        out_weight,
        hbm=7,
    )
    right, h, fac = lax.optimization_barrier((right, h, fac))
    tri, left = call(functools.partial(tri_kernel, lay), [one, one], [], right, *left)
    tri = lay.exchange_half(tri)
    grad_tri, tri = call(
        tri_back_kernel,
        [one, pltpu.HBM(one.shape, BF16)],
        [half, half, pltpu.SemaphoreType.DMA(())],
        tri,
        h,
    )
    grad_right, *grad_left = call(
        functools.partial(factor_back_kernel, lay),
        [pltpu.HBM(two_shape, BF16), some, some],
        [one_here, pltpu.VMEM(two_shape, BF16), pltpu.SemaphoreType.DMA((mine,))],
        lay.exchange_half(grad_tri),
        left,
        right,
    )
    grad_right = lay.exchange_all(grad_right)
    grad_left = lay.permute(*grad_left)
    grad_in_first, normed_first, fac_first, grad_in, normed_t, scale = call(
        logit_kernel,
        [
            pltpu.VMEM((rows // PARTS, width, cols), F32),
            pltpu.VMEM((rows // PARTS, width, cols), BF16),
            pltpu.VMEM((rows // PARTS, 4 * width, cols), BF16),
            pltpu.HBM((rows, width, cols), F32),
            pltpu.HBM((rows, width, cols), BF16),
            pltpu.VMEM((rows, cols), F32),
        ],
        [
            half,
            pltpu.VMEM((rows, width, cols), F32),
            half,
            pltpu.SemaphoreType.DMA((2,)),
            one_here,
            half,
            half,
            row,
            row,
            weight,
            row,
            row,
            out_weight_here,
            pltpu.SemaphoreType.DMA((10,)),
        ],
        fac,
        tri,
        pair_act,
        cotangent,
        in_gain,
        in_bias,
        proj_weight,
        out_gain,
        out_bias,
        out_weight,
        hbm=10,
    )
    return call(
        functools.partial(pair_kernel, lay),
        pltpu.HBM((rows, cols, width), BF16),
        [
            one_here,
            half,
            half,
            pltpu.VMEM((rows, 4 * width, cols), BF16),
            half,
            pltpu.VMEM((rows, width, cols), F32),
            half,
            pltpu.SemaphoreType.DMA((4, PARTS)),
        ],
        fac,
        normed_t,
        grad_in,
        fac_first,
        normed_first,
        grad_in_first,
        grad_right,
        scale,
        in_gain,
        proj_weight,
        *grad_left,
        hbm=3,
    )


def by_row(
    pair_act, cotangent, in_gain, in_bias, proj_weight, out_gain, out_bias, out_weight
):
    rows_here, cols_here, width = pair_act.shape
    flat = pair_act.astype(jnp.float32).reshape(rows_here * cols_here, width)
    normed, scale_inv = normalize(flat, -1)
    normal_in = (normed * in_gain + in_bias).astype(jnp.bfloat16)
    projected = jnp.einsum("pd,de->ep", normal_in, proj_weight, preferred_element_type=jnp.float32)
    blocks = jnp.split(projected, 5, axis=0)
    left_sig = jax.nn.sigmoid(blocks[1])
    right_sig = jax.nn.sigmoid(blocks[3])
    left_fac = (left_sig * blocks[0]).astype(jnp.bfloat16).reshape(width, rows_here, cols_here)
    right_fac = (right_sig * blocks[2]).astype(jnp.bfloat16).reshape(width, rows_here, cols_here)
    left_chan, right_chan = (
        lax.all_to_all(left_fac, "ch", split_axis=0, concat_axis=2, tiled=True),
        lax.all_to_all(right_fac, "ch", split_axis=0, concat_axis=2, tiled=True),
    )
    tri_chan = jnp.einsum(
        "cik,cjk->cij",
        left_chan,
        lax.all_gather(right_chan, "row", axis=1, tiled=True),
        preferred_element_type=jnp.float32,
    ).astype(jnp.bfloat16)
    tri_back = lax.all_to_all(tri_chan, "ch", split_axis=2, concat_axis=0, tiled=True)
    tri_hat, tri_inv = normalize(tri_back.astype(jnp.float32).reshape(width, -1), 0)
    normal_out = (tri_hat * out_gain[:, None] + out_bias[:, None]).astype(jnp.bfloat16)
    mixed = jnp.einsum("cp,ce->ep", normal_out, out_weight, preferred_element_type=jnp.float32)
    out_gate = jax.nn.sigmoid(blocks[4])
    grad_out = cotangent.astype(jnp.float32).reshape(rows_here * cols_here, width).T
    grad_mixed = (grad_out * out_gate).astype(jnp.bfloat16)
    grad_logit = grad_out * mixed * out_gate * (1.0 - out_gate)
    grad_normal = jnp.einsum(
        "ep,ce->cp", grad_mixed, out_weight, preferred_element_type=jnp.float32
    )
    grad_tri = norm_back(grad_normal * out_gain[:, None], tri_hat, tri_inv, 0)
    grad_tri = grad_tri.astype(jnp.bfloat16).reshape(width, rows_here, cols_here)
    grad_chan = lax.all_to_all(grad_tri, "ch", split_axis=0, concat_axis=2, tiled=True)
    grad_cols = lax.all_to_all(grad_chan, "row", split_axis=2, concat_axis=1, tiled=True)
    grad_left = jnp.einsum(
        "cij,cjk->cik",
        grad_chan,
        lax.all_gather(right_chan, "row", axis=1, tiled=True),
        preferred_element_type=jnp.float32,
    )
    grad_right = jnp.einsum(
        "cij,cik->cjk",
        grad_cols,
        lax.all_gather(left_chan, "row", axis=1, tiled=True),
        preferred_element_type=jnp.float32,
    )
    left_back, right_back = (
        lax.all_to_all(
            grad_left.astype(jnp.bfloat16), "ch", split_axis=2, concat_axis=0, tiled=True
        ),
        lax.all_to_all(
            grad_right.astype(jnp.bfloat16), "ch", split_axis=2, concat_axis=0, tiled=True
        ),
    )
    left_grad = left_back.astype(jnp.float32).reshape(width, -1)
    right_grad = right_back.astype(jnp.float32).reshape(width, -1)
    grad_proj = jnp.concatenate(
        [
            left_grad * left_sig,
            left_grad * blocks[0] * left_sig * (1.0 - left_sig),
            right_grad * right_sig,
            right_grad * blocks[2] * right_sig * (1.0 - right_sig),
            grad_logit,
        ],
        axis=0,
    ).astype(jnp.bfloat16)
    grad_in = jnp.einsum("ep,de->pd", grad_proj, proj_weight, preferred_element_type=jnp.float32)
    grad_pair = norm_back(grad_in * in_gain, normed, scale_inv, -1)
    return grad_pair.astype(jnp.bfloat16).reshape(rows_here, cols_here, width)


def solution(mesh):
    n_row, n_ch = mesh.shape["row"], mesh.shape["ch"]
    placed = (P("row", "ch", None), P("row", "ch", None), P(), P(), P(), P(), P(), P())

    def on_device(*args):
        rows, cols, width = args[0].shape
        devices, outer, group = n_row * n_ch, math.isqrt(n_row), BLOCK // rows
        if (
            devices & (devices - 1) == 0
            and n_row >= 4
            and n_row % outer == 0
            and outer % 2 == 0
            and width % (devices // 2) == 0
            and rows % (2 * PARTS) == 0
            and BLOCK % rows == 0
            and group % (width // (devices // 2)) == 0
            and width % (2 * group) == 0
            and cols % 128 == 0
        ):
            return by_channel(n_row, n_ch, *args)
        return by_row(*args)

    return jax.shard_map(
        on_device, mesh=mesh, in_specs=placed, out_specs=P("row", "ch", None), check_vma=False
    )
```

```python
import functools
import math

import jax
import jax.numpy as jnp
from jax import lax
from jax.experimental import pallas as pl
from jax.experimental.pallas import tpu as pltpu
from jax.sharding import PartitionSpec as P

EPSILON = 1e-05
F32 = jnp.float32
BF16 = jnp.bfloat16
UNROLL = 4
BLOCK = 256
PARTS = 4


def dot(a, b, da, db):
    return lax.dot_general(a, b, (((da,), (db,)), ((), ())), preferred_element_type=F32)


def sigmoid(values):
    return 0.5 * jnp.tanh(0.5 * values) + 0.5


def normalize(values, axis):
    center = jnp.mean(values, axis=axis, keepdims=True)
    shifted = values - center
    scale_inv = lax.rsqrt(jnp.mean(shifted * shifted, axis=axis, keepdims=True) + EPSILON)
    return (shifted * scale_inv, scale_inv)


def norm_back(grad_hat, normed, scale_inv, axis):
    first = jnp.mean(grad_hat, axis=axis, keepdims=True)
    second = jnp.mean(grad_hat * normed, axis=axis, keepdims=True)
    return scale_inv * (grad_hat - first - normed * second)


def column(row, width):
    return jnp.broadcast_to(row, (width, row.shape[-1])).T


def call(kernel, outs, scratch, *args, hbm=0, limit=16):
    single = not isinstance(outs, (list, tuple))
    args = [pltpu.with_memory_space_constraint(a, pltpu.HBM) if n < hbm else a for n, a in enumerate(args)]
    specs = [pl.BlockSpec(memory_space=pltpu.HBM if n < hbm else pltpu.VMEM) for n in range(len(args))]
    out_specs = [
        pl.BlockSpec(memory_space=getattr(out, "memory_space", pltpu.VMEM))
        for out in ([outs] if single else outs)
    ]
    return pl.pallas_call(
        kernel,
        out_shape=outs if single else tuple(outs),
        in_specs=specs,
        out_specs=out_specs[0] if single else tuple(out_specs),
        scratch_shapes=scratch,
        compiler_params=pltpu.CompilerParams(vmem_limit_bytes=limit * 1024 * 1024),
    )(*args)


def permutation(outer, inner):
    to = lax.broadcasted_iota(jnp.int32, (BLOCK, BLOCK), 0)
    start = lax.broadcasted_iota(jnp.int32, (BLOCK, BLOCK), 1)
    return (start == to % inner * outer + to // inner).astype(F32).astype(BF16)


def identity(size):
    first = lax.broadcasted_iota(jnp.int32, (size, size), 0)
    return (first == lax.broadcasted_iota(jnp.int32, (size, size), 1)).astype(F32).astype(BF16)


def swapped(swap, blocks):
    cols = blocks[0].shape[-1]
    wide = jnp.concatenate([block.reshape(BLOCK, cols) for block in blocks], axis=1)
    wide = dot(swap, wide, 1, 0).astype(BF16)
    return [wide[:, n * cols : (n + 1) * cols] for n in range(len(blocks))]


def fetched(sources, targets, sems):
    copies = [
        pltpu.make_async_copy(source, target, sems.at[n])
        for n, (source, target) in enumerate(zip(sources, targets))
    ]
    for copy in copies:
        copy.start()
    for copy in copies:
        copy.wait()


def weight_copies(w_hbm, w_ref, first, sems):
    width = w_hbm.shape[0]
    return [
        pltpu.make_async_copy(
            w_hbm.at[:, (first + n) * width : (first + n + 1) * width],
            w_ref.at[:, n * width : (n + 1) * width],
            sems.at[n],
        )
        for n in range(2)
    ]


def right_kernel(
    lay, x_hbm, gain_hbm, bias_hbm, w_hbm, r_hbm, n_ref, x_ref, gain_ref, bias_ref, w_ref, wt_ref, r_ref, right_ref, sems, out_sems
):
    rows, cols, width = x_ref.shape
    mine = width // lay.half
    parts = sems.shape[0] - 4
    size = rows // parts

    def fetch(p):
        here = pl.ds(p * size, size)
        return pltpu.make_async_copy(x_hbm.at[here], x_ref.at[here], sems.at[4 + p])

    small = [
        pltpu.make_async_copy(gain_hbm, gain_ref, sems.at[2]),
        pltpu.make_async_copy(bias_hbm, bias_ref, sems.at[3]),
    ]
    weights = weight_copies(w_hbm, w_ref, 2, sems)
    fetch(0).start()
    for copy in small + weights:
        copy.start()
    for p in range(1, parts):
        fetch(p).start()
    group = BLOCK // rows
    swap = permutation(group, rows)

    def normal(p):
        fetch(p).wait()
        for n in range(0, size, 2):
            i = p * size + n
            x = dot(eye, x_ref[pl.ds(i, 2)].reshape(2 * cols, width), 1, 1)
            normed, _s = normalize(x, 0)
            n_ref[p * size // 2 + n // 2] = (normed * gain + bias).astype(BF16)

    def project(p):
        for n in range(0, size, 2):
            i = p * size + n
            proj = dot(wt_ref[...], n_ref[p * size // 2 + n // 2], 1, 0)
            right = (sigmoid(proj[width:]) * proj[:width]).astype(BF16)
            for m in range(2):
                r_ref[i + m] = right[:, m * cols : (m + 1) * cols]

    def body(p, _):
        normal(p)
        project(p - 1)
        return 0

    eye = identity(width)
    for copy in small:
        copy.wait()
    gain = column(gain_ref[...], 2 * cols)
    bias = column(bias_ref[...], 2 * cols)
    normal(0)
    for copy in weights:
        copy.wait()
    wt_ref[...] = w_ref[...].astype(F32).T.astype(BF16)
    lax.fori_loop(1, parts, body, 0)
    project(parts - 1)
    out = []
    blocks = places(width, mine, rows)
    for k in range(0, len(blocks), 2):
        pair = blocks[k : k + 2]
        for (to, _here), right in zip(pair, swapped(swap, [r_ref[:, here] for _to, here in pair])):
            right_ref[to] = right.reshape(group // mine, mine, rows, cols)
            for share in range(to.start, to.stop):
                for n, device in enumerate(lay.order):
                    if lay.inside.index(device % lay.half) == share:
                        out.append(pltpu.make_async_copy(right_ref.at[share], r_hbm.at[n], out_sems.at[n]))
                        out[-1].start()
    for copy in out:
        copy.wait()


def left_kernel(lay, w_hbm, n_ref, mine_out, mate_out, w_ref, wt_ref, l_ref, left_ref, sems):
    rows, width, cols = l_ref.shape
    mine = width // lay.half
    group = BLOCK // rows
    weights = weight_copies(w_hbm, w_ref, 0, sems)
    for copy in weights:
        copy.start()
    for copy in weights:
        copy.wait()
    wt_ref[...] = w_ref[...].astype(F32).T.astype(BF16)
    swap = permutation(group, rows)

    def body(n, _):
        proj = dot(wt_ref[...], n_ref[n], 1, 0)
        left = (sigmoid(proj[width:]) * proj[:width]).astype(BF16)
        for m in range(2):
            l_ref[2 * n + m] = left[:, m * cols : (m + 1) * cols]
        return 0

    lax.fori_loop(0, rows // 2, body, 0, unroll=2)
    blocks = places(width, mine, rows)
    for k in range(0, len(blocks), 2):
        pair = blocks[k : k + 2]
        for (to, _here), left in zip(pair, swapped(swap, [l_ref[:, here] for _to, here in pair])):
            left_ref[to] = left.reshape(group // mine, mine, rows, cols)
    for n, s in enumerate(lay.hops):
        mine_out[n] = left_ref[lay.share(s)]
        mate_out[n] = left_ref[lay.share(s ^ lay.mate)]


def gate_kernel(*refs):
    sources, (h_ref, fac_hbm, fac_ref, wt_ref), targets, (sems, out_sems) = (
        refs[:7],
        refs[7:11],
        refs[11:18],
        refs[18:],
    )
    x_ref, cot_ref, gain_ref, bias_ref, w_ref, ogain_ref, ow_ref = targets
    rows, cols, width = x_ref.shape
    fetched(sources, targets, sems)
    wt_ref[...] = w_ref[:, : 4 * width].astype(F32).T.astype(BF16)
    ogain = column(ogain_ref[...], cols)

    def body(i, _):
        normed, _s = normalize(x_ref[i].astype(F32), -1)
        normal_in = (normed * gain_ref[...] + bias_ref[...]).astype(BF16)
        proj = dot(wt_ref[...], normal_in, 1, 1)
        for side in range(2):
            val = proj[2 * side * width : (2 * side + 1) * width]
            sig = sigmoid(proj[(2 * side + 1) * width : (2 * side + 2) * width])
            fac_ref[i, 2 * side * width : (2 * side + 1) * width] = sig.astype(BF16)
            fac_ref[i, (2 * side + 1) * width : (2 * side + 2) * width] = (
                val * sig * (1.0 - sig)
            ).astype(BF16)
        out_gate = sigmoid(dot(normal_in, w_ref[:, 4 * width :], 1, 0))
        grad_mixed = (cot_ref[i].astype(F32) * out_gate).astype(BF16)
        h_ref[i] = dot(ow_ref[...], grad_mixed, 1, 1) * ogain
        return 0

    size = rows // PARTS

    def send(p):
        here = pl.ds(p * size, size)
        return pltpu.make_async_copy(fac_ref.at[here], fac_hbm.at[here], out_sems.at[p])

    def part(p, _):
        for n in range(size):
            body(p * size + n, 0)
        send(p).start()
        return 0

    lax.fori_loop(0, PARTS, part, 0)
    for p in range(PARTS):
        send(p).wait()


def places(n_channels, mine, rows):
    group = BLOCK // rows
    return [
        (slice(c // mine, (c + group) // mine), slice(c, c + group)) for c in range(0, n_channels, group)
    ]


def to_rows(t_ref, ts_ref):
    rows, width, cols = ts_ref.shape
    mine = t_ref.shape[1]
    group = BLOCK // rows
    swap = permutation(rows, group)
    blocks = places(width, mine, rows)
    for n in range(0, len(blocks), 2):
        pair = blocks[n : n + 2]
        for (_to, here), block in zip(pair, swapped(swap, [t_ref[to] for to, _here in pair])):
            ts_ref[:, here] = block.reshape(rows, group, cols)


def tri_back_kernel(t_ref, h_ref, gt_ref, t_hbm, ts_ref, gs_ref, sem):
    rows, width, cols = h_ref.shape
    mine = t_ref.shape[1]
    group = BLOCK // rows
    copy = pltpu.make_async_copy(t_ref, t_hbm, sem)
    copy.start()
    back = permutation(group, rows)
    to_rows(t_ref, ts_ref)

    def body(i, _):
        tri, h = ts_ref[i].astype(F32), h_ref[i]
        shifted = tri - jnp.mean(tri, axis=0, keepdims=True)
        first = jnp.mean(h, axis=0, keepdims=True)
        both = jnp.mean(h * shifted, axis=0, keepdims=True)
        tri_inv = lax.rsqrt(jnp.mean(shifted * shifted, axis=0, keepdims=True) + EPSILON)
        gs_ref[i] = (tri_inv * (h - first - shifted * (both * tri_inv * tri_inv))).astype(BF16)
        return 0

    lax.fori_loop(0, rows, body, 0, unroll=UNROLL)
    blocks = places(width, mine, rows)
    for n in range(0, len(blocks), 2):
        pair = blocks[n : n + 2]
        for (to, _here), block in zip(pair, swapped(back, [gs_ref[:, here] for _to, here in pair])):
            gt_ref[to] = block.reshape(group // mine, mine, rows, cols)
    copy.wait()


def logit_kernel(*refs):
    (fac_hbm, *sources), refs = refs[:10], refs[10:]
    (gin0_ref, nt0_ref, fac0_ref, gin_hbm, nt_hbm, s_ref), refs = refs[:6], refs[6:]
    (ts_ref, gin_ref, nt_ref, out_sems), targets, sems = refs[:4], refs[4:13], refs[13]
    t_ref, x_ref, cot_ref, gain_ref, bias_ref, w_ref, ogain_ref, obias_ref, ow_ref = targets
    rows, cols, width = x_ref.shape
    first = pl.ds(0, nt0_ref.shape[0])
    fetched([*sources, fac_hbm.at[first]], [*targets, fac0_ref], sems)
    to_rows(t_ref, ts_ref)
    ogain = column(ogain_ref[...], cols)
    obias = column(obias_ref[...], cols)

    def body(i, _):
        normed, scale_inv = normalize(x_ref[i].astype(F32), -1)
        normal_in = (normed * gain_ref[...] + bias_ref[...]).astype(BF16)
        out_gate = sigmoid(dot(normal_in, w_ref[:, 4 * width :], 1, 0))
        tri_hat, _s = normalize(ts_ref[i].astype(F32), 0)
        normal_out = (tri_hat * ogain + obias).astype(BF16)
        mixed = dot(normal_out, ow_ref[...], 0, 0)
        grad_logit = cot_ref[i].astype(F32) * mixed * out_gate * (1.0 - out_gate)
        gin_ref[i] = dot(w_ref[:, 4 * width :], grad_logit.astype(BF16), 1, 1)
        nt_ref[i] = normed.T.astype(BF16)
        s_ref[pl.ds(i, 1), :] = jnp.broadcast_to(scale_inv, (cols, width)).T[:1]
        return 0

    lax.fori_loop(0, rows, body, 0, unroll=UNROLL)
    gin0_ref[...] = gin_ref[first]
    nt0_ref[...] = nt_ref[first]
    copies = [
        pltpu.make_async_copy(gin_ref, gin_hbm, out_sems.at[0]),
        pltpu.make_async_copy(nt_ref, nt_hbm, out_sems.at[1]),
    ]
    for copy in copies:
        copy.start()
    for copy in copies:
        copy.wait()


def pair_kernel(
    lay, fac_hbm, nt_hbm, gin_hbm, fac0_ref, nt0_ref, gin0_ref, r_ref, s_ref, gain_ref, w_ref, *refs
):
    l_refs, refs = refs[: lay.n_hops], refs[lay.n_hops :]
    out_hbm, l_ref, ls_ref, rs_ref, fac_ref, nt_ref, gin_ref, out_ref, sems = refs
    rows, cols, width = out_ref.shape
    mine = width // lay.half
    parts = sems.shape[1]
    size = rows // parts

    def fetch(p):
        here = pl.ds(p * size, size)
        return [
            pltpu.make_async_copy(fac_hbm.at[here], fac_ref.at[here], sems.at[0, p]),
            pltpu.make_async_copy(nt_hbm.at[here], nt_ref.at[here], sems.at[1, p]),
            pltpu.make_async_copy(gin_hbm.at[here], gin_ref.at[here], sems.at[2, p]),
        ]

    def send(p):
        here = pl.ds(p * size, size)
        return pltpu.make_async_copy(out_ref.at[here], out_hbm.at[here], sems.at[3, p])

    for p in range(1, parts):
        for copy in fetch(p):
            copy.start()
    gain = column(gain_ref[...], cols)
    eye = identity(cols)
    group = BLOCK // rows
    swap = permutation(rows, group)
    for s, source in lay.received(l_refs):
        l_ref[lay.share(s)] = source[...]
    for to, here in places(width, mine, rows):
        sums = []
        for share in range(to.start, to.stop):
            one, two = (
                r_ref[n].astype(F32)
                for n, device in enumerate(lay.order)
                if lay.inside.index(device % lay.half) == share
            )
            sums.append((one + two).astype(BF16))
        left, right = swapped(swap, [l_ref[to], jnp.stack(sums)])
        ls_ref[:, here] = left.reshape(rows, group, cols)
        rs_ref[:, here] = right.reshape(rows, group, cols)

    def part(p, fac_here, nt_here, gin_here):
        for n in range(0, size, 2):
            i = p * size + n
            blocks = []
            for m in range(2):
                left, right, fac = ls_ref[i + m], rs_ref[i + m], fac_here[i + m]
                blocks.append(
                    jnp.concatenate(
                        [
                            left * fac[:width],
                            left * fac[width : 2 * width],
                            right * fac[2 * width : 3 * width],
                            right * fac[3 * width :],
                        ],
                        axis=0,
                    )
                )
            grad_in = dot(w_ref[:, : 4 * width], jnp.concatenate(blocks, axis=1), 1, 0)
            for m in range(2):
                grad = (grad_in[:, m * cols : (m + 1) * cols] + gin_here[i + m]) * gain
                scale_inv = s_ref[pl.ds(i + m, 1), :]
                normed = nt_here[i + m].astype(F32)
                result = norm_back(grad, normed, scale_inv, 0).astype(BF16)
                out_ref[i + m] = dot(eye, result, 1, 1).astype(BF16)

    def body(p, _):
        for copy in fetch(p):
            copy.wait()
        part(p, fac_ref, nt_ref, gin_ref)
        send(p).start()
        return 0

    part(0, fac0_ref, nt0_ref, gin0_ref)
    send(0).start()
    lax.fori_loop(1, parts, body, 0)
    for p in range(parts):
        send(p).wait()


class Layout:
    def __init__(self, n_row, n_ch):
        self.n_row, self.n_ch = n_row, n_ch
        self.devices = n_row * n_ch
        self.half = self.devices // 2
        outer = math.isqrt(n_row)
        self.inner = self.devices // outer
        self.order = [o * self.inner + n for n in range(self.inner) for o in range(outer)]
        self.inside = [o * self.inner + n for n in range(self.inner) for o in range(outer // 2)]
        self.mate = n_ch
        self.hops = [s for s in range(self.half) if s & self.mate == 0]
        self.hops[3:] = self.hops[:2:-1]
        self.n_hops = len(self.hops) + 1
        self.all_place = self.place(self.order, n_row)
        self.half_place = self.place(self.inside, n_row // 2)
        self.near_place = self.place(list(range(self.half)), n_row // 2)

    def place(self, order, n_row):
        return [[order.index(r * self.n_ch + b) for b in range(self.n_ch)] for r in range(n_row)]

    def other(self, s):
        me = lax.axis_index("row") * self.n_ch + lax.axis_index("ch")
        return jnp.bitwise_xor(lax.rem(me, self.half), s)

    def share(self, s):
        other = self.other(s)
        return lax.rem(other, self.inner) * (self.half // self.inner) + lax.div(other, self.inner)

    def exchange_all(self, blocks):
        return lax.all_to_all(
            blocks, ("row", "ch"), split_axis=0, concat_axis=0, tiled=True, axis_index_groups=[self.order]
        )

    def exchange_half(self, blocks):
        groups = [[first + n for n in self.inside] for first in (0, self.half)]
        return lax.all_to_all(
            blocks, ("row", "ch"), split_axis=0, concat_axis=0, tiled=True, axis_index_groups=groups
        )

    def swap(self, block, s):
        return lax.ppermute(block, ("row", "ch"), [(n, n ^ s) for n in range(self.devices)])

    def permute(self, mine, mates):
        mates = self.swap(mates, self.mate)
        shape = jax.ShapeDtypeStruct((2,) + mine.shape[1:], mine.dtype)
        pairs = call(merge_kernel, [shape] * (len(self.hops) - 1), [], mine, mates)
        return [mine, mates] + [self.swap(pair, s) for pair, s in zip(pairs, self.hops[1:])]

    def received(self, refs):
        mine, mates, *pairs = refs
        found = [(0, mine.at[0]), (self.mate, mates.at[0])]
        for s, pair in zip(self.hops[1:], pairs):
            found += [(s, pair.at[0]), (s ^ self.mate, pair.at[1])]
        return found


def merge_kernel(mine_ref, mates_ref, *outs):
    for n, out_ref in enumerate(outs, 1):
        out_ref[0] = mine_ref[n]
        out_ref[1] = mates_ref[n]


def plane(ref, place, c):
    return jnp.concatenate(
        [
            jnp.concatenate([ref[n, c] for n in column_of], axis=0)
            for column_of in zip(*place)
        ],
        axis=1,
    )


def store_plane(ref, place, c, value):
    rows, cols = ref.shape[-2:]
    for r, row_of in enumerate(place):
        for b, n in enumerate(row_of):
            ref[n, c] = value[r * rows : (r + 1) * rows, b * cols : (b + 1) * cols]


def tri_kernel(lay, r_ref, *refs):
    l_refs, (t_ref, l_ref) = refs[: lay.n_hops], refs[lay.n_hops :]
    for s, source in lay.received(l_refs):
        l_ref[lay.other(s)] = source[...]
    for c in range(t_ref.shape[1]):
        tri = dot(plane(l_ref, lay.near_place, c), plane(r_ref, lay.all_place, c), 1, 1)
        store_plane(t_ref, lay.half_place, c, tri.astype(BF16))


def factor_back_kernel(lay, gt_ref, l_ref, r_ref, gr_hbm, *refs):
    mine_out, mate_out, gl_ref, gr_ref, sems = refs
    copies = []
    for c in range(gt_ref.shape[1]):
        right = dot(plane(gt_ref, lay.half_place, c), plane(l_ref, lay.near_place, c), 0, 0)
        store_plane(gr_ref, lay.all_place, c, right.astype(BF16))
        here = (slice(None), c)
        copies.append(pltpu.make_async_copy(gr_ref.at[here], gr_hbm.at[here], sems.at[c]))
        copies[-1].start()
    for c in range(gt_ref.shape[1]):
        left = dot(plane(gt_ref, lay.half_place, c), plane(r_ref, lay.all_place, c), 1, 0)
        store_plane(gl_ref, lay.near_place, c, left.astype(BF16))
    for n, s in enumerate(lay.hops):
        mine_out[n] = gl_ref[lay.other(s)]
        mate_out[n] = gl_ref[lay.other(s ^ lay.mate)]
    for copy in copies:
        copy.wait()


def by_channel(
    n_row, n_ch, pair_act, cotangent, in_gain, in_bias, proj_weight, out_gain, out_bias, out_weight
):
    lay = Layout(n_row, n_ch)
    rows, cols, width = pair_act.shape
    mine = width // lay.half
    struct = jax.ShapeDtypeStruct
    half = pltpu.VMEM((rows, width, cols), BF16)
    weight_t = pltpu.VMEM((4 * width, width), BF16)
    in_gain, in_bias, out_gain, out_bias = (
        v.reshape(1, width) for v in (in_gain, in_bias, out_gain, out_bias)
    )

    some = struct((len(lay.hops), mine, rows, cols), BF16)
    one = struct((lay.half, mine, rows, cols), BF16)
    one_here = pltpu.VMEM(one.shape, BF16)
    two_shape = (lay.devices, mine, rows, cols)
    row = pltpu.VMEM((1, width), F32)
    weight = pltpu.VMEM(proj_weight.shape, BF16)
    out_weight_here = pltpu.VMEM((width, width), BF16)
    both_weights = pltpu.VMEM((width, 2 * width), BF16)
    both_turned = pltpu.VMEM((2 * width, width), BF16)
    right, normal_in = call(
        functools.partial(right_kernel, lay),
        [pltpu.HBM(two_shape, BF16), struct((rows // 2, width, 2 * cols), BF16)],
        [
            half,
            row,
            row,
            both_weights,
            both_turned,
            half,
            one_here,
            pltpu.SemaphoreType.DMA((4 + PARTS,)),
            pltpu.SemaphoreType.DMA((lay.devices,)),
        ],
        pair_act,
        in_gain,
        in_bias,
        proj_weight,
        hbm=4,
    )
    left = call(
        functools.partial(left_kernel, lay),
        [some, some],
        [both_weights, both_turned, half, one_here, pltpu.SemaphoreType.DMA((2,))],
        proj_weight,
        normal_in,
        hbm=1,
    )
    right = lay.exchange_all(right)
    left = lay.permute(*left)
    h, fac = call(
        gate_kernel,
        [pltpu.VMEM((rows, width, cols), F32), pltpu.HBM((rows, 4 * width, cols), BF16)],
        [
            pltpu.VMEM((rows, 4 * width, cols), BF16),
            weight_t,
            half,
            half,
            row,
            row,
            weight,
            row,
            out_weight_here,
            pltpu.SemaphoreType.DMA((7,)),
            pltpu.SemaphoreType.DMA((PARTS,)),
        ],
        pair_act,
        cotangent,
        in_gain,
        in_bias,
        proj_weight,
        out_gain,
        out_weight,
        hbm=7,
    )
    right, h, fac = lax.optimization_barrier((right, h, fac))
    tri, left = call(functools.partial(tri_kernel, lay), [one, one], [], right, *left)
    tri = lay.exchange_half(tri)
    grad_tri, tri = call(
        tri_back_kernel,
        [one, pltpu.HBM(one.shape, BF16)],
        [half, half, pltpu.SemaphoreType.DMA(())],
        tri,
        h,
    )
    grad_right, *grad_left = call(
        functools.partial(factor_back_kernel, lay),
        [pltpu.HBM(two_shape, BF16), some, some],
        [one_here, pltpu.VMEM(two_shape, BF16), pltpu.SemaphoreType.DMA((mine,))],
        lay.exchange_half(grad_tri),
        left,
        right,
    )
    grad_right = lay.exchange_all(grad_right)
    grad_left = lay.permute(*grad_left)
    grad_in_first, normed_first, fac_first, grad_in, normed_t, scale = call(
        logit_kernel,
        [
            pltpu.VMEM((rows // PARTS, width, cols), F32),
            pltpu.VMEM((rows // PARTS, width, cols), BF16),
            pltpu.VMEM((rows // PARTS, 4 * width, cols), BF16),
            pltpu.HBM((rows, width, cols), F32),
            pltpu.HBM((rows, width, cols), BF16),
            pltpu.VMEM((rows, cols), F32),
        ],
        [
            half,
            pltpu.VMEM((rows, width, cols), F32),
            half,
            pltpu.SemaphoreType.DMA((2,)),
            one_here,
            half,
            half,
            row,
            row,
            weight,
            row,
            row,
            out_weight_here,
            pltpu.SemaphoreType.DMA((10,)),
        ],
        fac,
        tri,
        pair_act,
        cotangent,
        in_gain,
        in_bias,
        proj_weight,
        out_gain,
        out_bias,
        out_weight,
        hbm=10,
    )
    return call(
        functools.partial(pair_kernel, lay),
        pltpu.HBM((rows, cols, width), BF16),
        [
            one_here,
            half,
            half,
            pltpu.VMEM((rows, 4 * width, cols), BF16),
            half,
            pltpu.VMEM((rows, width, cols), F32),
            half,
            pltpu.SemaphoreType.DMA((4, PARTS)),
        ],
        fac,
        normed_t,
        grad_in,
        fac_first,
        normed_first,
        grad_in_first,
        grad_right,
        scale,
        in_gain,
        proj_weight,
        *grad_left,
        hbm=3,
    )


def by_row(
    pair_act, cotangent, in_gain, in_bias, proj_weight, out_gain, out_bias, out_weight
):
    rows_here, cols_here, width = pair_act.shape
    flat = pair_act.astype(jnp.float32).reshape(rows_here * cols_here, width)
    normed, scale_inv = normalize(flat, -1)
    normal_in = (normed * in_gain + in_bias).astype(jnp.bfloat16)
    projected = jnp.einsum("pd,de->ep", normal_in, proj_weight, preferred_element_type=jnp.float32)
    blocks = jnp.split(projected, 5, axis=0)
    left_sig = jax.nn.sigmoid(blocks[1])
    right_sig = jax.nn.sigmoid(blocks[3])
    left_fac = (left_sig * blocks[0]).astype(jnp.bfloat16).reshape(width, rows_here, cols_here)
    right_fac = (right_sig * blocks[2]).astype(jnp.bfloat16).reshape(width, rows_here, cols_here)
    left_chan, right_chan = (
        lax.all_to_all(left_fac, "ch", split_axis=0, concat_axis=2, tiled=True),
        lax.all_to_all(right_fac, "ch", split_axis=0, concat_axis=2, tiled=True),
    )
    tri_chan = jnp.einsum(
        "cik,cjk->cij",
        left_chan,
        lax.all_gather(right_chan, "row", axis=1, tiled=True),
        preferred_element_type=jnp.float32,
    ).astype(jnp.bfloat16)
    tri_back = lax.all_to_all(tri_chan, "ch", split_axis=2, concat_axis=0, tiled=True)
    tri_hat, tri_inv = normalize(tri_back.astype(jnp.float32).reshape(width, -1), 0)
    normal_out = (tri_hat * out_gain[:, None] + out_bias[:, None]).astype(jnp.bfloat16)
    mixed = jnp.einsum("cp,ce->ep", normal_out, out_weight, preferred_element_type=jnp.float32)
    out_gate = jax.nn.sigmoid(blocks[4])
    grad_out = cotangent.astype(jnp.float32).reshape(rows_here * cols_here, width).T
    grad_mixed = (grad_out * out_gate).astype(jnp.bfloat16)
    grad_logit = grad_out * mixed * out_gate * (1.0 - out_gate)
    grad_normal = jnp.einsum(
        "ep,ce->cp", grad_mixed, out_weight, preferred_element_type=jnp.float32
    )
    grad_tri = norm_back(grad_normal * out_gain[:, None], tri_hat, tri_inv, 0)
    grad_tri = grad_tri.astype(jnp.bfloat16).reshape(width, rows_here, cols_here)
    grad_chan = lax.all_to_all(grad_tri, "ch", split_axis=0, concat_axis=2, tiled=True)
    grad_cols = lax.all_to_all(grad_chan, "row", split_axis=2, concat_axis=1, tiled=True)
    grad_left = jnp.einsum(
        "cij,cjk->cik",
        grad_chan,
        lax.all_gather(right_chan, "row", axis=1, tiled=True),
        preferred_element_type=jnp.float32,
    )
    grad_right = jnp.einsum(
        "cij,cik->cjk",
        grad_cols,
        lax.all_gather(left_chan, "row", axis=1, tiled=True),
        preferred_element_type=jnp.float32,
    )
    left_back, right_back = (
        lax.all_to_all(
            grad_left.astype(jnp.bfloat16), "ch", split_axis=2, concat_axis=0, tiled=True
        ),
        lax.all_to_all(
            grad_right.astype(jnp.bfloat16), "ch", split_axis=2, concat_axis=0, tiled=True
        ),
    )
    left_grad = left_back.astype(jnp.float32).reshape(width, -1)
    right_grad = right_back.astype(jnp.float32).reshape(width, -1)
    grad_proj = jnp.concatenate(
        [
            left_grad * left_sig,
            left_grad * blocks[0] * left_sig * (1.0 - left_sig),
            right_grad * right_sig,
            right_grad * blocks[2] * right_sig * (1.0 - right_sig),
            grad_logit,
        ],
        axis=0,
    ).astype(jnp.bfloat16)
    grad_in = jnp.einsum("ep,de->pd", grad_proj, proj_weight, preferred_element_type=jnp.float32)
    grad_pair = norm_back(grad_in * in_gain, normed, scale_inv, -1)
    return grad_pair.astype(jnp.bfloat16).reshape(rows_here, cols_here, width)


def solution(mesh):
    n_row, n_ch = mesh.shape["row"], mesh.shape["ch"]
    placed = (P("row", "ch", None), P("row", "ch", None), P(), P(), P(), P(), P(), P())

    def on_device(*args):
        rows, cols, width = args[0].shape
        devices, outer, group = n_row * n_ch, math.isqrt(n_row), BLOCK // rows
        if (
            devices & (devices - 1) == 0
            and n_row >= 4
            and n_row % outer == 0
            and outer % 2 == 0
            and width % (devices // 2) == 0
            and rows % (2 * PARTS) == 0
            and BLOCK % rows == 0
            and group % (width // (devices // 2)) == 0
            and width % (2 * group) == 0
            and cols % 128 == 0
        ):
            return by_channel(n_row, n_ch, *args)
        return by_row(*args)

    return jax.shard_map(
        on_device, mesh=mesh, in_specs=placed, out_specs=P("row", "ch", None), check_vma=False
    )
```

```python
import functools
import math

import jax
import jax.numpy as jnp
from jax import lax
from jax.experimental import pallas as pl
from jax.experimental.pallas import tpu as pltpu
from jax.sharding import PartitionSpec as P

EPSILON = 1e-05
F32 = jnp.float32
BF16 = jnp.bfloat16
UNROLL = 4
BLOCK = 256
PARTS = 4
INSIDE_16 = (0, 11, 4, 13, 2, 14, 1, 8, 7, 9, 6, 10, 5, 12, 3, 15)


def dot(a, b, da, db):
    return lax.dot_general(a, b, (((da,), (db,)), ((), ())), preferred_element_type=F32)


def sigmoid(values):
    return 0.5 * jnp.tanh(0.5 * values) + 0.5


def normalize(values, axis):
    center = jnp.mean(values, axis=axis, keepdims=True)
    shifted = values - center
    scale_inv = lax.rsqrt(jnp.mean(shifted * shifted, axis=axis, keepdims=True) + EPSILON)
    return (shifted * scale_inv, scale_inv)


def norm_back(grad_hat, normed, scale_inv, axis):
    first = jnp.mean(grad_hat, axis=axis, keepdims=True)
    second = jnp.mean(grad_hat * normed, axis=axis, keepdims=True)
    return scale_inv * (grad_hat - first - normed * second)


def column(row, width):
    return jnp.broadcast_to(row, (width, row.shape[-1])).T


def call(kernel, outs, scratch, *args, hbm=0, limit=16):
    single = not isinstance(outs, (list, tuple))
    args = [pltpu.with_memory_space_constraint(a, pltpu.HBM) if n < hbm else a for n, a in enumerate(args)]
    specs = [pl.BlockSpec(memory_space=pltpu.HBM if n < hbm else pltpu.VMEM) for n in range(len(args))]
    out_specs = [
        pl.BlockSpec(memory_space=getattr(out, "memory_space", pltpu.VMEM))
        for out in ([outs] if single else outs)
    ]
    return pl.pallas_call(
        kernel,
        out_shape=outs if single else tuple(outs),
        in_specs=specs,
        out_specs=out_specs[0] if single else tuple(out_specs),
        scratch_shapes=scratch,
        compiler_params=pltpu.CompilerParams(vmem_limit_bytes=limit * 1024 * 1024),
    )(*args)


def permutation(outer, inner):
    to = lax.broadcasted_iota(jnp.int32, (BLOCK, BLOCK), 0)
    start = lax.broadcasted_iota(jnp.int32, (BLOCK, BLOCK), 1)
    return (start == to % inner * outer + to // inner).astype(F32).astype(BF16)


def identity(size):
    first = lax.broadcasted_iota(jnp.int32, (size, size), 0)
    return (first == lax.broadcasted_iota(jnp.int32, (size, size), 1)).astype(F32).astype(BF16)


def swapped(swap, blocks):
    cols = blocks[0].shape[-1]
    wide = jnp.concatenate([block.reshape(BLOCK, cols) for block in blocks], axis=1)
    wide = dot(swap, wide, 1, 0).astype(BF16)
    return [wide[:, n * cols : (n + 1) * cols] for n in range(len(blocks))]


def fetched(sources, targets, sems):
    copies = [
        pltpu.make_async_copy(source, target, sems.at[n])
        for n, (source, target) in enumerate(zip(sources, targets))
    ]
    for copy in copies:
        copy.start()
    for copy in copies:
        copy.wait()


def weight_copies(w_hbm, w_ref, first, sems):
    width = w_hbm.shape[0]
    return [
        pltpu.make_async_copy(
            w_hbm.at[:, (first + n) * width : (first + n + 1) * width],
            w_ref.at[:, n * width : (n + 1) * width],
            sems.at[n],
        )
        for n in range(2)
    ]


def right_kernel(
    lay, x_hbm, gain_hbm, bias_hbm, w_hbm, r_hbm, n_ref, x_ref, gain_ref, bias_ref, w_ref, wt_ref, r_ref, right_ref, sems, out_sems
):
    rows, cols, width = x_ref.shape
    mine = width // lay.half
    parts = sems.shape[0] - 4
    size = rows // parts

    def fetch(p):
        here = pl.ds(p * size, size)
        return pltpu.make_async_copy(x_hbm.at[here], x_ref.at[here], sems.at[4 + p])

    small = [
        pltpu.make_async_copy(gain_hbm, gain_ref, sems.at[2]),
        pltpu.make_async_copy(bias_hbm, bias_ref, sems.at[3]),
    ]
    weights = weight_copies(w_hbm, w_ref, 2, sems)
    fetch(0).start()
    for copy in small + weights:
        copy.start()
    for p in range(1, parts):
        fetch(p).start()
    group = BLOCK // rows
    swap = permutation(group, rows)

    def normal(p):
        fetch(p).wait()
        for n in range(0, size, 2):
            i = p * size + n
            shifted = dot(center, x_ref[pl.ds(i, 2)].reshape(2 * cols, width), 1, 1)
            scale_inv = lax.rsqrt(jnp.mean(shifted * shifted, axis=0, keepdims=True) + EPSILON)
            n_ref[p * size // 2 + n // 2] = (shifted * scale_inv * gain + bias).astype(BF16)

    def project(p):
        for n in range(0, size, 2):
            i = p * size + n
            proj = dot(wt_ref[...], n_ref[p * size // 2 + n // 2], 1, 0)
            right = (sigmoid(proj[width:]) * proj[:width]).astype(BF16)
            for m in range(2):
                r_ref[i + m] = right[:, m * cols : (m + 1) * cols]

    def body(p, _):
        normal(p)
        project(p - 1)
        return 0

    center = (identity(width).astype(F32) - 1.0 / width).astype(BF16)
    for copy in small:
        copy.wait()
    gain = column(gain_ref[...], 2 * cols)
    bias = column(bias_ref[...], 2 * cols)
    normal(0)
    for copy in weights:
        copy.wait()
    wt_ref[...] = w_ref[...].astype(F32).T.astype(BF16)
    lax.fori_loop(1, parts, body, 0)
    project(parts - 1)
    out = []
    blocks = places(width, mine, rows)
    for k in range(0, len(blocks), 2):
        pair = blocks[k : k + 2]
        for (to, _here), right in zip(pair, swapped(swap, [r_ref[:, here] for _to, here in pair])):
            right_ref[to] = right.reshape(group // mine, mine, rows, cols)
            for share in range(to.start, to.stop):
                for n, device in enumerate(lay.order):
                    if device % lay.half == share:
                        out.append(pltpu.make_async_copy(right_ref.at[share], r_hbm.at[n], out_sems.at[n]))
                        out[-1].start()
    for copy in out:
        copy.wait()


def left_kernel(lay, w_hbm, n_ref, mine_out, mate_out, w_ref, wt_ref, l_ref, left_ref, sems):
    rows, width, cols = l_ref.shape
    mine = width // lay.half
    group = BLOCK // rows
    weights = weight_copies(w_hbm, w_ref, 0, sems)
    for copy in weights:
        copy.start()
    for copy in weights:
        copy.wait()
    wt_ref[...] = w_ref[...].astype(F32).T.astype(BF16)
    swap = permutation(group, rows)

    def body(n, _):
        proj = dot(wt_ref[...], n_ref[n], 1, 0)
        left = (sigmoid(proj[width:]) * proj[:width]).astype(BF16)
        for m in range(2):
            l_ref[2 * n + m] = left[:, m * cols : (m + 1) * cols]
        return 0

    lax.fori_loop(0, rows // 2, body, 0, unroll=2)
    blocks = places(width, mine, rows)
    for k in range(0, len(blocks), 2):
        pair = blocks[k : k + 2]
        for (to, _here), left in zip(pair, swapped(swap, [l_ref[:, here] for _to, here in pair])):
            left_ref[to] = left.reshape(group // mine, mine, rows, cols)
    for n, s in enumerate(lay.hops):
        mine_out[n] = left_ref[lay.other(s)]
        mate_out[n] = left_ref[lay.other(s ^ lay.mate)]


def gate_kernel(*refs):
    sources, (h_ref, fac_hbm, fac_ref, wt_ref), targets, (sems, out_sems) = (
        refs[:7],
        refs[7:11],
        refs[11:18],
        refs[18:],
    )
    x_ref, cot_ref, gain_ref, bias_ref, w_ref, ogain_ref, ow_ref = targets
    rows, cols, width = x_ref.shape
    fetched(sources, targets, sems)
    wt_ref[...] = w_ref[:, : 4 * width].astype(F32).T.astype(BF16)
    ogain = column(ogain_ref[...], cols)

    def body(i, _):
        normed, _s = normalize(x_ref[i].astype(F32), -1)
        normal_in = (normed * gain_ref[...] + bias_ref[...]).astype(BF16)
        proj = dot(wt_ref[...], normal_in, 1, 1)
        for side in range(2):
            val = proj[2 * side * width : (2 * side + 1) * width]
            sig = sigmoid(proj[(2 * side + 1) * width : (2 * side + 2) * width])
            fac_ref[i, 2 * side * width : (2 * side + 1) * width] = sig.astype(BF16)
            fac_ref[i, (2 * side + 1) * width : (2 * side + 2) * width] = (
                val * sig * (1.0 - sig)
            ).astype(BF16)
        out_gate = sigmoid(dot(normal_in, w_ref[:, 4 * width :], 1, 0))
        grad_mixed = (cot_ref[i].astype(F32) * out_gate).astype(BF16)
        h_ref[i] = dot(ow_ref[...], grad_mixed, 1, 1) * ogain
        return 0

    size = rows // PARTS

    def send(p):
        here = pl.ds(p * size, size)
        return pltpu.make_async_copy(fac_ref.at[here], fac_hbm.at[here], out_sems.at[p])

    def part(p, _):
        for n in range(size):
            body(p * size + n, 0)
        send(p).start()
        return 0

    lax.fori_loop(0, PARTS, part, 0)
    for p in range(PARTS):
        send(p).wait()


def places(n_channels, mine, rows):
    group = BLOCK // rows
    return [
        (slice(c // mine, (c + group) // mine), slice(c, c + group)) for c in range(0, n_channels, group)
    ]


def to_rows(lay, t_ref, ts_ref):
    rows, width, cols = ts_ref.shape
    mine = t_ref.shape[1]
    group = BLOCK // rows
    swap = permutation(rows, group)
    blocks = places(width, mine, rows)
    for n in range(0, len(blocks), 2):
        pair = blocks[n : n + 2]
        for (_to, here), block in zip(pair, swapped(swap, [lay.shares(t_ref, to) for to, _here in pair])):
            ts_ref[:, here] = block.reshape(rows, group, cols)


def tri_back_kernel(lay, t_ref, h_ref, gt_ref, t_hbm, ts_ref, gs_ref, sem):
    rows, width, cols = h_ref.shape
    mine = t_ref.shape[1]
    group = BLOCK // rows
    copy = pltpu.make_async_copy(t_ref, t_hbm, sem)
    copy.start()
    back = permutation(group, rows)
    to_rows(lay, t_ref, ts_ref)

    def body(i, _):
        tri, h = ts_ref[i].astype(F32), h_ref[i]
        shifted = tri - jnp.mean(tri, axis=0, keepdims=True)
        first = jnp.mean(h, axis=0, keepdims=True)
        both = jnp.mean(h * shifted, axis=0, keepdims=True)
        tri_inv = lax.rsqrt(jnp.mean(shifted * shifted, axis=0, keepdims=True) + EPSILON)
        gs_ref[i] = (tri_inv * (h - first - shifted * (both * tri_inv * tri_inv))).astype(BF16)
        return 0

    lax.fori_loop(0, rows, body, 0, unroll=UNROLL)
    blocks = places(width, mine, rows)
    for n in range(0, len(blocks), 2):
        pair = blocks[n : n + 2]
        for (to, _here), block in zip(pair, swapped(back, [gs_ref[:, here] for _to, here in pair])):
            block = block.reshape(group // mine, mine, rows, cols)
            for share in range(to.start, to.stop):
                gt_ref[lay.inside.index(share)] = block[share - to.start]
    copy.wait()


def logit_kernel(lay, *refs):
    (fac_hbm, *sources), refs = refs[:10], refs[10:]
    (gin0_ref, nt0_ref, fac0_ref, gin_hbm, nt_hbm, s_ref), refs = refs[:6], refs[6:]
    (ts_ref, gin_ref, nt_ref, out_sems), targets, sems = refs[:4], refs[4:13], refs[13]
    t_ref, x_ref, cot_ref, gain_ref, bias_ref, w_ref, ogain_ref, obias_ref, ow_ref = targets
    rows, cols, width = x_ref.shape
    first = pl.ds(0, nt0_ref.shape[0])
    fetched([*sources, fac_hbm.at[first]], [*targets, fac0_ref], sems)
    to_rows(lay, t_ref, ts_ref)
    ogain = column(ogain_ref[...], cols)
    obias = column(obias_ref[...], cols)

    def body(i, _):
        normed, scale_inv = normalize(x_ref[i].astype(F32), -1)
        normal_in = (normed * gain_ref[...] + bias_ref[...]).astype(BF16)
        out_gate = sigmoid(dot(normal_in, w_ref[:, 4 * width :], 1, 0))
        tri_hat, _s = normalize(ts_ref[i].astype(F32), 0)
        normal_out = (tri_hat * ogain + obias).astype(BF16)
        mixed = dot(normal_out, ow_ref[...], 0, 0)
        grad_logit = cot_ref[i].astype(F32) * mixed * out_gate * (1.0 - out_gate)
        gin_ref[i] = dot(w_ref[:, 4 * width :], grad_logit.astype(BF16), 1, 1)
        nt_ref[i] = normed.T.astype(BF16)
        s_ref[pl.ds(i, 1), :] = jnp.broadcast_to(scale_inv, (cols, width)).T[:1]
        return 0

    lax.fori_loop(0, rows, body, 0, unroll=UNROLL)
    gin0_ref[...] = gin_ref[first]
    nt0_ref[...] = nt_ref[first]
    copies = [
        pltpu.make_async_copy(gin_ref, gin_hbm, out_sems.at[0]),
        pltpu.make_async_copy(nt_ref, nt_hbm, out_sems.at[1]),
    ]
    for copy in copies:
        copy.start()
    for copy in copies:
        copy.wait()


def pair_kernel(
    lay, fac_hbm, nt_hbm, gin_hbm, fac0_ref, nt0_ref, gin0_ref, r_ref, s_ref, gain_ref, w_ref, *refs
):
    l_refs, refs = refs[: lay.n_hops], refs[lay.n_hops :]
    out_hbm, l_ref, ls_ref, rs_ref, fac_ref, nt_ref, gin_ref, out_ref, sems = refs
    rows, cols, width = out_ref.shape
    mine = width // lay.half
    parts = sems.shape[1]
    size = rows // parts

    def fetch(p):
        here = pl.ds(p * size, size)
        return [
            pltpu.make_async_copy(fac_hbm.at[here], fac_ref.at[here], sems.at[0, p]),
            pltpu.make_async_copy(nt_hbm.at[here], nt_ref.at[here], sems.at[1, p]),
            pltpu.make_async_copy(gin_hbm.at[here], gin_ref.at[here], sems.at[2, p]),
        ]

    def send(p):
        here = pl.ds(p * size, size)
        return pltpu.make_async_copy(out_ref.at[here], out_hbm.at[here], sems.at[3, p])

    for p in range(1, parts):
        for copy in fetch(p):
            copy.start()
    gain = column(gain_ref[...], cols)
    eye = identity(cols)
    group = BLOCK // rows
    swap = permutation(rows, group)
    for s, source in lay.received(l_refs):
        l_ref[lay.other(s)] = source[...]
    for to, here in places(width, mine, rows):
        sums = []
        for share in range(to.start, to.stop):
            one, two = (
                r_ref[n].astype(F32)
                for n, device in enumerate(lay.order)
                if device % lay.half == share
            )
            sums.append((one + two).astype(BF16))
        left, right = swapped(swap, [l_ref[to], jnp.stack(sums)])
        ls_ref[:, here] = left.reshape(rows, group, cols)
        rs_ref[:, here] = right.reshape(rows, group, cols)

    def part(p, fac_here, nt_here, gin_here):
        for n in range(0, size, 2):
            i = p * size + n
            blocks = []
            for m in range(2):
                left, right, fac = ls_ref[i + m], rs_ref[i + m], fac_here[i + m]
                blocks.append(
                    jnp.concatenate(
                        [
                            left * fac[:width],
                            left * fac[width : 2 * width],
                            right * fac[2 * width : 3 * width],
                            right * fac[3 * width :],
                        ],
                        axis=0,
                    )
                )
            grad_in = dot(w_ref[:, : 4 * width], jnp.concatenate(blocks, axis=1), 1, 0)
            for m in range(2):
                grad = (grad_in[:, m * cols : (m + 1) * cols] + gin_here[i + m]) * gain
                scale_inv = s_ref[pl.ds(i + m, 1), :]
                normed = nt_here[i + m].astype(F32)
                result = norm_back(grad, normed, scale_inv, 0).astype(BF16)
                out_ref[i + m] = dot(eye, result, 1, 1).astype(BF16)

    def body(p, _):
        for copy in fetch(p):
            copy.wait()
        part(p, fac_ref, nt_ref, gin_ref)
        send(p).start()
        return 0

    part(0, fac0_ref, nt0_ref, gin0_ref)
    send(0).start()
    lax.fori_loop(1, parts, body, 0)
    for p in range(parts):
        send(p).wait()


class Layout:
    def __init__(self, n_row, n_ch):
        self.n_row, self.n_ch = n_row, n_ch
        self.devices = n_row * n_ch
        self.half = self.devices // 2
        outer = math.isqrt(n_row)
        self.inner = self.devices // outer
        self.order = [o * self.inner + n for n in range(self.inner) for o in range(outer)]
        self.inside = [o * self.inner + n for n in range(self.inner) for o in range(outer // 2)]
        if self.half == len(INSIDE_16):
            self.inside = list(INSIDE_16)
        self.mate = n_ch
        self.hops = [s for s in range(self.half) if s & self.mate == 0]
        self.hops[3:] = self.hops[:2:-1]
        self.n_hops = len(self.hops) + 1
        self.all_place = self.place(self.order, n_row)
        self.half_place = self.place(self.inside, n_row // 2)
        self.near_place = self.place(list(range(self.half)), n_row // 2)

    def place(self, order, n_row):
        return [[order.index(r * self.n_ch + b) for b in range(self.n_ch)] for r in range(n_row)]

    def shares(self, ref, here):
        return jnp.stack([ref[self.inside.index(share)] for share in range(here.start, here.stop)])

    def other(self, s):
        me = lax.axis_index("row") * self.n_ch + lax.axis_index("ch")
        return jnp.bitwise_xor(lax.rem(me, self.half), s)

    def exchange_all(self, blocks):
        return lax.all_to_all(
            blocks, ("row", "ch"), split_axis=0, concat_axis=0, tiled=True, axis_index_groups=[self.order]
        )

    def exchange_half(self, blocks):
        groups = [[first + n for n in self.inside] for first in (0, self.half)]
        return lax.all_to_all(
            blocks, ("row", "ch"), split_axis=0, concat_axis=0, tiled=True, axis_index_groups=groups
        )

    def swap(self, block, s):
        return lax.ppermute(block, ("row", "ch"), [(n, n ^ s) for n in range(self.devices)])

    def permute(self, mine, mates):
        mates = self.swap(mates, self.mate)
        shape = jax.ShapeDtypeStruct((2,) + mine.shape[1:], mine.dtype)
        pairs = call(merge_kernel, [shape] * (len(self.hops) - 1), [], mine, mates)
        return [mine, mates] + [self.swap(pair, s) for pair, s in zip(pairs, self.hops[1:])]

    def received(self, refs):
        mine, mates, *pairs = refs
        found = [(0, mine.at[0]), (self.mate, mates.at[0])]
        for s, pair in zip(self.hops[1:], pairs):
            found += [(s, pair.at[0]), (s ^ self.mate, pair.at[1])]
        return found


def merge_kernel(mine_ref, mates_ref, *outs):
    for n, out_ref in enumerate(outs, 1):
        out_ref[0] = mine_ref[n]
        out_ref[1] = mates_ref[n]


def plane(ref, place, c):
    return jnp.concatenate(
        [
            jnp.concatenate([ref[n, c] for n in column_of], axis=0)
            for column_of in zip(*place)
        ],
        axis=1,
    )


def store_plane(ref, place, c, value):
    rows, cols = ref.shape[-2:]
    for r, row_of in enumerate(place):
        for b, n in enumerate(row_of):
            ref[n, c] = value[r * rows : (r + 1) * rows, b * cols : (b + 1) * cols]


def tri_kernel(lay, r_ref, *refs):
    l_refs, (t_ref, l_ref) = refs[: lay.n_hops], refs[lay.n_hops :]
    for s, source in lay.received(l_refs):
        l_ref[lay.other(s)] = source[...]
    for c in range(t_ref.shape[1]):
        tri = dot(plane(l_ref, lay.near_place, c), plane(r_ref, lay.all_place, c), 1, 1)
        store_plane(t_ref, lay.half_place, c, tri.astype(BF16))


def factor_back_kernel(lay, gt_ref, l_ref, r_ref, gr_hbm, *refs):
    mine_out, mate_out, gl_ref, gr_ref, sems = refs
    copies = []
    for c in range(gt_ref.shape[1]):
        right = dot(plane(gt_ref, lay.half_place, c), plane(l_ref, lay.near_place, c), 0, 0)
        store_plane(gr_ref, lay.all_place, c, right.astype(BF16))
        here = (slice(None), c)
        copies.append(pltpu.make_async_copy(gr_ref.at[here], gr_hbm.at[here], sems.at[c]))
        copies[-1].start()
    for c in range(gt_ref.shape[1]):
        left = dot(plane(gt_ref, lay.half_place, c), plane(r_ref, lay.all_place, c), 1, 0)
        store_plane(gl_ref, lay.near_place, c, left.astype(BF16))
    for n, s in enumerate(lay.hops):
        mine_out[n] = gl_ref[lay.other(s)]
        mate_out[n] = gl_ref[lay.other(s ^ lay.mate)]
    for copy in copies:
        copy.wait()


def by_channel(
    n_row, n_ch, pair_act, cotangent, in_gain, in_bias, proj_weight, out_gain, out_bias, out_weight
):
    lay = Layout(n_row, n_ch)
    rows, cols, width = pair_act.shape
    mine = width // lay.half
    struct = jax.ShapeDtypeStruct
    half = pltpu.VMEM((rows, width, cols), BF16)
    weight_t = pltpu.VMEM((4 * width, width), BF16)
    in_gain, in_bias, out_gain, out_bias = (
        v.reshape(1, width) for v in (in_gain, in_bias, out_gain, out_bias)
    )

    some = struct((len(lay.hops), mine, rows, cols), BF16)
    one = struct((lay.half, mine, rows, cols), BF16)
    one_here = pltpu.VMEM(one.shape, BF16)
    two_shape = (lay.devices, mine, rows, cols)
    row = pltpu.VMEM((1, width), F32)
    weight = pltpu.VMEM(proj_weight.shape, BF16)
    out_weight_here = pltpu.VMEM((width, width), BF16)
    both_weights = pltpu.VMEM((width, 2 * width), BF16)
    both_turned = pltpu.VMEM((2 * width, width), BF16)
    right, normal_in = call(
        functools.partial(right_kernel, lay),
        [pltpu.HBM(two_shape, BF16), struct((rows // 2, width, 2 * cols), BF16)],
        [
            half,
            row,
            row,
            both_weights,
            both_turned,
            half,
            one_here,
            pltpu.SemaphoreType.DMA((4 + PARTS // 2,)),
            pltpu.SemaphoreType.DMA((lay.devices,)),
        ],
        pair_act,
        in_gain,
        in_bias,
        proj_weight,
        hbm=4,
    )
    left = call(
        functools.partial(left_kernel, lay),
        [some, some],
        [both_weights, both_turned, half, one_here, pltpu.SemaphoreType.DMA((2,))],
        proj_weight,
        normal_in,
        hbm=1,
    )
    right = lay.exchange_all(right)
    left = lay.permute(*left)
    h, fac = call(
        gate_kernel,
        [pltpu.VMEM((rows, width, cols), F32), pltpu.HBM((rows, 4 * width, cols), BF16)],
        [
            pltpu.VMEM((rows, 4 * width, cols), BF16),
            weight_t,
            half,
            half,
            row,
            row,
            weight,
            row,
            out_weight_here,
            pltpu.SemaphoreType.DMA((7,)),
            pltpu.SemaphoreType.DMA((PARTS,)),
        ],
        pair_act,
        cotangent,
        in_gain,
        in_bias,
        proj_weight,
        out_gain,
        out_weight,
        hbm=7,
    )
    right, h, fac = lax.optimization_barrier((right, h, fac))
    tri, left = call(functools.partial(tri_kernel, lay), [one, one], [], right, *left)
    tri = lay.exchange_half(tri)
    grad_tri, tri = call(
        functools.partial(tri_back_kernel, lay),
        [one, pltpu.HBM(one.shape, BF16)],
        [half, half, pltpu.SemaphoreType.DMA(())],
        tri,
        h,
    )
    grad_right, *grad_left = call(
        functools.partial(factor_back_kernel, lay),
        [pltpu.HBM(two_shape, BF16), some, some],
        [one_here, pltpu.VMEM(two_shape, BF16), pltpu.SemaphoreType.DMA((mine,))],
        lay.exchange_half(grad_tri),
        left,
        right,
    )
    grad_right = lay.exchange_all(grad_right)
    grad_left = lay.permute(*grad_left)
    grad_in_first, normed_first, fac_first, grad_in, normed_t, scale = call(
        functools.partial(logit_kernel, lay),
        [
            pltpu.VMEM((rows // PARTS, width, cols), F32),
            pltpu.VMEM((rows // PARTS, width, cols), BF16),
            pltpu.VMEM((rows // PARTS, 4 * width, cols), BF16),
            pltpu.HBM((rows, width, cols), F32),
            pltpu.HBM((rows, width, cols), BF16),
            pltpu.VMEM((rows, cols), F32),
        ],
        [
            half,
            pltpu.VMEM((rows, width, cols), F32),
            half,
            pltpu.SemaphoreType.DMA((2,)),
            one_here,
            half,
            half,
            row,
            row,
            weight,
            row,
            row,
            out_weight_here,
            pltpu.SemaphoreType.DMA((10,)),
        ],
        fac,
        tri,
        pair_act,
        cotangent,
        in_gain,
        in_bias,
        proj_weight,
        out_gain,
        out_bias,
        out_weight,
        hbm=10,
    )
    return call(
        functools.partial(pair_kernel, lay),
        pltpu.HBM((rows, cols, width), BF16),
        [
            one_here,
            half,
            half,
            pltpu.VMEM((rows, 4 * width, cols), BF16),
            half,
            pltpu.VMEM((rows, width, cols), F32),
            half,
            pltpu.SemaphoreType.DMA((4, PARTS)),
        ],
        fac,
        normed_t,
        grad_in,
        fac_first,
        normed_first,
        grad_in_first,
        grad_right,
        scale,
        in_gain,
        proj_weight,
        *grad_left,
        hbm=3,
    )


def by_row(
    pair_act, cotangent, in_gain, in_bias, proj_weight, out_gain, out_bias, out_weight
):
    rows_here, cols_here, width = pair_act.shape
    flat = pair_act.astype(jnp.float32).reshape(rows_here * cols_here, width)
    normed, scale_inv = normalize(flat, -1)
    normal_in = (normed * in_gain + in_bias).astype(jnp.bfloat16)
    projected = jnp.einsum("pd,de->ep", normal_in, proj_weight, preferred_element_type=jnp.float32)
    blocks = jnp.split(projected, 5, axis=0)
    left_sig = jax.nn.sigmoid(blocks[1])
    right_sig = jax.nn.sigmoid(blocks[3])
    left_fac = (left_sig * blocks[0]).astype(jnp.bfloat16).reshape(width, rows_here, cols_here)
    right_fac = (right_sig * blocks[2]).astype(jnp.bfloat16).reshape(width, rows_here, cols_here)
    left_chan, right_chan = (
        lax.all_to_all(left_fac, "ch", split_axis=0, concat_axis=2, tiled=True),
        lax.all_to_all(right_fac, "ch", split_axis=0, concat_axis=2, tiled=True),
    )
    tri_chan = jnp.einsum(
        "cik,cjk->cij",
        left_chan,
        lax.all_gather(right_chan, "row", axis=1, tiled=True),
        preferred_element_type=jnp.float32,
    ).astype(jnp.bfloat16)
    tri_back = lax.all_to_all(tri_chan, "ch", split_axis=2, concat_axis=0, tiled=True)
    tri_hat, tri_inv = normalize(tri_back.astype(jnp.float32).reshape(width, -1), 0)
    normal_out = (tri_hat * out_gain[:, None] + out_bias[:, None]).astype(jnp.bfloat16)
    mixed = jnp.einsum("cp,ce->ep", normal_out, out_weight, preferred_element_type=jnp.float32)
    out_gate = jax.nn.sigmoid(blocks[4])
    grad_out = cotangent.astype(jnp.float32).reshape(rows_here * cols_here, width).T
    grad_mixed = (grad_out * out_gate).astype(jnp.bfloat16)
    grad_logit = grad_out * mixed * out_gate * (1.0 - out_gate)
    grad_normal = jnp.einsum(
        "ep,ce->cp", grad_mixed, out_weight, preferred_element_type=jnp.float32
    )
    grad_tri = norm_back(grad_normal * out_gain[:, None], tri_hat, tri_inv, 0)
    grad_tri = grad_tri.astype(jnp.bfloat16).reshape(width, rows_here, cols_here)
    grad_chan = lax.all_to_all(grad_tri, "ch", split_axis=0, concat_axis=2, tiled=True)
    grad_cols = lax.all_to_all(grad_chan, "row", split_axis=2, concat_axis=1, tiled=True)
    grad_left = jnp.einsum(
        "cij,cjk->cik",
        grad_chan,
        lax.all_gather(right_chan, "row", axis=1, tiled=True),
        preferred_element_type=jnp.float32,
    )
    grad_right = jnp.einsum(
        "cij,cik->cjk",
        grad_cols,
        lax.all_gather(left_chan, "row", axis=1, tiled=True),
        preferred_element_type=jnp.float32,
    )
    left_back, right_back = (
        lax.all_to_all(
            grad_left.astype(jnp.bfloat16), "ch", split_axis=2, concat_axis=0, tiled=True
        ),
        lax.all_to_all(
            grad_right.astype(jnp.bfloat16), "ch", split_axis=2, concat_axis=0, tiled=True
        ),
    )
    left_grad = left_back.astype(jnp.float32).reshape(width, -1)
    right_grad = right_back.astype(jnp.float32).reshape(width, -1)
    grad_proj = jnp.concatenate(
        [
            left_grad * left_sig,
            left_grad * blocks[0] * left_sig * (1.0 - left_sig),
            right_grad * right_sig,
            right_grad * blocks[2] * right_sig * (1.0 - right_sig),
            grad_logit,
        ],
        axis=0,
    ).astype(jnp.bfloat16)
    grad_in = jnp.einsum("ep,de->pd", grad_proj, proj_weight, preferred_element_type=jnp.float32)
    grad_pair = norm_back(grad_in * in_gain, normed, scale_inv, -1)
    return grad_pair.astype(jnp.bfloat16).reshape(rows_here, cols_here, width)


def solution(mesh):
    n_row, n_ch = mesh.shape["row"], mesh.shape["ch"]
    placed = (P("row", "ch", None), P("row", "ch", None), P(), P(), P(), P(), P(), P())

    def on_device(*args):
        rows, cols, width = args[0].shape
        devices, outer, group = n_row * n_ch, math.isqrt(n_row), BLOCK // rows
        if (
            devices & (devices - 1) == 0
            and n_row >= 4
            and n_row % outer == 0
            and outer % 2 == 0
            and width % (devices // 2) == 0
            and rows % (2 * PARTS) == 0
            and BLOCK % rows == 0
            and group % (width // (devices // 2)) == 0
            and width % (2 * group) == 0
            and cols % 128 == 0
            and width <= 256
            and width & (width - 1) == 0
        ):
            return by_channel(n_row, n_ch, *args)
        return by_row(*args)

    return jax.shard_map(
        on_device, mesh=mesh, in_specs=placed, out_specs=P("row", "ch", None), check_vma=False
    )
```

```python
import functools
import math

import jax
import jax.numpy as jnp
from jax import lax
from jax.experimental import pallas as pl
from jax.experimental.pallas import tpu as pltpu
from jax.sharding import PartitionSpec as P

EPSILON = 1e-05
F32 = jnp.float32
BF16 = jnp.bfloat16
UNROLL = 4
BLOCK = 256
PARTS = 4


def dot(a, b, da, db):
    return lax.dot_general(a, b, (((da,), (db,)), ((), ())), preferred_element_type=F32)


def sigmoid(values):
    return 0.5 * jnp.tanh(0.5 * values) + 0.5


def normalize(values, axis):
    center = jnp.mean(values, axis=axis, keepdims=True)
    shifted = values - center
    scale_inv = lax.rsqrt(jnp.mean(shifted * shifted, axis=axis, keepdims=True) + EPSILON)
    return (shifted * scale_inv, scale_inv)


def norm_back(grad_hat, normed, scale_inv, axis):
    first = jnp.mean(grad_hat, axis=axis, keepdims=True)
    second = jnp.mean(grad_hat * normed, axis=axis, keepdims=True)
    return scale_inv * (grad_hat - first - normed * second)


def column(row, width):
    return jnp.broadcast_to(row, (width, row.shape[-1])).T


def call(kernel, outs, scratch, *args, hbm=0, limit=16):
    single = not isinstance(outs, (list, tuple))
    args = [pltpu.with_memory_space_constraint(a, pltpu.HBM) if n < hbm else a for n, a in enumerate(args)]
    specs = [pl.BlockSpec(memory_space=pltpu.HBM if n < hbm else pltpu.VMEM) for n in range(len(args))]
    out_specs = [
        pl.BlockSpec(memory_space=getattr(out, "memory_space", pltpu.VMEM))
        for out in ([outs] if single else outs)
    ]
    return pl.pallas_call(
        kernel,
        out_shape=outs if single else tuple(outs),
        in_specs=specs,
        out_specs=out_specs[0] if single else tuple(out_specs),
        scratch_shapes=scratch,
        compiler_params=pltpu.CompilerParams(vmem_limit_bytes=limit * 1024 * 1024),
    )(*args)


def permutation(outer, inner):
    to = lax.broadcasted_iota(jnp.int32, (BLOCK, BLOCK), 0)
    start = lax.broadcasted_iota(jnp.int32, (BLOCK, BLOCK), 1)
    return (start == to % inner * outer + to // inner).astype(F32).astype(BF16)


def identity(size):
    first = lax.broadcasted_iota(jnp.int32, (size, size), 0)
    return (first == lax.broadcasted_iota(jnp.int32, (size, size), 1)).astype(F32).astype(BF16)


def swapped(swap, blocks):
    cols = blocks[0].shape[-1]
    wide = jnp.concatenate([block.reshape(BLOCK, cols) for block in blocks], axis=1)
    wide = dot(swap, wide, 1, 0).astype(BF16)
    return [wide[:, n * cols : (n + 1) * cols] for n in range(len(blocks))]


def fetched(sources, targets, sems):
    copies = [
        pltpu.make_async_copy(source, target, sems.at[n])
        for n, (source, target) in enumerate(zip(sources, targets))
    ]
    for copy in copies:
        copy.start()
    for copy in copies:
        copy.wait()


def weight_copies(w_hbm, w_ref, first, sems):
    width = w_hbm.shape[0]
    return [
        pltpu.make_async_copy(
            w_hbm.at[:, (first + n) * width : (first + n + 1) * width],
            w_ref.at[:, n * width : (n + 1) * width],
            sems.at[n],
        )
        for n in range(2)
    ]


def right_kernel(
    lay, x_hbm, gain_hbm, bias_hbm, w_hbm, r_hbm, n_ref, x_ref, gain_ref, bias_ref, w_ref, wt_ref, r_ref, right_ref, sems, out_sems
):
    rows, cols, width = x_ref.shape
    mine = width // lay.half
    parts = sems.shape[0] - 4
    size = rows // parts

    def fetch(p):
        here = pl.ds(p * size, size)
        return pltpu.make_async_copy(x_hbm.at[here], x_ref.at[here], sems.at[4 + p])

    small = [
        pltpu.make_async_copy(gain_hbm, gain_ref, sems.at[2]),
        pltpu.make_async_copy(bias_hbm, bias_ref, sems.at[3]),
    ]
    weights = weight_copies(w_hbm, w_ref, 2, sems)
    fetch(0).start()
    for copy in small + weights:
        copy.start()
    for p in range(1, parts):
        fetch(p).start()
    group = BLOCK // rows
    swap = permutation(group, rows)

    def normal(p):
        fetch(p).wait()
        for n in range(0, size, 2):
            i = p * size + n
            shifted = dot(center, x_ref[pl.ds(i, 2)].reshape(2 * cols, width), 1, 1)
            scale_inv = lax.rsqrt(jnp.mean(shifted * shifted, axis=0, keepdims=True) + EPSILON)
            n_ref[p * size // 2 + n // 2] = (shifted * scale_inv * gain + bias).astype(BF16)

    def project(p):
        for n in range(0, size, 2):
            i = p * size + n
            proj = dot(wt_ref[...], n_ref[p * size // 2 + n // 2], 1, 0)
            right = (sigmoid(proj[width:]) * proj[:width]).astype(BF16)
            for m in range(2):
                r_ref[i + m] = right[:, m * cols : (m + 1) * cols]

    def body(p, _):
        normal(p)
        project(p - 1)
        return 0

    center = (identity(width).astype(F32) - 1.0 / width).astype(BF16)
    for copy in small:
        copy.wait()
    gain = column(gain_ref[...], 2 * cols)
    bias = column(bias_ref[...], 2 * cols)
    normal(0)
    for copy in weights:
        copy.wait()
    wt_ref[...] = w_ref[...].astype(F32).T.astype(BF16)
    lax.fori_loop(1, parts, body, 0)
    project(parts - 1)
    out = []
    blocks = places(width, mine, rows)
    for k in range(0, len(blocks), 2):
        pair = blocks[k : k + 2]
        for (to, _here), right in zip(pair, swapped(swap, [r_ref[:, here] for _to, here in pair])):
            right_ref[to] = right.reshape(group // mine, mine, rows, cols)
            for share in range(to.start, to.stop):
                for n, device in enumerate(lay.order):
                    if device % lay.half == share:
                        out.append(pltpu.make_async_copy(right_ref.at[share], r_hbm.at[n], out_sems.at[n]))
                        out[-1].start()
    for copy in out:
        copy.wait()


def left_kernel(lay, w_hbm, n_ref, mine_out, mate_out, w_ref, wt_ref, l_ref, left_ref, sems):
    rows, width, cols = l_ref.shape
    mine = width // lay.half
    group = BLOCK // rows
    weights = weight_copies(w_hbm, w_ref, 0, sems)
    for copy in weights:
        copy.start()
    for copy in weights:
        copy.wait()
    wt_ref[...] = w_ref[...].astype(F32).T.astype(BF16)
    swap = permutation(group, rows)

    def body(n, _):
        proj = dot(wt_ref[...], n_ref[n], 1, 0)
        left = (sigmoid(proj[width:]) * proj[:width]).astype(BF16)
        for m in range(2):
            l_ref[2 * n + m] = left[:, m * cols : (m + 1) * cols]
        return 0

    lax.fori_loop(0, rows // 2, body, 0, unroll=2)
    blocks = places(width, mine, rows)
    for k in range(0, len(blocks), 2):
        pair = blocks[k : k + 2]
        for (to, _here), left in zip(pair, swapped(swap, [l_ref[:, here] for _to, here in pair])):
            left_ref[to] = left.reshape(group // mine, mine, rows, cols)
    for n, s in enumerate(lay.hops):
        mine_out[n] = left_ref[lay.other(s)]
        mate_out[n] = left_ref[lay.other(s ^ lay.mate)]


def gate_kernel(*refs):
    sources, (h_ref, fac_hbm, fac_ref, wt_ref), targets, (sems, out_sems) = (
        refs[:7],
        refs[7:11],
        refs[11:18],
        refs[18:],
    )
    x_ref, cot_ref, gain_ref, bias_ref, w_ref, ogain_ref, ow_ref = targets
    rows, cols, width = x_ref.shape
    fetched(sources, targets, sems)
    wt_ref[...] = w_ref[:, : 4 * width].astype(F32).T.astype(BF16)
    ogain = column(ogain_ref[...], cols)

    def body(i, _):
        normed, _s = normalize(x_ref[i].astype(F32), -1)
        normal_in = (normed * gain_ref[...] + bias_ref[...]).astype(BF16)
        proj = dot(wt_ref[...], normal_in, 1, 1)
        for side in range(2):
            val = proj[2 * side * width : (2 * side + 1) * width]
            sig = sigmoid(proj[(2 * side + 1) * width : (2 * side + 2) * width])
            fac_ref[i, 2 * side * width : (2 * side + 1) * width] = sig.astype(BF16)
            fac_ref[i, (2 * side + 1) * width : (2 * side + 2) * width] = (
                val * sig * (1.0 - sig)
            ).astype(BF16)
        out_gate = sigmoid(dot(normal_in, w_ref[:, 4 * width :], 1, 0))
        grad_mixed = (cot_ref[i].astype(F32) * out_gate).astype(BF16)
        h_ref[i] = dot(ow_ref[...], grad_mixed, 1, 1) * ogain
        return 0

    size = rows // PARTS

    def send(p):
        here = pl.ds(p * size, size)
        return pltpu.make_async_copy(fac_ref.at[here], fac_hbm.at[here], out_sems.at[p])

    def part(p, _):
        for n in range(size):
            body(p * size + n, 0)
        send(p).start()
        return 0

    lax.fori_loop(0, PARTS, part, 0)
    for p in range(PARTS):
        send(p).wait()


def places(n_channels, mine, rows):
    group = BLOCK // rows
    return [
        (slice(c // mine, (c + group) // mine), slice(c, c + group)) for c in range(0, n_channels, group)
    ]


def to_rows(lay, t_ref, ts_ref):
    rows, width, cols = ts_ref.shape
    mine = t_ref.shape[1]
    group = BLOCK // rows
    swap = permutation(rows, group)
    blocks = places(width, mine, rows)
    for n in range(0, len(blocks), 2):
        pair = blocks[n : n + 2]
        for (_to, here), block in zip(pair, swapped(swap, [lay.shares(t_ref, to) for to, _here in pair])):
            ts_ref[:, here] = block.reshape(rows, group, cols)


def tri_back_kernel(lay, t_ref, h_ref, gt_ref, t_hbm, ts_ref, gs_ref, sem):
    rows, width, cols = h_ref.shape
    mine = t_ref.shape[1]
    group = BLOCK // rows
    copy = pltpu.make_async_copy(t_ref, t_hbm, sem)
    copy.start()
    back = permutation(group, rows)
    to_rows(lay, t_ref, ts_ref)

    def body(i, _):
        tri, h = ts_ref[i].astype(F32), h_ref[i]
        shifted = tri - jnp.mean(tri, axis=0, keepdims=True)
        first = jnp.mean(h, axis=0, keepdims=True)
        both = jnp.mean(h * shifted, axis=0, keepdims=True)
        tri_inv = lax.rsqrt(jnp.mean(shifted * shifted, axis=0, keepdims=True) + EPSILON)
        gs_ref[i] = (tri_inv * (h - first - shifted * (both * tri_inv * tri_inv))).astype(BF16)
        return 0

    lax.fori_loop(0, rows, body, 0, unroll=2 * UNROLL)
    blocks = places(width, mine, rows)
    for n in range(0, len(blocks), 2):
        pair = blocks[n : n + 2]
        for (to, _here), block in zip(pair, swapped(back, [gs_ref[:, here] for _to, here in pair])):
            block = block.reshape(group // mine, mine, rows, cols)
            for share in range(to.start, to.stop):
                gt_ref[lay.inside.index(share)] = block[share - to.start]
    copy.wait()


def logit_kernel(lay, *refs):
    (fac_hbm, *sources), refs = refs[:10], refs[10:]
    (gin0_ref, nt0_ref, fac0_ref, gin_hbm, nt_hbm, s_ref), refs = refs[:6], refs[6:]
    (ts_ref, gin_ref, nt_ref, out_sems), targets, sems = refs[:4], refs[4:13], refs[13]
    t_ref, x_ref, cot_ref, gain_ref, bias_ref, w_ref, ogain_ref, obias_ref, ow_ref = targets
    rows, cols, width = x_ref.shape
    first = pl.ds(0, nt0_ref.shape[0])
    fetched([*sources, fac_hbm.at[first]], [*targets, fac0_ref], sems)
    to_rows(lay, t_ref, ts_ref)
    ogain = column(ogain_ref[...], cols)
    obias = column(obias_ref[...], cols)

    def body(i, _):
        normed, scale_inv = normalize(x_ref[i].astype(F32), -1)
        normal_in = (normed * gain_ref[...] + bias_ref[...]).astype(BF16)
        out_gate = sigmoid(dot(normal_in, w_ref[:, 4 * width :], 1, 0))
        tri_hat, _s = normalize(ts_ref[i].astype(F32), 0)
        normal_out = (tri_hat * ogain + obias).astype(BF16)
        mixed = dot(normal_out, ow_ref[...], 0, 0)
        grad_logit = cot_ref[i].astype(F32) * mixed * out_gate * (1.0 - out_gate)
        gin_ref[i] = dot(w_ref[:, 4 * width :], grad_logit.astype(BF16), 1, 1)
        nt_ref[i] = normed.T.astype(BF16)
        s_ref[pl.ds(i, 1), :] = jnp.broadcast_to(scale_inv, (cols, width)).T[:1]
        return 0

    lax.fori_loop(0, rows, body, 0, unroll=UNROLL)
    gin0_ref[...] = gin_ref[first]
    nt0_ref[...] = nt_ref[first]
    copies = [
        pltpu.make_async_copy(gin_ref, gin_hbm, out_sems.at[0]),
        pltpu.make_async_copy(nt_ref, nt_hbm, out_sems.at[1]),
    ]
    for copy in copies:
        copy.start()
    for copy in copies:
        copy.wait()


def pair_kernel(
    lay, fac_hbm, nt_hbm, gin_hbm, fac0_ref, nt0_ref, gin0_ref, r_ref, s_ref, gain_ref, w_ref, *refs
):
    l_refs, refs = refs[: lay.n_hops], refs[lay.n_hops :]
    out_hbm, l_ref, ls_ref, rs_ref, fac_ref, nt_ref, gin_ref, out_ref, sems = refs
    rows, cols, width = out_ref.shape
    mine = width // lay.half
    parts = sems.shape[1]
    size = rows // parts

    def fetch(p):
        here = pl.ds(p * size, size)
        return [
            pltpu.make_async_copy(fac_hbm.at[here], fac_ref.at[here], sems.at[0, p]),
            pltpu.make_async_copy(nt_hbm.at[here], nt_ref.at[here], sems.at[1, p]),
            pltpu.make_async_copy(gin_hbm.at[here], gin_ref.at[here], sems.at[2, p]),
        ]

    def send(p):
        here = pl.ds(p * size, size)
        return pltpu.make_async_copy(out_ref.at[here], out_hbm.at[here], sems.at[3, p])

    for p in range(1, parts):
        for copy in fetch(p):
            copy.start()
    gain = column(gain_ref[...], cols)
    eye = identity(cols)
    group = BLOCK // rows
    swap = permutation(rows, group)
    for s, source in lay.received(l_refs):
        l_ref[lay.other(s)] = source[...]
    for to, here in places(width, mine, rows):
        sums = []
        for share in range(to.start, to.stop):
            one, two = (
                r_ref[n].astype(F32)
                for n, device in enumerate(lay.order)
                if device % lay.half == share
            )
            sums.append((one + two).astype(BF16))
        left, right = swapped(swap, [l_ref[to], jnp.stack(sums)])
        ls_ref[:, here] = left.reshape(rows, group, cols)
        rs_ref[:, here] = right.reshape(rows, group, cols)

    def part(p, fac_here, nt_here, gin_here):
        for n in range(0, size, 2):
            i = p * size + n
            blocks = []
            for m in range(2):
                left, right, fac = ls_ref[i + m], rs_ref[i + m], fac_here[i + m]
                blocks.append(
                    jnp.concatenate(
                        [
                            left * fac[:width],
                            left * fac[width : 2 * width],
                            right * fac[2 * width : 3 * width],
                            right * fac[3 * width :],
                        ],
                        axis=0,
                    )
                )
            grad_in = dot(w_ref[:, : 4 * width], jnp.concatenate(blocks, axis=1), 1, 0)
            for m in range(2):
                grad = (grad_in[:, m * cols : (m + 1) * cols] + gin_here[i + m]) * gain
                scale_inv = s_ref[pl.ds(i + m, 1), :]
                normed = nt_here[i + m].astype(F32)
                result = norm_back(grad, normed, scale_inv, 0).astype(BF16)
                out_ref[i + m] = dot(eye, result, 1, 1).astype(BF16)

    part(0, fac0_ref, nt0_ref, gin0_ref)
    send(0).start()
    for p in range(1, parts):
        for copy in fetch(p):
            copy.wait()
    for p in range(1, parts):
        part(p, fac_ref, nt_ref, gin_ref)
        send(p).start()
    for p in range(parts):
        send(p).wait()


class Layout:
    def __init__(self, n_row, n_ch):
        self.n_row, self.n_ch = n_row, n_ch
        self.devices = n_row * n_ch
        self.half = self.devices // 2
        outer = math.isqrt(n_row)
        self.inner = self.devices // outer
        self.order = [o * self.inner + n for n in range(self.inner) for o in range(outer)]
        self.inside = [o * self.inner + n for n in range(self.inner) for o in range(outer // 2)]
        self.mate = n_ch
        self.hops = [s for s in range(self.half) if s & self.mate == 0]
        self.hops[3:] = self.hops[:2:-1]
        self.n_hops = len(self.hops) + 1
        self.all_place = self.place(self.order, n_row)
        self.half_place = self.place(self.inside, n_row // 2)
        self.near_place = self.place(list(range(self.half)), n_row // 2)

    def place(self, order, n_row):
        return [[order.index(r * self.n_ch + b) for b in range(self.n_ch)] for r in range(n_row)]

    def shares(self, ref, here):
        return jnp.stack([ref[self.inside.index(share)] for share in range(here.start, here.stop)])

    def other(self, s):
        me = lax.axis_index("row") * self.n_ch + lax.axis_index("ch")
        return jnp.bitwise_xor(lax.rem(me, self.half), s)

    def exchange_all(self, blocks):
        return lax.all_to_all(
            blocks, ("row", "ch"), split_axis=0, concat_axis=0, tiled=True, axis_index_groups=[self.order]
        )

    def exchange_half(self, blocks):
        groups = [[first + n for n in self.inside] for first in (0, self.half)]
        return lax.all_to_all(
            blocks, ("row", "ch"), split_axis=0, concat_axis=0, tiled=True, axis_index_groups=groups
        )

    def swap(self, block, s):
        return lax.ppermute(block, ("row", "ch"), [(n, n ^ s) for n in range(self.devices)])

    def permute(self, mine, mates):
        mates = self.swap(mates, self.mate)
        shape = jax.ShapeDtypeStruct((2,) + mine.shape[1:], mine.dtype)
        pairs = call(merge_kernel, [shape] * (len(self.hops) - 1), [], mine, mates)
        return [mine, mates] + [self.swap(pair, s) for pair, s in zip(pairs, self.hops[1:])]

    def received(self, refs):
        mine, mates, *pairs = refs
        found = [(0, mine.at[0]), (self.mate, mates.at[0])]
        for s, pair in zip(self.hops[1:], pairs):
            found += [(s, pair.at[0]), (s ^ self.mate, pair.at[1])]
        return found


def merge_kernel(mine_ref, mates_ref, *outs):
    for n, out_ref in enumerate(outs, 1):
        out_ref[0] = mine_ref[n]
        out_ref[1] = mates_ref[n]


def plane(ref, place, c):
    return jnp.concatenate(
        [
            jnp.concatenate([ref[n, c] for n in column_of], axis=0)
            for column_of in zip(*place)
        ],
        axis=1,
    )


def store_plane(ref, place, c, value):
    rows, cols = ref.shape[-2:]
    for r, row_of in enumerate(place):
        for b, n in enumerate(row_of):
            ref[n, c] = value[r * rows : (r + 1) * rows, b * cols : (b + 1) * cols]


def tri_kernel(lay, r_ref, *refs):
    l_refs, (t_ref, l_ref) = refs[: lay.n_hops], refs[lay.n_hops :]
    for s, source in lay.received(l_refs):
        l_ref[lay.other(s)] = source[...]
    for c in range(t_ref.shape[1]):
        tri = dot(plane(l_ref, lay.near_place, c), plane(r_ref, lay.all_place, c), 1, 1)
        store_plane(t_ref, lay.half_place, c, tri.astype(BF16))


def factor_back_kernel(lay, gt_ref, l_ref, r_ref, gr_hbm, *refs):
    mine_out, mate_out, gl_ref, gr_ref, sems = refs
    copies = []
    for c in range(gt_ref.shape[1]):
        right = dot(plane(gt_ref, lay.half_place, c), plane(l_ref, lay.near_place, c), 0, 0)
        store_plane(gr_ref, lay.all_place, c, right.astype(BF16))
        here = (slice(None), c)
        copies.append(pltpu.make_async_copy(gr_ref.at[here], gr_hbm.at[here], sems.at[c]))
        copies[-1].start()
    for c in range(gt_ref.shape[1]):
        left = dot(plane(gt_ref, lay.half_place, c), plane(r_ref, lay.all_place, c), 1, 0)
        store_plane(gl_ref, lay.near_place, c, left.astype(BF16))
    for n, s in enumerate(lay.hops):
        mine_out[n] = gl_ref[lay.other(s)]
        mate_out[n] = gl_ref[lay.other(s ^ lay.mate)]
    for copy in copies:
        copy.wait()


def by_channel(
    n_row, n_ch, pair_act, cotangent, in_gain, in_bias, proj_weight, out_gain, out_bias, out_weight
):
    lay = Layout(n_row, n_ch)
    rows, cols, width = pair_act.shape
    mine = width // lay.half
    struct = jax.ShapeDtypeStruct
    half = pltpu.VMEM((rows, width, cols), BF16)
    weight_t = pltpu.VMEM((4 * width, width), BF16)
    in_gain, in_bias, out_gain, out_bias = (
        v.reshape(1, width) for v in (in_gain, in_bias, out_gain, out_bias)
    )

    some = struct((len(lay.hops), mine, rows, cols), BF16)
    one = struct((lay.half, mine, rows, cols), BF16)
    one_here = pltpu.VMEM(one.shape, BF16)
    two_shape = (lay.devices, mine, rows, cols)
    row = pltpu.VMEM((1, width), F32)
    weight = pltpu.VMEM(proj_weight.shape, BF16)
    out_weight_here = pltpu.VMEM((width, width), BF16)
    both_weights = pltpu.VMEM((width, 2 * width), BF16)
    both_turned = pltpu.VMEM((2 * width, width), BF16)
    right, normal_in = call(
        functools.partial(right_kernel, lay),
        [pltpu.HBM(two_shape, BF16), struct((rows // 2, width, 2 * cols), BF16)],
        [
            half,
            row,
            row,
            both_weights,
            both_turned,
            half,
            one_here,
            pltpu.SemaphoreType.DMA((4 + PARTS // 2,)),
            pltpu.SemaphoreType.DMA((lay.devices,)),
        ],
        pair_act,
        in_gain,
        in_bias,
        proj_weight,
        hbm=4,
    )
    left = call(
        functools.partial(left_kernel, lay),
        [some, some],
        [both_weights, both_turned, half, one_here, pltpu.SemaphoreType.DMA((2,))],
        proj_weight,
        normal_in,
        hbm=1,
    )
    right = lay.exchange_all(right)
    left = lay.permute(*left)
    h, fac = call(
        gate_kernel,
        [pltpu.VMEM((rows, width, cols), F32), pltpu.HBM((rows, 4 * width, cols), BF16)],
        [
            pltpu.VMEM((rows, 4 * width, cols), BF16),
            weight_t,
            half,
            half,
            row,
            row,
            weight,
            row,
            out_weight_here,
            pltpu.SemaphoreType.DMA((7,)),
            pltpu.SemaphoreType.DMA((PARTS,)),
        ],
        pair_act,
        cotangent,
        in_gain,
        in_bias,
        proj_weight,
        out_gain,
        out_weight,
        hbm=7,
    )
    right, h, fac = lax.optimization_barrier((right, h, fac))
    tri, left = call(functools.partial(tri_kernel, lay), [one, one], [], right, *left)
    tri = lay.exchange_half(tri)
    grad_tri, tri = call(
        functools.partial(tri_back_kernel, lay),
        [one, pltpu.HBM(one.shape, BF16)],
        [half, half, pltpu.SemaphoreType.DMA(())],
        tri,
        h,
    )
    grad_right, *grad_left = call(
        functools.partial(factor_back_kernel, lay),
        [pltpu.HBM(two_shape, BF16), some, some],
        [one_here, pltpu.VMEM(two_shape, BF16), pltpu.SemaphoreType.DMA((mine,))],
        lay.exchange_half(grad_tri),
        left,
        right,
    )
    grad_right = lay.exchange_all(grad_right)
    grad_left = lay.permute(*grad_left)
    grad_in_first, normed_first, fac_first, grad_in, normed_t, scale = call(
        functools.partial(logit_kernel, lay),
        [
            pltpu.VMEM((rows // PARTS, width, cols), F32),
            pltpu.VMEM((rows // PARTS, width, cols), BF16),
            pltpu.VMEM((rows // PARTS, 4 * width, cols), BF16),
            pltpu.HBM((rows, width, cols), F32),
            pltpu.HBM((rows, width, cols), BF16),
            pltpu.VMEM((rows, cols), F32),
        ],
        [
            half,
            pltpu.VMEM((rows, width, cols), F32),
            half,
            pltpu.SemaphoreType.DMA((2,)),
            one_here,
            half,
            half,
            row,
            row,
            weight,
            row,
            row,
            out_weight_here,
            pltpu.SemaphoreType.DMA((10,)),
        ],
        fac,
        tri,
        pair_act,
        cotangent,
        in_gain,
        in_bias,
        proj_weight,
        out_gain,
        out_bias,
        out_weight,
        hbm=10,
    )
    return call(
        functools.partial(pair_kernel, lay),
        pltpu.HBM((rows, cols, width), BF16),
        [
            one_here,
            half,
            half,
            pltpu.VMEM((rows, 4 * width, cols), BF16),
            half,
            pltpu.VMEM((rows, width, cols), F32),
            half,
            pltpu.SemaphoreType.DMA((4, PARTS)),
        ],
        fac,
        normed_t,
        grad_in,
        fac_first,
        normed_first,
        grad_in_first,
        grad_right,
        scale,
        in_gain,
        proj_weight,
        *grad_left,
        hbm=3,
    )


def by_row(
    pair_act, cotangent, in_gain, in_bias, proj_weight, out_gain, out_bias, out_weight
):
    rows_here, cols_here, width = pair_act.shape
    flat = pair_act.astype(jnp.float32).reshape(rows_here * cols_here, width)
    normed, scale_inv = normalize(flat, -1)
    normal_in = (normed * in_gain + in_bias).astype(jnp.bfloat16)
    projected = jnp.einsum("pd,de->ep", normal_in, proj_weight, preferred_element_type=jnp.float32)
    blocks = jnp.split(projected, 5, axis=0)
    left_sig = jax.nn.sigmoid(blocks[1])
    right_sig = jax.nn.sigmoid(blocks[3])
    left_fac = (left_sig * blocks[0]).astype(jnp.bfloat16).reshape(width, rows_here, cols_here)
    right_fac = (right_sig * blocks[2]).astype(jnp.bfloat16).reshape(width, rows_here, cols_here)
    left_chan, right_chan = (
        lax.all_to_all(left_fac, "ch", split_axis=0, concat_axis=2, tiled=True),
        lax.all_to_all(right_fac, "ch", split_axis=0, concat_axis=2, tiled=True),
    )
    tri_chan = jnp.einsum(
        "cik,cjk->cij",
        left_chan,
        lax.all_gather(right_chan, "row", axis=1, tiled=True),
        preferred_element_type=jnp.float32,
    ).astype(jnp.bfloat16)
    tri_back = lax.all_to_all(tri_chan, "ch", split_axis=2, concat_axis=0, tiled=True)
    tri_hat, tri_inv = normalize(tri_back.astype(jnp.float32).reshape(width, -1), 0)
    normal_out = (tri_hat * out_gain[:, None] + out_bias[:, None]).astype(jnp.bfloat16)
    mixed = jnp.einsum("cp,ce->ep", normal_out, out_weight, preferred_element_type=jnp.float32)
    out_gate = jax.nn.sigmoid(blocks[4])
    grad_out = cotangent.astype(jnp.float32).reshape(rows_here * cols_here, width).T
    grad_mixed = (grad_out * out_gate).astype(jnp.bfloat16)
    grad_logit = grad_out * mixed * out_gate * (1.0 - out_gate)
    grad_normal = jnp.einsum(
        "ep,ce->cp", grad_mixed, out_weight, preferred_element_type=jnp.float32
    )
    grad_tri = norm_back(grad_normal * out_gain[:, None], tri_hat, tri_inv, 0)
    grad_tri = grad_tri.astype(jnp.bfloat16).reshape(width, rows_here, cols_here)
    grad_chan = lax.all_to_all(grad_tri, "ch", split_axis=0, concat_axis=2, tiled=True)
    grad_cols = lax.all_to_all(grad_chan, "row", split_axis=2, concat_axis=1, tiled=True)
    grad_left = jnp.einsum(
        "cij,cjk->cik",
        grad_chan,
        lax.all_gather(right_chan, "row", axis=1, tiled=True),
        preferred_element_type=jnp.float32,
    )
    grad_right = jnp.einsum(
        "cij,cik->cjk",
        grad_cols,
        lax.all_gather(left_chan, "row", axis=1, tiled=True),
        preferred_element_type=jnp.float32,
    )
    left_back, right_back = (
        lax.all_to_all(
            grad_left.astype(jnp.bfloat16), "ch", split_axis=2, concat_axis=0, tiled=True
        ),
        lax.all_to_all(
            grad_right.astype(jnp.bfloat16), "ch", split_axis=2, concat_axis=0, tiled=True
        ),
    )
    left_grad = left_back.astype(jnp.float32).reshape(width, -1)
    right_grad = right_back.astype(jnp.float32).reshape(width, -1)
    grad_proj = jnp.concatenate(
        [
            left_grad * left_sig,
            left_grad * blocks[0] * left_sig * (1.0 - left_sig),
            right_grad * right_sig,
            right_grad * blocks[2] * right_sig * (1.0 - right_sig),
            grad_logit,
        ],
        axis=0,
    ).astype(jnp.bfloat16)
    grad_in = jnp.einsum("ep,de->pd", grad_proj, proj_weight, preferred_element_type=jnp.float32)
    grad_pair = norm_back(grad_in * in_gain, normed, scale_inv, -1)
    return grad_pair.astype(jnp.bfloat16).reshape(rows_here, cols_here, width)


def solution(mesh):
    n_row, n_ch = mesh.shape["row"], mesh.shape["ch"]
    placed = (P("row", "ch", None), P("row", "ch", None), P(), P(), P(), P(), P(), P())

    def on_device(*args):
        rows, cols, width = args[0].shape
        devices, outer, group = n_row * n_ch, math.isqrt(n_row), BLOCK // rows
        if (
            devices & (devices - 1) == 0
            and n_row >= 4
            and n_row % outer == 0
            and outer % 2 == 0
            and width % (devices // 2) == 0
            and rows % (2 * PARTS) == 0
            and BLOCK % rows == 0
            and group % (width // (devices // 2)) == 0
            and width % (2 * group) == 0
            and cols % 128 == 0
            and width <= 256
            and width & (width - 1) == 0
        ):
            return by_channel(n_row, n_ch, *args)
        return by_row(*args)

    return jax.shard_map(
        on_device, mesh=mesh, in_specs=placed, out_specs=P("row", "ch", None), check_vma=False
    )
```

```python
import functools
import math

import jax
import jax.numpy as jnp
from jax import lax
from jax.experimental import pallas as pl
from jax.experimental.pallas import tpu as pltpu
from jax.sharding import PartitionSpec as P

EPSILON = 1e-05
F32 = jnp.float32
BF16 = jnp.bfloat16
UNROLL = 4
BLOCK = 256
PARTS = 4


def dot(a, b, da, db):
    return lax.dot_general(a, b, (((da,), (db,)), ((), ())), preferred_element_type=F32)


def sigmoid(values):
    return 0.5 * jnp.tanh(0.5 * values) + 0.5


def normalize(values, axis):
    center = jnp.mean(values, axis=axis, keepdims=True)
    shifted = values - center
    scale_inv = lax.rsqrt(jnp.mean(shifted * shifted, axis=axis, keepdims=True) + EPSILON)
    return (shifted * scale_inv, scale_inv)


def norm_back(grad_hat, normed, scale_inv, axis):
    first = jnp.mean(grad_hat, axis=axis, keepdims=True)
    second = jnp.mean(grad_hat * normed, axis=axis, keepdims=True)
    return scale_inv * (grad_hat - first - normed * second)


def column(row, width):
    return jnp.broadcast_to(row, (width, row.shape[-1])).T


def call(kernel, outs, scratch, *args, hbm=0, limit=16):
    single = not isinstance(outs, (list, tuple))
    args = [pltpu.with_memory_space_constraint(a, pltpu.HBM) if n < hbm else a for n, a in enumerate(args)]
    specs = [pl.BlockSpec(memory_space=pltpu.HBM if n < hbm else pltpu.VMEM) for n in range(len(args))]
    out_specs = [
        pl.BlockSpec(memory_space=getattr(out, "memory_space", pltpu.VMEM))
        for out in ([outs] if single else outs)
    ]
    return pl.pallas_call(
        kernel,
        out_shape=outs if single else tuple(outs),
        in_specs=specs,
        out_specs=out_specs[0] if single else tuple(out_specs),
        scratch_shapes=scratch,
        compiler_params=pltpu.CompilerParams(vmem_limit_bytes=limit * 1024 * 1024),
    )(*args)


def permutation(outer, inner):
    to = lax.broadcasted_iota(jnp.int32, (BLOCK, BLOCK), 0)
    start = lax.broadcasted_iota(jnp.int32, (BLOCK, BLOCK), 1)
    return (start == to % inner * outer + to // inner).astype(F32).astype(BF16)


def identity(size):
    first = lax.broadcasted_iota(jnp.int32, (size, size), 0)
    return (first == lax.broadcasted_iota(jnp.int32, (size, size), 1)).astype(F32).astype(BF16)


def swapped(swap, blocks):
    cols = blocks[0].shape[-1]
    wide = jnp.concatenate([block.reshape(BLOCK, cols) for block in blocks], axis=1)
    wide = dot(swap, wide, 1, 0).astype(BF16)
    return [wide[:, n * cols : (n + 1) * cols] for n in range(len(blocks))]


def fetched(sources, targets, sems):
    copies = [
        pltpu.make_async_copy(source, target, sems.at[n])
        for n, (source, target) in enumerate(zip(sources, targets))
    ]
    for copy in copies:
        copy.start()
    for copy in copies:
        copy.wait()


def weight_copies(w_hbm, w_ref, first, sems):
    width = w_hbm.shape[0]
    return [
        pltpu.make_async_copy(
            w_hbm.at[:, (first + n) * width : (first + n + 1) * width],
            w_ref.at[:, n * width : (n + 1) * width],
            sems.at[n],
        )
        for n in range(2)
    ]


def right_kernel(
    lay, x_hbm, gain_hbm, bias_hbm, w_hbm, r_hbm, n_ref, x_ref, gain_ref, bias_ref, w_ref, wt_ref, r_ref, right_ref, sems, out_sems
):
    rows, cols, width = x_ref.shape
    mine = width // lay.half
    parts = (sems.shape[0] - 4) // 2
    size = rows // parts

    def fetch(p):
        copies = []
        for n in range(2):
            here = pl.ds(p * size + n * size // 2, size // 2)
            copies.append(pltpu.make_async_copy(x_hbm.at[here], x_ref.at[here], sems.at[4 + 2 * p + n]))
        return copies

    small = [
        pltpu.make_async_copy(gain_hbm, gain_ref, sems.at[2]),
        pltpu.make_async_copy(bias_hbm, bias_ref, sems.at[3]),
    ]
    weights = weight_copies(w_hbm, w_ref, 2, sems)
    for copy in fetch(0) + small + weights:
        copy.start()
    for p in range(1, parts):
        for copy in fetch(p):
            copy.start()
    group = BLOCK // rows
    swap = permutation(group, rows)

    def normal(p):
        for copy in fetch(p):
            copy.wait()
        for n in range(0, size, 2):
            i = p * size + n
            shifted = dot(center, x_ref[pl.ds(i, 2)].reshape(2 * cols, width), 1, 1)
            scale_inv = lax.rsqrt(jnp.mean(shifted * shifted, axis=0, keepdims=True) + EPSILON)
            n_ref[p * size // 2 + n // 2] = (shifted * scale_inv * gain + bias).astype(BF16)

    def project(p):
        for n in range(0, size, 2):
            i = p * size + n
            proj = dot(wt_ref[...], n_ref[p * size // 2 + n // 2], 1, 0)
            right = (sigmoid(proj[width:]) * proj[:width]).astype(BF16)
            for m in range(2):
                r_ref[i + m] = right[:, m * cols : (m + 1) * cols]

    def body(p, _):
        normal(p)
        project(p - 1)
        return 0

    center = (identity(width).astype(F32) - 1.0 / width).astype(BF16)
    for copy in small:
        copy.wait()
    gain = column(gain_ref[...], 2 * cols)
    bias = column(bias_ref[...], 2 * cols)
    normal(0)
    for copy in weights:
        copy.wait()
    wt_ref[...] = w_ref[...].astype(F32).T.astype(BF16)
    lax.fori_loop(1, parts, body, 0)
    project(parts - 1)
    out = []
    blocks = places(width, mine, rows)
    for k in range(0, len(blocks), 2):
        pair = blocks[k : k + 2]
        for (to, _here), right in zip(pair, swapped(swap, [r_ref[:, here] for _to, here in pair])):
            right_ref[to] = right.reshape(group // mine, mine, rows, cols)
            for share in range(to.start, to.stop):
                for n, device in enumerate(lay.order):
                    if device % lay.half == share:
                        out.append(pltpu.make_async_copy(right_ref.at[share], r_hbm.at[n], out_sems.at[n]))
                        out[-1].start()
    for copy in out:
        copy.wait()


def left_kernel(lay, w_hbm, n_ref, mine_out, mate_out, w_ref, wt_ref, l_ref, left_ref, sems):
    rows, width, cols = l_ref.shape
    mine = width // lay.half
    group = BLOCK // rows
    weights = weight_copies(w_hbm, w_ref, 0, sems)
    for copy in weights:
        copy.start()
    for copy in weights:
        copy.wait()
    wt_ref[...] = w_ref[...].astype(F32).T.astype(BF16)
    swap = permutation(group, rows)

    def body(n, _):
        proj = dot(wt_ref[...], n_ref[n], 1, 0)
        left = (sigmoid(proj[width:]) * proj[:width]).astype(BF16)
        for m in range(2):
            l_ref[2 * n + m] = left[:, m * cols : (m + 1) * cols]
        return 0

    lax.fori_loop(0, rows // 2, body, 0, unroll=2)
    blocks = places(width, mine, rows)
    for k in range(0, len(blocks), 2):
        pair = blocks[k : k + 2]
        for (to, _here), left in zip(pair, swapped(swap, [l_ref[:, here] for _to, here in pair])):
            left_ref[to] = left.reshape(group // mine, mine, rows, cols)
    for n, s in enumerate(lay.hops):
        mine_out[n] = left_ref[lay.other(s)]
        mate_out[n] = left_ref[lay.other(s ^ lay.mate)]


def gate_kernel(*refs):
    sources, (h_ref, fac_hbm, fac_ref, wt_ref), targets, (sems, out_sems) = (
        refs[:7],
        refs[7:11],
        refs[11:18],
        refs[18:],
    )
    x_ref, cot_ref, gain_ref, bias_ref, w_ref, ogain_ref, ow_ref = targets
    rows, cols, width = x_ref.shape
    fetched(sources, targets, sems)
    wt_ref[...] = w_ref[:, : 4 * width].astype(F32).T.astype(BF16)
    ogain = column(ogain_ref[...], cols)

    def body(i, _):
        normed, _s = normalize(x_ref[i].astype(F32), -1)
        normal_in = (normed * gain_ref[...] + bias_ref[...]).astype(BF16)
        proj = dot(wt_ref[...], normal_in, 1, 1)
        for side in range(2):
            val = proj[2 * side * width : (2 * side + 1) * width]
            sig = sigmoid(proj[(2 * side + 1) * width : (2 * side + 2) * width])
            fac_ref[i, 2 * side * width : (2 * side + 1) * width] = sig.astype(BF16)
            fac_ref[i, (2 * side + 1) * width : (2 * side + 2) * width] = (
                val * sig * (1.0 - sig)
            ).astype(BF16)
        out_gate = sigmoid(dot(normal_in, w_ref[:, 4 * width :], 1, 0))
        grad_mixed = (cot_ref[i].astype(F32) * out_gate).astype(BF16)
        h_ref[i] = dot(ow_ref[...], grad_mixed, 1, 1) * ogain
        return 0

    size = rows // PARTS

    def send(p):
        here = pl.ds(p * size, size)
        return pltpu.make_async_copy(fac_ref.at[here], fac_hbm.at[here], out_sems.at[p])

    def part(p, _):
        for n in range(size):
            body(p * size + n, 0)
        send(p).start()
        return 0

    lax.fori_loop(0, PARTS, part, 0)
    for p in range(PARTS):
        send(p).wait()


def places(n_channels, mine, rows):
    group = BLOCK // rows
    return [
        (slice(c // mine, (c + group) // mine), slice(c, c + group)) for c in range(0, n_channels, group)
    ]


def to_rows(lay, t_ref, ts_ref):
    rows, width, cols = ts_ref.shape
    mine = t_ref.shape[1]
    group = BLOCK // rows
    swap = permutation(rows, group)
    blocks = places(width, mine, rows)
    for n in range(0, len(blocks), 2):
        pair = blocks[n : n + 2]
        for (_to, here), block in zip(pair, swapped(swap, [lay.shares(t_ref, to) for to, _here in pair])):
            ts_ref[:, here] = block.reshape(rows, group, cols)


def split_copies(source, target, sems):
    parts = sems.shape[0]
    size = source.shape[0] // parts
    return [
        pltpu.make_async_copy(source.at[pl.ds(p * size, size)], target.at[pl.ds(p * size, size)], sems.at[p])
        for p in range(parts)
    ]


def tri_back_kernel(lay, t_ref, h_ref, gt_ref, t_hbm, ts_ref, gs_ref, sems):
    rows, width, cols = h_ref.shape
    mine = t_ref.shape[1]
    group = BLOCK // rows
    copies = split_copies(t_ref, t_hbm, sems)
    for copy in copies:
        copy.start()
    back = permutation(group, rows)
    to_rows(lay, t_ref, ts_ref)

    def body(i, _):
        tri, h = ts_ref[i].astype(F32), h_ref[i]
        shifted = tri - jnp.mean(tri, axis=0, keepdims=True)
        first = jnp.mean(h, axis=0, keepdims=True)
        both = jnp.mean(h * shifted, axis=0, keepdims=True)
        tri_inv = lax.rsqrt(jnp.mean(shifted * shifted, axis=0, keepdims=True) + EPSILON)
        gs_ref[i] = (tri_inv * (h - first - shifted * (both * tri_inv * tri_inv))).astype(BF16)
        return 0

    lax.fori_loop(0, rows, body, 0, unroll=2 * UNROLL)
    blocks = places(width, mine, rows)
    for n in range(0, len(blocks), 2):
        pair = blocks[n : n + 2]
        for (to, _here), block in zip(pair, swapped(back, [gs_ref[:, here] for _to, here in pair])):
            block = block.reshape(group // mine, mine, rows, cols)
            for share in range(to.start, to.stop):
                gt_ref[lay.inside.index(share)] = block[share - to.start]
    for copy in copies:
        copy.wait()


def logit_kernel(lay, *refs):
    (fac_hbm, *sources), refs = refs[:10], refs[10:]
    (gin0_ref, nt0_ref, fac0_ref, gin_hbm, nt_hbm, s_ref), refs = refs[:6], refs[6:]
    (ts_ref, gin_ref, nt_ref, out_sems), targets, sems = refs[:4], refs[4:13], refs[13]
    t_ref, x_ref, cot_ref, gain_ref, bias_ref, w_ref, ogain_ref, obias_ref, ow_ref = targets
    rows, cols, width = x_ref.shape
    first = pl.ds(0, nt0_ref.shape[0])
    fetched([*sources, fac_hbm.at[first]], [*targets, fac0_ref], sems)
    to_rows(lay, t_ref, ts_ref)
    ogain = column(ogain_ref[...], cols)
    obias = column(obias_ref[...], cols)

    def body(i, _):
        normed, scale_inv = normalize(x_ref[i].astype(F32), -1)
        normal_in = (normed * gain_ref[...] + bias_ref[...]).astype(BF16)
        out_gate = sigmoid(dot(normal_in, w_ref[:, 4 * width :], 1, 0))
        tri_hat, _s = normalize(ts_ref[i].astype(F32), 0)
        normal_out = (tri_hat * ogain + obias).astype(BF16)
        mixed = dot(normal_out, ow_ref[...], 0, 0)
        grad_logit = cot_ref[i].astype(F32) * mixed * out_gate * (1.0 - out_gate)
        gin_ref[i] = dot(w_ref[:, 4 * width :], grad_logit.astype(BF16), 1, 1)
        nt_ref[i] = normed.T.astype(BF16)
        s_ref[pl.ds(i, 1), :] = jnp.broadcast_to(scale_inv, (cols, width)).T[:1]
        return 0

    lax.fori_loop(0, rows, body, 0, unroll=UNROLL)
    gin0_ref[...] = gin_ref[first]
    nt0_ref[...] = nt_ref[first]
    copies = [
        pltpu.make_async_copy(gin_ref, gin_hbm, out_sems.at[0]),
        pltpu.make_async_copy(nt_ref, nt_hbm, out_sems.at[1]),
    ]
    for copy in copies:
        copy.start()
    for copy in copies:
        copy.wait()


def pair_kernel(
    lay, fac_hbm, nt_hbm, gin_hbm, fac0_ref, nt0_ref, gin0_ref, r_ref, s_ref, gain_ref, w_ref, *refs
):
    l_refs, refs = refs[: lay.n_hops], refs[lay.n_hops :]
    out_hbm, l_ref, ls_ref, rs_ref, fac_ref, nt_ref, gin_ref, out_ref, sems = refs
    rows, cols, width = out_ref.shape
    mine = width // lay.half
    parts = sems.shape[1]
    size = rows // parts

    def fetch(p):
        here = pl.ds(p * size, size)
        return [
            pltpu.make_async_copy(fac_hbm.at[here], fac_ref.at[here], sems.at[0, p]),
            pltpu.make_async_copy(nt_hbm.at[here], nt_ref.at[here], sems.at[1, p]),
            pltpu.make_async_copy(gin_hbm.at[here], gin_ref.at[here], sems.at[2, p]),
        ]

    def send(p):
        here = pl.ds(p * size, size)
        return pltpu.make_async_copy(out_ref.at[here], out_hbm.at[here], sems.at[3, p])

    for p in range(1, parts):
        for copy in fetch(p):
            copy.start()
    gain = column(gain_ref[...], cols)
    eye = identity(cols)
    group = BLOCK // rows
    swap = permutation(rows, group)
    for s, source in lay.received(l_refs):
        l_ref[lay.other(s)] = source[...]
    for to, here in places(width, mine, rows):
        sums = []
        for share in range(to.start, to.stop):
            one, two = (
                r_ref[n].astype(F32)
                for n, device in enumerate(lay.order)
                if device % lay.half == share
            )
            sums.append((one + two).astype(BF16))
        left, right = swapped(swap, [l_ref[to], jnp.stack(sums)])
        ls_ref[:, here] = left.reshape(rows, group, cols)
        rs_ref[:, here] = right.reshape(rows, group, cols)

    def part(p, fac_here, nt_here, gin_here):
        for n in range(0, size, 2):
            i = p * size + n
            blocks = []
            for m in range(2):
                left, right, fac = ls_ref[i + m], rs_ref[i + m], fac_here[i + m]
                blocks.append(
                    jnp.concatenate(
                        [
                            left * fac[:width],
                            left * fac[width : 2 * width],
                            right * fac[2 * width : 3 * width],
                            right * fac[3 * width :],
                        ],
                        axis=0,
                    )
                )
            grad_in = dot(w_ref[:, : 4 * width], jnp.concatenate(blocks, axis=1), 1, 0)
            for m in range(2):
                grad = (grad_in[:, m * cols : (m + 1) * cols] + gin_here[i + m]) * gain
                scale_inv = s_ref[pl.ds(i + m, 1), :]
                normed = nt_here[i + m].astype(F32)
                result = norm_back(grad, normed, scale_inv, 0).astype(BF16)
                out_ref[i + m] = dot(eye, result, 1, 1).astype(BF16)

    part(0, fac0_ref, nt0_ref, gin0_ref)
    send(0).start()
    for p in range(1, parts):
        for copy in fetch(p):
            copy.wait()
    for p in range(1, parts):
        part(p, fac_ref, nt_ref, gin_ref)
        send(p).start()
    for p in range(parts):
        send(p).wait()


class Layout:
    def __init__(self, n_row, n_ch):
        self.n_row, self.n_ch = n_row, n_ch
        self.devices = n_row * n_ch
        self.half = self.devices // 2
        outer = math.isqrt(n_row)
        self.inner = self.devices // outer
        self.order = [o * self.inner + n for n in range(self.inner) for o in range(outer)]
        self.inside = [o * self.inner + n for n in range(self.inner) for o in range(outer // 2)]
        self.mate = n_ch
        self.hops = [s for s in range(self.half) if s & self.mate == 0]
        self.hops[3:] = self.hops[:2:-1]
        self.n_hops = len(self.hops) + 1
        self.all_place = self.place(self.order, n_row)
        self.half_place = self.place(self.inside, n_row // 2)
        self.near_place = self.place(list(range(self.half)), n_row // 2)

    def place(self, order, n_row):
        return [[order.index(r * self.n_ch + b) for b in range(self.n_ch)] for r in range(n_row)]

    def shares(self, ref, here):
        return jnp.stack([ref[self.inside.index(share)] for share in range(here.start, here.stop)])

    def other(self, s):
        me = lax.axis_index("row") * self.n_ch + lax.axis_index("ch")
        return jnp.bitwise_xor(lax.rem(me, self.half), s)

    def exchange_all(self, blocks):
        return lax.all_to_all(
            blocks, ("row", "ch"), split_axis=0, concat_axis=0, tiled=True, axis_index_groups=[self.order]
        )

    def exchange_half(self, blocks):
        groups = [[first + n for n in self.inside] for first in (0, self.half)]
        return lax.all_to_all(
            blocks, ("row", "ch"), split_axis=0, concat_axis=0, tiled=True, axis_index_groups=groups
        )

    def swap(self, block, s):
        return lax.ppermute(block, ("row", "ch"), [(n, n ^ s) for n in range(self.devices)])

    def permute(self, mine, mates):
        mates = self.swap(mates, self.mate)
        shape = jax.ShapeDtypeStruct((2,) + mine.shape[1:], mine.dtype)
        pairs = call(merge_kernel, [shape] * (len(self.hops) - 1), [], mine, mates)
        return [mine, mates] + [self.swap(pair, s) for pair, s in zip(pairs, self.hops[1:])]

    def received(self, refs):
        mine, mates, *pairs = refs
        found = [(0, mine.at[0]), (self.mate, mates.at[0])]
        for s, pair in zip(self.hops[1:], pairs):
            found += [(s, pair.at[0]), (s ^ self.mate, pair.at[1])]
        return found


def merge_kernel(mine_ref, mates_ref, *outs):
    for n, out_ref in enumerate(outs, 1):
        out_ref[0] = mine_ref[n]
        out_ref[1] = mates_ref[n]


def plane(ref, place, c):
    return jnp.concatenate(
        [
            jnp.concatenate([ref[n, c] for n in column_of], axis=0)
            for column_of in zip(*place)
        ],
        axis=1,
    )


def store_plane(ref, place, c, value):
    rows, cols = ref.shape[-2:]
    for r, row_of in enumerate(place):
        for b, n in enumerate(row_of):
            ref[n, c] = value[r * rows : (r + 1) * rows, b * cols : (b + 1) * cols]


def tri_kernel(lay, r_ref, *refs):
    l_refs, (t_ref, l_ref) = refs[: lay.n_hops], refs[lay.n_hops :]
    for s, source in lay.received(l_refs):
        l_ref[lay.other(s)] = source[...]
    for c in range(t_ref.shape[1]):
        tri = dot(plane(l_ref, lay.near_place, c), plane(r_ref, lay.all_place, c), 1, 1)
        store_plane(t_ref, lay.half_place, c, tri.astype(BF16))


def right_back_kernel(lay, gt_ref, l_ref, gr_hbm, gr_ref, sems):
    copies = []
    for c in range(gt_ref.shape[1]):
        right = dot(plane(gt_ref, lay.half_place, c), plane(l_ref, lay.near_place, c), 0, 0)
        store_plane(gr_ref, lay.all_place, c, right.astype(BF16))
        here = (slice(None), c)
        copies.append(pltpu.make_async_copy(gr_ref.at[here], gr_hbm.at[here], sems.at[c]))
        copies[-1].start()
    for copy in copies:
        copy.wait()


def left_back_kernel(lay, gt_ref, r_ref, mine_out, mate_out, gl_ref):
    for c in range(gt_ref.shape[1]):
        left = dot(plane(gt_ref, lay.half_place, c), plane(r_ref, lay.all_place, c), 1, 0)
        store_plane(gl_ref, lay.near_place, c, left.astype(BF16))
    for n, s in enumerate(lay.hops):
        mine_out[n] = gl_ref[lay.other(s)]
        mate_out[n] = gl_ref[lay.other(s ^ lay.mate)]


def by_channel(
    n_row, n_ch, pair_act, cotangent, in_gain, in_bias, proj_weight, out_gain, out_bias, out_weight
):
    lay = Layout(n_row, n_ch)
    rows, cols, width = pair_act.shape
    mine = width // lay.half
    struct = jax.ShapeDtypeStruct
    half = pltpu.VMEM((rows, width, cols), BF16)
    weight_t = pltpu.VMEM((4 * width, width), BF16)
    in_gain, in_bias, out_gain, out_bias = (
        v.reshape(1, width) for v in (in_gain, in_bias, out_gain, out_bias)
    )

    some = struct((len(lay.hops), mine, rows, cols), BF16)
    one = struct((lay.half, mine, rows, cols), BF16)
    one_here = pltpu.VMEM(one.shape, BF16)
    two_shape = (lay.devices, mine, rows, cols)
    row = pltpu.VMEM((1, width), F32)
    weight = pltpu.VMEM(proj_weight.shape, BF16)
    out_weight_here = pltpu.VMEM((width, width), BF16)
    both_weights = pltpu.VMEM((width, 2 * width), BF16)
    both_turned = pltpu.VMEM((2 * width, width), BF16)
    right, normal_in = call(
        functools.partial(right_kernel, lay),
        [pltpu.HBM(two_shape, BF16), struct((rows // 2, width, 2 * cols), BF16)],
        [
            half,
            row,
            row,
            both_weights,
            both_turned,
            half,
            one_here,
            pltpu.SemaphoreType.DMA((4 + PARTS,)),
            pltpu.SemaphoreType.DMA((lay.devices,)),
        ],
        pair_act,
        in_gain,
        in_bias,
        proj_weight,
        hbm=4,
    )
    left = call(
        functools.partial(left_kernel, lay),
        [some, some],
        [both_weights, both_turned, half, one_here, pltpu.SemaphoreType.DMA((2,))],
        proj_weight,
        normal_in,
        hbm=1,
    )
    right = lay.exchange_all(right)
    left = lay.permute(*left)
    h, fac = call(
        gate_kernel,
        [pltpu.VMEM((rows, width, cols), F32), pltpu.HBM((rows, 4 * width, cols), BF16)],
        [
            pltpu.VMEM((rows, 4 * width, cols), BF16),
            weight_t,
            half,
            half,
            row,
            row,
            weight,
            row,
            out_weight_here,
            pltpu.SemaphoreType.DMA((7,)),
            pltpu.SemaphoreType.DMA((PARTS,)),
        ],
        pair_act,
        cotangent,
        in_gain,
        in_bias,
        proj_weight,
        out_gain,
        out_weight,
        hbm=7,
    )
    right, h, fac = lax.optimization_barrier((right, h, fac))
    tri, left = call(functools.partial(tri_kernel, lay), [one, one], [], right, *left)
    tri = lay.exchange_half(tri)
    grad_tri, tri = call(
        functools.partial(tri_back_kernel, lay),
        [one, pltpu.HBM(one.shape, BF16)],
        [half, half, pltpu.SemaphoreType.DMA((PARTS,))],
        tri,
        h,
    )
    grad_tri = lay.exchange_half(grad_tri)
    grad_right = call(
        functools.partial(right_back_kernel, lay),
        pltpu.HBM(two_shape, BF16),
        [pltpu.VMEM(two_shape, BF16), pltpu.SemaphoreType.DMA((mine,))],
        grad_tri,
        left,
    )
    grad_left = call(
        functools.partial(left_back_kernel, lay), [some, some], [one_here], grad_tri, right
    )
    grad_right = lay.exchange_all(grad_right)
    grad_left = lay.permute(*grad_left)
    grad_in_first, normed_first, fac_first, grad_in, normed_t, scale = call(
        functools.partial(logit_kernel, lay),
        [
            pltpu.VMEM((rows // PARTS, width, cols), F32),
            pltpu.VMEM((rows // PARTS, width, cols), BF16),
            pltpu.VMEM((rows // PARTS, 4 * width, cols), BF16),
            pltpu.HBM((rows, width, cols), F32),
            pltpu.HBM((rows, width, cols), BF16),
            pltpu.VMEM((rows, cols), F32),
        ],
        [
            half,
            pltpu.VMEM((rows, width, cols), F32),
            half,
            pltpu.SemaphoreType.DMA((2,)),
            one_here,
            half,
            half,
            row,
            row,
            weight,
            row,
            row,
            out_weight_here,
            pltpu.SemaphoreType.DMA((10,)),
        ],
        fac,
        tri,
        pair_act,
        cotangent,
        in_gain,
        in_bias,
        proj_weight,
        out_gain,
        out_bias,
        out_weight,
        hbm=10,
    )
    return call(
        functools.partial(pair_kernel, lay),
        pltpu.HBM((rows, cols, width), BF16),
        [
            one_here,
            half,
            half,
            pltpu.VMEM((rows, 4 * width, cols), BF16),
            half,
            pltpu.VMEM((rows, width, cols), F32),
            half,
            pltpu.SemaphoreType.DMA((4, PARTS)),
        ],
        fac,
        normed_t,
        grad_in,
        fac_first,
        normed_first,
        grad_in_first,
        grad_right,
        scale,
        in_gain,
        proj_weight,
        *grad_left,
        hbm=3,
    )


def by_row(
    pair_act, cotangent, in_gain, in_bias, proj_weight, out_gain, out_bias, out_weight
):
    rows_here, cols_here, width = pair_act.shape
    flat = pair_act.astype(jnp.float32).reshape(rows_here * cols_here, width)
    normed, scale_inv = normalize(flat, -1)
    normal_in = (normed * in_gain + in_bias).astype(jnp.bfloat16)
    projected = jnp.einsum("pd,de->ep", normal_in, proj_weight, preferred_element_type=jnp.float32)
    blocks = jnp.split(projected, 5, axis=0)
    left_sig = jax.nn.sigmoid(blocks[1])
    right_sig = jax.nn.sigmoid(blocks[3])
    left_fac = (left_sig * blocks[0]).astype(jnp.bfloat16).reshape(width, rows_here, cols_here)
    right_fac = (right_sig * blocks[2]).astype(jnp.bfloat16).reshape(width, rows_here, cols_here)
    left_chan, right_chan = (
        lax.all_to_all(left_fac, "ch", split_axis=0, concat_axis=2, tiled=True),
        lax.all_to_all(right_fac, "ch", split_axis=0, concat_axis=2, tiled=True),
    )
    tri_chan = jnp.einsum(
        "cik,cjk->cij",
        left_chan,
        lax.all_gather(right_chan, "row", axis=1, tiled=True),
        preferred_element_type=jnp.float32,
    ).astype(jnp.bfloat16)
    tri_back = lax.all_to_all(tri_chan, "ch", split_axis=2, concat_axis=0, tiled=True)
    tri_hat, tri_inv = normalize(tri_back.astype(jnp.float32).reshape(width, -1), 0)
    normal_out = (tri_hat * out_gain[:, None] + out_bias[:, None]).astype(jnp.bfloat16)
    mixed = jnp.einsum("cp,ce->ep", normal_out, out_weight, preferred_element_type=jnp.float32)
    out_gate = jax.nn.sigmoid(blocks[4])
    grad_out = cotangent.astype(jnp.float32).reshape(rows_here * cols_here, width).T
    grad_mixed = (grad_out * out_gate).astype(jnp.bfloat16)
    grad_logit = grad_out * mixed * out_gate * (1.0 - out_gate)
    grad_normal = jnp.einsum(
        "ep,ce->cp", grad_mixed, out_weight, preferred_element_type=jnp.float32
    )
    grad_tri = norm_back(grad_normal * out_gain[:, None], tri_hat, tri_inv, 0)
    grad_tri = grad_tri.astype(jnp.bfloat16).reshape(width, rows_here, cols_here)
    grad_chan = lax.all_to_all(grad_tri, "ch", split_axis=0, concat_axis=2, tiled=True)
    grad_cols = lax.all_to_all(grad_chan, "row", split_axis=2, concat_axis=1, tiled=True)
    grad_left = jnp.einsum(
        "cij,cjk->cik",
        grad_chan,
        lax.all_gather(right_chan, "row", axis=1, tiled=True),
        preferred_element_type=jnp.float32,
    )
    grad_right = jnp.einsum(
        "cij,cik->cjk",
        grad_cols,
        lax.all_gather(left_chan, "row", axis=1, tiled=True),
        preferred_element_type=jnp.float32,
    )
    left_back, right_back = (
        lax.all_to_all(
            grad_left.astype(jnp.bfloat16), "ch", split_axis=2, concat_axis=0, tiled=True
        ),
        lax.all_to_all(
            grad_right.astype(jnp.bfloat16), "ch", split_axis=2, concat_axis=0, tiled=True
        ),
    )
    left_grad = left_back.astype(jnp.float32).reshape(width, -1)
    right_grad = right_back.astype(jnp.float32).reshape(width, -1)
    grad_proj = jnp.concatenate(
        [
            left_grad * left_sig,
            left_grad * blocks[0] * left_sig * (1.0 - left_sig),
            right_grad * right_sig,
            right_grad * blocks[2] * right_sig * (1.0 - right_sig),
            grad_logit,
        ],
        axis=0,
    ).astype(jnp.bfloat16)
    grad_in = jnp.einsum("ep,de->pd", grad_proj, proj_weight, preferred_element_type=jnp.float32)
    grad_pair = norm_back(grad_in * in_gain, normed, scale_inv, -1)
    return grad_pair.astype(jnp.bfloat16).reshape(rows_here, cols_here, width)


def solution(mesh):
    n_row, n_ch = mesh.shape["row"], mesh.shape["ch"]
    placed = (P("row", "ch", None), P("row", "ch", None), P(), P(), P(), P(), P(), P())

    def on_device(*args):
        rows, cols, width = args[0].shape
        devices, outer, group = n_row * n_ch, math.isqrt(n_row), BLOCK // rows
        if (
            devices & (devices - 1) == 0
            and n_row >= 4
            and n_row % outer == 0
            and outer % 2 == 0
            and width % (devices // 2) == 0
            and rows % (2 * PARTS) == 0
            and BLOCK % rows == 0
            and group % (width // (devices // 2)) == 0
            and width % (2 * group) == 0
            and cols % 128 == 0
            and width <= 256
            and width & (width - 1) == 0
        ):
            return by_channel(n_row, n_ch, *args)
        return by_row(*args)

    return jax.shard_map(
        on_device, mesh=mesh, in_specs=placed, out_specs=P("row", "ch", None), check_vma=False
    )
```

```python
import functools
import math

import jax
import jax.numpy as jnp
from jax import lax
from jax.experimental import pallas as pl
from jax.experimental.pallas import tpu as pltpu
from jax.sharding import PartitionSpec as P

EPSILON = 1e-05
F32 = jnp.float32
BF16 = jnp.bfloat16
UNROLL = 4
BLOCK = 256
PARTS = 4


def dot(a, b, da, db):
    return lax.dot_general(a, b, (((da,), (db,)), ((), ())), preferred_element_type=F32)


def sigmoid(values):
    return 0.5 * jnp.tanh(0.5 * values) + 0.5


def normalize(values, axis):
    center = jnp.mean(values, axis=axis, keepdims=True)
    shifted = values - center
    scale_inv = lax.rsqrt(jnp.mean(shifted * shifted, axis=axis, keepdims=True) + EPSILON)
    return (shifted * scale_inv, scale_inv)


def norm_back(grad_hat, normed, scale_inv, axis):
    first = jnp.mean(grad_hat, axis=axis, keepdims=True)
    second = jnp.mean(grad_hat * normed, axis=axis, keepdims=True)
    return scale_inv * (grad_hat - first - normed * second)


def column(row, width):
    return jnp.broadcast_to(row, (width, row.shape[-1])).T


def call(kernel, outs, scratch, *args, hbm=0, limit=16):
    single = not isinstance(outs, (list, tuple))
    args = [pltpu.with_memory_space_constraint(a, pltpu.HBM) if n < hbm else a for n, a in enumerate(args)]
    specs = [pl.BlockSpec(memory_space=pltpu.HBM if n < hbm else pltpu.VMEM) for n in range(len(args))]
    out_specs = [
        pl.BlockSpec(memory_space=getattr(out, "memory_space", pltpu.VMEM))
        for out in ([outs] if single else outs)
    ]
    return pl.pallas_call(
        kernel,
        out_shape=outs if single else tuple(outs),
        in_specs=specs,
        out_specs=out_specs[0] if single else tuple(out_specs),
        scratch_shapes=scratch,
        compiler_params=pltpu.CompilerParams(vmem_limit_bytes=limit * 1024 * 1024),
    )(*args)


def permutation(outer, inner):
    to = lax.broadcasted_iota(jnp.int32, (BLOCK, BLOCK), 0)
    start = lax.broadcasted_iota(jnp.int32, (BLOCK, BLOCK), 1)
    return (start == to % inner * outer + to // inner).astype(F32).astype(BF16)


def identity(size):
    first = lax.broadcasted_iota(jnp.int32, (size, size), 0)
    return (first == lax.broadcasted_iota(jnp.int32, (size, size), 1)).astype(F32).astype(BF16)


def swapped(swap, blocks):
    cols = blocks[0].shape[-1]
    wide = jnp.concatenate([block.reshape(BLOCK, cols) for block in blocks], axis=1)
    wide = dot(swap, wide, 1, 0).astype(BF16)
    return [wide[:, n * cols : (n + 1) * cols] for n in range(len(blocks))]


def fetched(sources, targets, sems):
    copies = [
        pltpu.make_async_copy(source, target, sems.at[n])
        for n, (source, target) in enumerate(zip(sources, targets))
    ]
    for copy in copies:
        copy.start()
    for copy in copies:
        copy.wait()


def weight_copies(w_hbm, w_ref, first, sems):
    width = w_hbm.shape[0]
    return [
        pltpu.make_async_copy(
            w_hbm.at[:, (first + n) * width : (first + n + 1) * width],
            w_ref.at[:, n * width : (n + 1) * width],
            sems.at[n],
        )
        for n in range(2)
    ]


def right_kernel(
    lay, x_hbm, gain_hbm, bias_hbm, w_hbm, r_hbm, n_ref, x_ref, gain_ref, bias_ref, w_ref, wt_ref, r_ref, right_ref, sems, out_sems
):
    rows, cols, width = x_ref.shape
    mine = width // lay.half
    parts = sems.shape[0] - 4
    size = rows // parts

    def fetch(p):
        here = pl.ds(p * size, size)
        return pltpu.make_async_copy(x_hbm.at[here], x_ref.at[here], sems.at[4 + p])

    small = [
        pltpu.make_async_copy(gain_hbm, gain_ref, sems.at[2]),
        pltpu.make_async_copy(bias_hbm, bias_ref, sems.at[3]),
    ]
    weights = weight_copies(w_hbm, w_ref, 2, sems)
    fetch(0).start()
    for copy in small + weights:
        copy.start()
    for p in range(1, parts):
        fetch(p).start()
    group = BLOCK // rows
    swap = permutation(group, rows)

    def normal(p):
        fetch(p).wait()
        for n in range(0, size, 2):
            i = p * size + n
            shifted = dot(center, x_ref[pl.ds(i, 2)].reshape(2 * cols, width), 1, 1)
            scale_inv = lax.rsqrt(jnp.mean(shifted * shifted, axis=0, keepdims=True) + EPSILON)
            n_ref[p * size // 2 + n // 2] = (shifted * scale_inv * gain + bias).astype(BF16)

    def project(p):
        for n in range(0, size, 2):
            i = p * size + n
            proj = dot(wt_ref[...], n_ref[p * size // 2 + n // 2], 1, 0)
            right = (sigmoid(proj[width:]) * proj[:width]).astype(BF16)
            for m in range(2):
                r_ref[i + m] = right[:, m * cols : (m + 1) * cols]

    def body(p, _):
        normal(p)
        project(p - 1)
        return 0

    center = (identity(width).astype(F32) - 1.0 / width).astype(BF16)
    for copy in small:
        copy.wait()
    gain = column(gain_ref[...], 2 * cols)
    bias = column(bias_ref[...], 2 * cols)
    normal(0)
    for copy in weights:
        copy.wait()
    wt_ref[...] = w_ref[...].astype(F32).T.astype(BF16)
    lax.fori_loop(1, parts, body, 0)
    project(parts - 1)
    out = []
    blocks = places(width, mine, rows)
    for k in range(0, len(blocks), 2):
        pair = blocks[k : k + 2]
        for (to, _here), right in zip(pair, swapped(swap, [r_ref[:, here] for _to, here in pair])):
            right_ref[to] = right.reshape(group // mine, mine, rows, cols)
            for share in range(to.start, to.stop):
                for n, device in enumerate(lay.order):
                    if device % lay.half == share:
                        out.append(pltpu.make_async_copy(right_ref.at[share], r_hbm.at[n], out_sems.at[n]))
                        out[-1].start()
    for copy in out:
        copy.wait()


def left_kernel(lay, w_hbm, n_ref, mine_out, mate_out, w_ref, wt_ref, l_ref, left_ref, sems):
    rows, width, cols = l_ref.shape
    mine = width // lay.half
    group = BLOCK // rows
    weights = weight_copies(w_hbm, w_ref, 0, sems)
    for copy in weights:
        copy.start()
    for copy in weights:
        copy.wait()
    wt_ref[...] = w_ref[...].astype(F32).T.astype(BF16)
    swap = permutation(group, rows)

    def body(n, _):
        proj = dot(wt_ref[...], n_ref[n], 1, 0)
        left = (sigmoid(proj[width:]) * proj[:width]).astype(BF16)
        for m in range(2):
            l_ref[2 * n + m] = left[:, m * cols : (m + 1) * cols]
        return 0

    lax.fori_loop(0, rows // 2, body, 0, unroll=2)
    blocks = places(width, mine, rows)
    for k in range(0, len(blocks), 2):
        pair = blocks[k : k + 2]
        for (to, _here), left in zip(pair, swapped(swap, [l_ref[:, here] for _to, here in pair])):
            left_ref[to] = left.reshape(group // mine, mine, rows, cols)
    for n, s in enumerate(lay.hops):
        mine_out[n] = left_ref[lay.other(s)]
        mate_out[n] = left_ref[lay.other(s ^ lay.mate)]


def gate_kernel(*refs):
    sources, (h_ref, fac_hbm, fac_ref, wt_ref), targets, (sems, out_sems) = (
        refs[:7],
        refs[7:11],
        refs[11:18],
        refs[18:],
    )
    x_ref, cot_ref, gain_ref, bias_ref, w_ref, ogain_ref, ow_ref = targets
    rows, cols, width = x_ref.shape
    fetched(sources, targets, sems)
    wt_ref[...] = w_ref[:, : 4 * width].astype(F32).T.astype(BF16)
    ogain = column(ogain_ref[...], cols)

    def body(i, _):
        normed, _s = normalize(x_ref[i].astype(F32), -1)
        normal_in = (normed * gain_ref[...] + bias_ref[...]).astype(BF16)
        proj = dot(wt_ref[...], normal_in, 1, 1)
        for side in range(2):
            val = proj[2 * side * width : (2 * side + 1) * width]
            sig = sigmoid(proj[(2 * side + 1) * width : (2 * side + 2) * width])
            fac_ref[i, 2 * side * width : (2 * side + 1) * width] = sig.astype(BF16)
            fac_ref[i, (2 * side + 1) * width : (2 * side + 2) * width] = (
                val * sig * (1.0 - sig)
            ).astype(BF16)
        out_gate = sigmoid(dot(normal_in, w_ref[:, 4 * width :], 1, 0))
        grad_mixed = (cot_ref[i].astype(F32) * out_gate).astype(BF16)
        h_ref[i] = dot(ow_ref[...], grad_mixed, 1, 1) * ogain
        return 0

    size = rows // PARTS

    def send(p):
        here = pl.ds(p * size, size)
        return pltpu.make_async_copy(fac_ref.at[here], fac_hbm.at[here], out_sems.at[p])

    def part(p, _):
        for n in range(size):
            body(p * size + n, 0)
        send(p).start()
        return 0

    lax.fori_loop(0, PARTS, part, 0)
    for p in range(PARTS):
        send(p).wait()


def places(n_channels, mine, rows):
    group = BLOCK // rows
    return [
        (slice(c // mine, (c + group) // mine), slice(c, c + group)) for c in range(0, n_channels, group)
    ]


def to_rows(lay, t_ref, ts_ref):
    rows, width, cols = ts_ref.shape
    mine = t_ref.shape[1]
    group = BLOCK // rows
    swap = permutation(rows, group)
    blocks = places(width, mine, rows)
    for n in range(0, len(blocks), 2):
        pair = blocks[n : n + 2]
        for (_to, here), block in zip(pair, swapped(swap, [lay.shares(t_ref, to) for to, _here in pair])):
            ts_ref[:, here] = block.reshape(rows, group, cols)


def tri_back_kernel(lay, t_ref, h_ref, gt_ref, t_hbm, ts_ref, gs_ref, sem):
    rows, width, cols = h_ref.shape
    mine = t_ref.shape[1]
    group = BLOCK // rows
    copy = pltpu.make_async_copy(t_ref, t_hbm, sem)
    copy.start()
    back = permutation(group, rows)
    to_rows(lay, t_ref, ts_ref)

    def body(i, _):
        tri, h = ts_ref[i].astype(F32), h_ref[i]
        shifted = tri - jnp.mean(tri, axis=0, keepdims=True)
        first = jnp.mean(h, axis=0, keepdims=True)
        both = jnp.mean(h * shifted, axis=0, keepdims=True)
        tri_inv = lax.rsqrt(jnp.mean(shifted * shifted, axis=0, keepdims=True) + EPSILON)
        gs_ref[i] = (tri_inv * (h - first - shifted * (both * tri_inv * tri_inv))).astype(BF16)
        return 0

    lax.fori_loop(0, rows, body, 0, unroll=2 * UNROLL)
    blocks = places(width, mine, rows)
    for n in range(0, len(blocks), 2):
        pair = blocks[n : n + 2]
        for (to, _here), block in zip(pair, swapped(back, [gs_ref[:, here] for _to, here in pair])):
            block = block.reshape(group // mine, mine, rows, cols)
            for share in range(to.start, to.stop):
                gt_ref[lay.inside.index(share)] = block[share - to.start]
    copy.wait()


def logit_kernel(lay, *refs):
    (fac_hbm, *sources), refs = refs[:10], refs[10:]
    (gin0_ref, nt0_ref, fac0_ref, gin_hbm, nt_hbm, s_ref), refs = refs[:6], refs[6:]
    (ts_ref, gin_ref, nt_ref, out_sems), targets, sems = refs[:4], refs[4:13], refs[13]
    t_ref, x_ref, cot_ref, gain_ref, bias_ref, w_ref, ogain_ref, obias_ref, ow_ref = targets
    rows, cols, width = x_ref.shape
    first = pl.ds(0, nt0_ref.shape[0])
    fetched([*sources, fac_hbm.at[first]], [*targets, fac0_ref], sems)
    to_rows(lay, t_ref, ts_ref)
    ogain = column(ogain_ref[...], cols)
    obias = column(obias_ref[...], cols)

    def body(i, _):
        normed, scale_inv = normalize(x_ref[i].astype(F32), -1)
        normal_in = (normed * gain_ref[...] + bias_ref[...]).astype(BF16)
        out_gate = sigmoid(dot(normal_in, w_ref[:, 4 * width :], 1, 0))
        tri_hat, _s = normalize(ts_ref[i].astype(F32), 0)
        normal_out = (tri_hat * ogain + obias).astype(BF16)
        mixed = dot(normal_out, ow_ref[...], 0, 0)
        grad_logit = cot_ref[i].astype(F32) * mixed * out_gate * (1.0 - out_gate)
        gin_ref[i] = dot(w_ref[:, 4 * width :], grad_logit.astype(BF16), 1, 1).astype(BF16)
        nt_ref[i] = normed.T.astype(BF16)
        s_ref[pl.ds(i, 1), :] = jnp.broadcast_to(scale_inv, (cols, width)).T[:1]
        return 0

    lax.fori_loop(0, rows, body, 0, unroll=UNROLL)
    gin0_ref[...] = gin_ref[first]
    nt0_ref[...] = nt_ref[first]
    copies = [
        pltpu.make_async_copy(gin_ref, gin_hbm, out_sems.at[0]),
        pltpu.make_async_copy(nt_ref, nt_hbm, out_sems.at[1]),
    ]
    for copy in copies:
        copy.start()
    for copy in copies:
        copy.wait()


def pair_kernel(
    lay, fac_hbm, nt_hbm, gin_hbm, fac0_ref, nt0_ref, gin0_ref, r_ref, s_ref, gain_ref, w_ref, *refs
):
    l_refs, refs = refs[: lay.n_hops], refs[lay.n_hops :]
    out_hbm, l_ref, ls_ref, rs_ref, fac_ref, nt_ref, gin_ref, out_ref, sems, out_sems = refs
    rows, cols, width = out_ref.shape
    mine = width // lay.half
    parts = sems.shape[1]
    size = rows // parts

    def fetch(p):
        here = pl.ds(p * size, size)
        return [
            pltpu.make_async_copy(fac_hbm.at[here], fac_ref.at[here], sems.at[0, p]),
            pltpu.make_async_copy(nt_hbm.at[here], nt_ref.at[here], sems.at[1, p]),
            pltpu.make_async_copy(gin_hbm.at[here], gin_ref.at[here], sems.at[2, p]),
        ]

    def send(n):
        here = pl.ds(2 * n, 2)
        return pltpu.make_async_copy(out_ref.at[here], out_hbm.at[here], out_sems.at[n])

    for p in range(1, parts):
        for copy in fetch(p):
            copy.start()
    gain = column(gain_ref[...], cols)
    eye = identity(cols)
    group = BLOCK // rows
    swap = permutation(rows, group)
    for s, source in lay.received(l_refs):
        l_ref[lay.other(s)] = source[...]
    for to, here in places(width, mine, rows):
        sums = []
        for share in range(to.start, to.stop):
            one, two = (
                r_ref[n].astype(F32)
                for n, device in enumerate(lay.order)
                if device % lay.half == share
            )
            sums.append((one + two).astype(BF16))
        left, right = swapped(swap, [l_ref[to], jnp.stack(sums)])
        ls_ref[:, here] = left.reshape(rows, group, cols)
        rs_ref[:, here] = right.reshape(rows, group, cols)

    def part(p, fac_here, nt_here, gin_here):
        for n in range(0, size, 2):
            i = p * size + n
            blocks = []
            for m in range(2):
                left, right, fac = ls_ref[i + m], rs_ref[i + m], fac_here[i + m]
                blocks.append(
                    jnp.concatenate(
                        [
                            left * fac[:width],
                            left * fac[width : 2 * width],
                            right * fac[2 * width : 3 * width],
                            right * fac[3 * width :],
                        ],
                        axis=0,
                    )
                )
            grad_in = dot(w_ref[:, : 4 * width], jnp.concatenate(blocks, axis=1), 1, 0)
            for m in range(2):
                grad = (grad_in[:, m * cols : (m + 1) * cols] + gin_here[i + m].astype(F32)) * gain
                scale_inv = s_ref[pl.ds(i + m, 1), :]
                normed = nt_here[i + m].astype(F32)
                result = norm_back(grad, normed, scale_inv, 0).astype(BF16)
                out_ref[i + m] = dot(eye, result, 1, 1).astype(BF16)
            send(i // 2).start()

    part(0, fac0_ref, nt0_ref, gin0_ref)
    for p in range(1, parts):
        for copy in fetch(p):
            copy.wait()
    for p in range(1, parts):
        part(p, fac_ref, nt_ref, gin_ref)
    for n in range(rows // 2):
        send(n).wait()


class Layout:
    def __init__(self, n_row, n_ch):
        self.n_row, self.n_ch = n_row, n_ch
        self.devices = n_row * n_ch
        self.half = self.devices // 2
        outer = math.isqrt(n_row)
        self.inner = self.devices // outer
        near = [
            2 * n_ch * far + n_ch * core + b
            for far in range(self.inner // (2 * n_ch))
            for b in range(n_ch)
            for core in range(2)
        ]
        self.order = [o * self.inner + n for n in near for o in range(outer)]
        self.inside = [o * self.inner + n for n in near for o in range(outer // 2)]
        self.mate = n_ch
        self.hops = [s for s in range(self.half) if s & self.mate == 0]
        self.hops[3:] = self.hops[:2:-1]
        self.n_hops = len(self.hops) + 1
        self.all_place = self.place(self.order, n_row)
        self.half_place = self.place(self.inside, n_row // 2)
        self.near_place = self.place(list(range(self.half)), n_row // 2)

    def place(self, order, n_row):
        return [[order.index(r * self.n_ch + b) for b in range(self.n_ch)] for r in range(n_row)]

    def shares(self, ref, here):
        return jnp.stack([ref[self.inside.index(share)] for share in range(here.start, here.stop)])

    def other(self, s):
        me = lax.axis_index("row") * self.n_ch + lax.axis_index("ch")
        return jnp.bitwise_xor(lax.rem(me, self.half), s)

    def exchange_all(self, blocks):
        return lax.all_to_all(
            blocks, ("row", "ch"), split_axis=0, concat_axis=0, tiled=True, axis_index_groups=[self.order]
        )

    def exchange_half(self, blocks):
        groups = [[first + n for n in self.inside] for first in (0, self.half)]
        return lax.all_to_all(
            blocks, ("row", "ch"), split_axis=0, concat_axis=0, tiled=True, axis_index_groups=groups
        )

    def swap(self, block, s):
        return lax.ppermute(block, ("row", "ch"), [(n, n ^ s) for n in range(self.devices)])

    def permute(self, mine, mates):
        mates = self.swap(mates, self.mate)
        shape = jax.ShapeDtypeStruct((2,) + mine.shape[1:], mine.dtype)
        pairs = call(merge_kernel, [shape] * (len(self.hops) - 1), [], mine, mates)
        return [mine, mates] + [self.swap(pair, s) for pair, s in zip(pairs, self.hops[1:])]

    def received(self, refs):
        mine, mates, *pairs = refs
        found = [(0, mine.at[0]), (self.mate, mates.at[0])]
        for s, pair in zip(self.hops[1:], pairs):
            found += [(s, pair.at[0]), (s ^ self.mate, pair.at[1])]
        return found


def merge_kernel(mine_ref, mates_ref, *outs):
    for n, out_ref in enumerate(outs, 1):
        out_ref[0] = mine_ref[n]
        out_ref[1] = mates_ref[n]


def plane(ref, place, c):
    return jnp.concatenate(
        [
            jnp.concatenate([ref[n, c] for n in column_of], axis=0)
            for column_of in zip(*place)
        ],
        axis=1,
    )


def store_plane(ref, place, c, value):
    rows, cols = ref.shape[-2:]
    for r, row_of in enumerate(place):
        for b, n in enumerate(row_of):
            ref[n, c] = value[r * rows : (r + 1) * rows, b * cols : (b + 1) * cols]


def tri_kernel(lay, r_ref, *refs):
    l_refs, (t_ref, l_ref) = refs[: lay.n_hops], refs[lay.n_hops :]
    for s, source in lay.received(l_refs):
        l_ref[lay.other(s)] = source[...]
    for c in range(t_ref.shape[1]):
        tri = dot(plane(l_ref, lay.near_place, c), plane(r_ref, lay.all_place, c), 1, 1)
        store_plane(t_ref, lay.half_place, c, tri.astype(BF16))


def factor_back_kernel(lay, gt_ref, l_ref, r_ref, gr_hbm, *refs):
    mine_out, mate_out, gl_ref, gr_ref, sems = refs
    copies = []
    for c in range(gt_ref.shape[1]):
        right = dot(plane(gt_ref, lay.half_place, c), plane(l_ref, lay.near_place, c), 0, 0)
        store_plane(gr_ref, lay.all_place, c, right.astype(BF16))
        here = (slice(None), c)
        copies.append(pltpu.make_async_copy(gr_ref.at[here], gr_hbm.at[here], sems.at[c]))
        copies[-1].start()
    for c in range(gt_ref.shape[1]):
        left = dot(plane(gt_ref, lay.half_place, c), plane(r_ref, lay.all_place, c), 1, 0)
        store_plane(gl_ref, lay.near_place, c, left.astype(BF16))
    for n, s in enumerate(lay.hops):
        mine_out[n] = gl_ref[lay.other(s)]
        mate_out[n] = gl_ref[lay.other(s ^ lay.mate)]
    for copy in copies:
        copy.wait()


def by_channel(
    n_row, n_ch, pair_act, cotangent, in_gain, in_bias, proj_weight, out_gain, out_bias, out_weight
):
    lay = Layout(n_row, n_ch)
    rows, cols, width = pair_act.shape
    mine = width // lay.half
    struct = jax.ShapeDtypeStruct
    half = pltpu.VMEM((rows, width, cols), BF16)
    weight_t = pltpu.VMEM((4 * width, width), BF16)
    in_gain, in_bias, out_gain, out_bias = (
        v.reshape(1, width) for v in (in_gain, in_bias, out_gain, out_bias)
    )

    some = struct((len(lay.hops), mine, rows, cols), BF16)
    one = struct((lay.half, mine, rows, cols), BF16)
    one_here = pltpu.VMEM(one.shape, BF16)
    two_shape = (lay.devices, mine, rows, cols)
    row = pltpu.VMEM((1, width), F32)
    weight = pltpu.VMEM(proj_weight.shape, BF16)
    out_weight_here = pltpu.VMEM((width, width), BF16)
    both_weights = pltpu.VMEM((width, 2 * width), BF16)
    both_turned = pltpu.VMEM((2 * width, width), BF16)
    right, normal_in = call(
        functools.partial(right_kernel, lay),
        [pltpu.HBM(two_shape, BF16), struct((rows // 2, width, 2 * cols), BF16)],
        [
            half,
            row,
            row,
            both_weights,
            both_turned,
            half,
            one_here,
            pltpu.SemaphoreType.DMA((4 + PARTS // 2,)),
            pltpu.SemaphoreType.DMA((lay.devices,)),
        ],
        pair_act,
        in_gain,
        in_bias,
        proj_weight,
        hbm=4,
    )
    left = call(
        functools.partial(left_kernel, lay),
        [some, some],
        [both_weights, both_turned, half, one_here, pltpu.SemaphoreType.DMA((2,))],
        proj_weight,
        normal_in,
        hbm=1,
    )
    right = lay.exchange_all(right)
    left = lay.permute(*left)
    h, fac = call(
        gate_kernel,
        [pltpu.VMEM((rows, width, cols), F32), pltpu.HBM((rows, 4 * width, cols), BF16)],
        [
            pltpu.VMEM((rows, 4 * width, cols), BF16),
            weight_t,
            half,
            half,
            row,
            row,
            weight,
            row,
            out_weight_here,
            pltpu.SemaphoreType.DMA((7,)),
            pltpu.SemaphoreType.DMA((PARTS,)),
        ],
        pair_act,
        cotangent,
        in_gain,
        in_bias,
        proj_weight,
        out_gain,
        out_weight,
        hbm=7,
    )
    right, h, fac = lax.optimization_barrier((right, h, fac))
    tri, left = call(functools.partial(tri_kernel, lay), [one, one], [], right, *left)
    tri = lay.exchange_half(tri)
    grad_tri, tri = call(
        functools.partial(tri_back_kernel, lay),
        [one, pltpu.HBM(one.shape, BF16)],
        [half, half, pltpu.SemaphoreType.DMA(())],
        tri,
        h,
    )
    grad_right, *grad_left = call(
        functools.partial(factor_back_kernel, lay),
        [pltpu.HBM(two_shape, BF16), some, some],
        [one_here, pltpu.VMEM(two_shape, BF16), pltpu.SemaphoreType.DMA((mine,))],
        lay.exchange_half(grad_tri),
        left,
        right,
    )
    grad_right = lay.exchange_all(grad_right)
    grad_left = lay.permute(*grad_left)
    grad_in_first, normed_first, fac_first, grad_in, normed_t, scale = call(
        functools.partial(logit_kernel, lay),
        [
            pltpu.VMEM((rows // PARTS, width, cols), BF16),
            pltpu.VMEM((rows // PARTS, width, cols), BF16),
            pltpu.VMEM((rows // PARTS, 4 * width, cols), BF16),
            pltpu.HBM((rows, width, cols), BF16),
            pltpu.HBM((rows, width, cols), BF16),
            pltpu.VMEM((rows, cols), F32),
        ],
        [
            half,
            half,
            half,
            pltpu.SemaphoreType.DMA((2,)),
            one_here,
            half,
            half,
            row,
            row,
            weight,
            row,
            row,
            out_weight_here,
            pltpu.SemaphoreType.DMA((10,)),
        ],
        fac,
        tri,
        pair_act,
        cotangent,
        in_gain,
        in_bias,
        proj_weight,
        out_gain,
        out_bias,
        out_weight,
        hbm=10,
    )
    return call(
        functools.partial(pair_kernel, lay),
        pltpu.HBM((rows, cols, width), BF16),
        [
            one_here,
            half,
            half,
            pltpu.VMEM((rows, 4 * width, cols), BF16),
            half,
            half,
            half,
            pltpu.SemaphoreType.DMA((3, PARTS)),
            pltpu.SemaphoreType.DMA((rows // 2,)),
        ],
        fac,
        normed_t,
        grad_in,
        fac_first,
        normed_first,
        grad_in_first,
        grad_right,
        scale,
        in_gain,
        proj_weight,
        *grad_left,
        hbm=3,
    )


def by_row(
    pair_act, cotangent, in_gain, in_bias, proj_weight, out_gain, out_bias, out_weight
):
    rows_here, cols_here, width = pair_act.shape
    flat = pair_act.astype(jnp.float32).reshape(rows_here * cols_here, width)
    normed, scale_inv = normalize(flat, -1)
    normal_in = (normed * in_gain + in_bias).astype(jnp.bfloat16)
    projected = jnp.einsum("pd,de->ep", normal_in, proj_weight, preferred_element_type=jnp.float32)
    blocks = jnp.split(projected, 5, axis=0)
    left_sig = jax.nn.sigmoid(blocks[1])
    right_sig = jax.nn.sigmoid(blocks[3])
    left_fac = (left_sig * blocks[0]).astype(jnp.bfloat16).reshape(width, rows_here, cols_here)
    right_fac = (right_sig * blocks[2]).astype(jnp.bfloat16).reshape(width, rows_here, cols_here)
    left_chan, right_chan = (
        lax.all_to_all(left_fac, "ch", split_axis=0, concat_axis=2, tiled=True),
        lax.all_to_all(right_fac, "ch", split_axis=0, concat_axis=2, tiled=True),
    )
    tri_chan = jnp.einsum(
        "cik,cjk->cij",
        left_chan,
        lax.all_gather(right_chan, "row", axis=1, tiled=True),
        preferred_element_type=jnp.float32,
    ).astype(jnp.bfloat16)
    tri_back = lax.all_to_all(tri_chan, "ch", split_axis=2, concat_axis=0, tiled=True)
    tri_hat, tri_inv = normalize(tri_back.astype(jnp.float32).reshape(width, -1), 0)
    normal_out = (tri_hat * out_gain[:, None] + out_bias[:, None]).astype(jnp.bfloat16)
    mixed = jnp.einsum("cp,ce->ep", normal_out, out_weight, preferred_element_type=jnp.float32)
    out_gate = jax.nn.sigmoid(blocks[4])
    grad_out = cotangent.astype(jnp.float32).reshape(rows_here * cols_here, width).T
    grad_mixed = (grad_out * out_gate).astype(jnp.bfloat16)
    grad_logit = grad_out * mixed * out_gate * (1.0 - out_gate)
    grad_normal = jnp.einsum(
        "ep,ce->cp", grad_mixed, out_weight, preferred_element_type=jnp.float32
    )
    grad_tri = norm_back(grad_normal * out_gain[:, None], tri_hat, tri_inv, 0)
    grad_tri = grad_tri.astype(jnp.bfloat16).reshape(width, rows_here, cols_here)
    grad_chan = lax.all_to_all(grad_tri, "ch", split_axis=0, concat_axis=2, tiled=True)
    grad_cols = lax.all_to_all(grad_chan, "row", split_axis=2, concat_axis=1, tiled=True)
    grad_left = jnp.einsum(
        "cij,cjk->cik",
        grad_chan,
        lax.all_gather(right_chan, "row", axis=1, tiled=True),
        preferred_element_type=jnp.float32,
    )
    grad_right = jnp.einsum(
        "cij,cik->cjk",
        grad_cols,
        lax.all_gather(left_chan, "row", axis=1, tiled=True),
        preferred_element_type=jnp.float32,
    )
    left_back, right_back = (
        lax.all_to_all(
            grad_left.astype(jnp.bfloat16), "ch", split_axis=2, concat_axis=0, tiled=True
        ),
        lax.all_to_all(
            grad_right.astype(jnp.bfloat16), "ch", split_axis=2, concat_axis=0, tiled=True
        ),
    )
    left_grad = left_back.astype(jnp.float32).reshape(width, -1)
    right_grad = right_back.astype(jnp.float32).reshape(width, -1)
    grad_proj = jnp.concatenate(
        [
            left_grad * left_sig,
            left_grad * blocks[0] * left_sig * (1.0 - left_sig),
            right_grad * right_sig,
            right_grad * blocks[2] * right_sig * (1.0 - right_sig),
            grad_logit,
        ],
        axis=0,
    ).astype(jnp.bfloat16)
    grad_in = jnp.einsum("ep,de->pd", grad_proj, proj_weight, preferred_element_type=jnp.float32)
    grad_pair = norm_back(grad_in * in_gain, normed, scale_inv, -1)
    return grad_pair.astype(jnp.bfloat16).reshape(rows_here, cols_here, width)


def solution(mesh):
    n_row, n_ch = mesh.shape["row"], mesh.shape["ch"]
    placed = (P("row", "ch", None), P("row", "ch", None), P(), P(), P(), P(), P(), P())

    def on_device(*args):
        rows, cols, width = args[0].shape
        devices, outer, group = n_row * n_ch, math.isqrt(n_row), BLOCK // rows
        if (
            devices & (devices - 1) == 0
            and n_row >= 4
            and n_row % outer == 0
            and (devices // outer) % (2 * n_ch) == 0
            and outer % 2 == 0
            and width % (devices // 2) == 0
            and rows % (2 * PARTS) == 0
            and BLOCK % rows == 0
            and group % (width // (devices // 2)) == 0
            and width % (2 * group) == 0
            and cols % 128 == 0
            and width <= 256
            and width & (width - 1) == 0
        ):
            return by_channel(n_row, n_ch, *args)
        return by_row(*args)

    return jax.shard_map(
        on_device, mesh=mesh, in_specs=placed, out_specs=P("row", "ch", None), check_vma=False
    )
```

```python
import functools
import math

import jax
import jax.numpy as jnp
from jax import lax
from jax.experimental import pallas as pl
from jax.experimental.pallas import tpu as pltpu
from jax.sharding import PartitionSpec as P

EPSILON = 1e-05
F32 = jnp.float32
BF16 = jnp.bfloat16
UNROLL = 4
BLOCK = 256
PARTS = 4


def dot(a, b, da, db):
    return lax.dot_general(a, b, (((da,), (db,)), ((), ())), preferred_element_type=F32)


def sigmoid(values):
    return 0.5 * jnp.tanh(0.5 * values) + 0.5


def normalize(values, axis):
    center = jnp.mean(values, axis=axis, keepdims=True)
    shifted = values - center
    scale_inv = lax.rsqrt(jnp.mean(shifted * shifted, axis=axis, keepdims=True) + EPSILON)
    return (shifted * scale_inv, scale_inv)


def norm_back(grad_hat, normed, scale_inv, axis):
    first = jnp.mean(grad_hat, axis=axis, keepdims=True)
    second = jnp.mean(grad_hat * normed, axis=axis, keepdims=True)
    return scale_inv * (grad_hat - first - normed * second)


def column(row, width):
    return jnp.broadcast_to(row, (width, row.shape[-1])).T


def call(kernel, outs, scratch, *args, hbm=0, limit=16):
    single = not isinstance(outs, (list, tuple))
    args = [pltpu.with_memory_space_constraint(a, pltpu.HBM) if n < hbm else a for n, a in enumerate(args)]
    specs = [pl.BlockSpec(memory_space=pltpu.HBM if n < hbm else pltpu.VMEM) for n in range(len(args))]
    out_specs = [
        pl.BlockSpec(memory_space=getattr(out, "memory_space", pltpu.VMEM))
        for out in ([outs] if single else outs)
    ]
    return pl.pallas_call(
        kernel,
        out_shape=outs if single else tuple(outs),
        in_specs=specs,
        out_specs=out_specs[0] if single else tuple(out_specs),
        scratch_shapes=scratch,
        compiler_params=pltpu.CompilerParams(vmem_limit_bytes=limit * 1024 * 1024),
    )(*args)


def permutation(outer, inner):
    to = lax.broadcasted_iota(jnp.int32, (BLOCK, BLOCK), 0)
    start = lax.broadcasted_iota(jnp.int32, (BLOCK, BLOCK), 1)
    return (start == to % inner * outer + to // inner).astype(F32).astype(BF16)


def identity(size):
    first = lax.broadcasted_iota(jnp.int32, (size, size), 0)
    return (first == lax.broadcasted_iota(jnp.int32, (size, size), 1)).astype(F32).astype(BF16)


def swapped(swap, blocks):
    cols = blocks[0].shape[-1]
    wide = jnp.concatenate([block.reshape(BLOCK, cols) for block in blocks], axis=1)
    wide = dot(swap, wide, 1, 0).astype(BF16)
    return [wide[:, n * cols : (n + 1) * cols] for n in range(len(blocks))]


def fetched(sources, targets, sems):
    copies = [
        pltpu.make_async_copy(source, target, sems.at[n])
        for n, (source, target) in enumerate(zip(sources, targets))
    ]
    for copy in copies:
        copy.start()
    for copy in copies:
        copy.wait()


def weight_copies(w_hbm, w_ref, first, sems):
    width = w_hbm.shape[0]
    return [
        pltpu.make_async_copy(
            w_hbm.at[:, (first + n) * width : (first + n + 1) * width],
            w_ref.at[:, n * width : (n + 1) * width],
            sems.at[n],
        )
        for n in range(2)
    ]


def right_kernel(
    lay, x_hbm, gain_hbm, bias_hbm, w_hbm, r_hbm, n_ref, x_ref, gain_ref, bias_ref, w_ref, wt_ref, r_ref, right_ref, sems, out_sems
):
    rows, cols, width = x_ref.shape
    mine = width // lay.half
    parts = sems.shape[0] - 4
    size = rows // parts

    def fetch(p):
        here = pl.ds(p * size, size)
        return pltpu.make_async_copy(x_hbm.at[here], x_ref.at[here], sems.at[4 + p])

    small = [
        pltpu.make_async_copy(gain_hbm, gain_ref, sems.at[2]),
        pltpu.make_async_copy(bias_hbm, bias_ref, sems.at[3]),
    ]
    weights = weight_copies(w_hbm, w_ref, 2, sems)
    fetch(0).start()
    for copy in small + weights:
        copy.start()
    for p in range(1, parts):
        fetch(p).start()
    group = BLOCK // rows
    swap = permutation(group, rows)

    def normal(p):
        fetch(p).wait()
        for n in range(0, size, 2):
            i = p * size + n
            shifted = dot(center, x_ref[pl.ds(i, 2)].reshape(2 * cols, width), 1, 1)
            scale_inv = lax.rsqrt(jnp.mean(shifted * shifted, axis=0, keepdims=True) + EPSILON)
            n_ref[p * size // 2 + n // 2] = (shifted * scale_inv * gain + bias).astype(BF16)

    def project(p):
        for n in range(0, size, 2):
            i = p * size + n
            proj = dot(wt_ref[...], n_ref[p * size // 2 + n // 2], 1, 0)
            right = (sigmoid(proj[width:]) * proj[:width]).astype(BF16)
            for m in range(2):
                r_ref[i + m] = right[:, m * cols : (m + 1) * cols]

    def body(p, _):
        normal(p)
        project(p - 1)
        return 0

    center = (identity(width).astype(F32) - 1.0 / width).astype(BF16)
    for copy in small:
        copy.wait()
    gain = column(gain_ref[...], 2 * cols)
    bias = column(bias_ref[...], 2 * cols)
    normal(0)
    for copy in weights:
        copy.wait()
    wt_ref[...] = w_ref[...].astype(F32).T.astype(BF16)
    lax.fori_loop(1, parts, body, 0)
    project(parts - 1)
    out = []
    blocks = places(width, mine, rows)
    for k in range(0, len(blocks), 2):
        pair = blocks[k : k + 2]
        for (to, _here), right in zip(pair, swapped(swap, [r_ref[:, here] for _to, here in pair])):
            right_ref[to] = right.reshape(group // mine, mine, rows, cols)
            for share in range(to.start, to.stop):
                for n, device in enumerate(lay.order):
                    if device % lay.half == share:
                        out.append(pltpu.make_async_copy(right_ref.at[share], r_hbm.at[n], out_sems.at[n]))
                        out[-1].start()
    for copy in out:
        copy.wait()


def left_kernel(lay, w_hbm, n_ref, mine_out, mate_out, w_ref, wt_ref, l_ref, left_ref, sems):
    rows, width, cols = l_ref.shape
    mine = width // lay.half
    group = BLOCK // rows
    weights = weight_copies(w_hbm, w_ref, 0, sems)
    for copy in weights:
        copy.start()
    for copy in weights:
        copy.wait()
    wt_ref[...] = w_ref[...].astype(F32).T.astype(BF16)
    swap = permutation(group, rows)

    def body(n, _):
        proj = dot(wt_ref[...], n_ref[n], 1, 0)
        left = (sigmoid(proj[width:]) * proj[:width]).astype(BF16)
        for m in range(2):
            l_ref[2 * n + m] = left[:, m * cols : (m + 1) * cols]
        return 0

    lax.fori_loop(0, rows // 2, body, 0, unroll=2)
    blocks = places(width, mine, rows)
    for k in range(0, len(blocks), 2):
        pair = blocks[k : k + 2]
        for (to, _here), left in zip(pair, swapped(swap, [l_ref[:, here] for _to, here in pair])):
            left_ref[to] = left.reshape(group // mine, mine, rows, cols)
    for n, s in enumerate(lay.hops):
        mine_out[n] = left_ref[lay.other(s)]
        mate_out[n] = left_ref[lay.other(s ^ lay.mate)]


def gate_kernel(*refs):
    sources, (h_ref, fac_hbm, fac_ref, wt_ref), targets, (sems, out_sems) = (
        refs[:7],
        refs[7:11],
        refs[11:18],
        refs[18:],
    )
    x_ref, cot_ref, gain_ref, bias_ref, w_ref, ogain_ref, ow_ref = targets
    rows, cols, width = x_ref.shape
    fetched(sources, targets, sems)
    wt_ref[...] = w_ref[:, : 4 * width].astype(F32).T.astype(BF16)
    ogain = column(ogain_ref[...], cols)

    def body(i, _):
        normed, _s = normalize(x_ref[i].astype(F32), -1)
        normal_in = (normed * gain_ref[...] + bias_ref[...]).astype(BF16)
        proj = dot(wt_ref[...], normal_in, 1, 1)
        for side in range(2):
            val = proj[2 * side * width : (2 * side + 1) * width]
            sig = sigmoid(proj[(2 * side + 1) * width : (2 * side + 2) * width])
            fac_ref[i, 2 * side * width : (2 * side + 1) * width] = sig.astype(BF16)
            fac_ref[i, (2 * side + 1) * width : (2 * side + 2) * width] = (
                val * sig * (1.0 - sig)
            ).astype(BF16)
        out_gate = sigmoid(dot(normal_in, w_ref[:, 4 * width :], 1, 0))
        grad_mixed = (cot_ref[i].astype(F32) * out_gate).astype(BF16)
        h_ref[i] = dot(ow_ref[...], grad_mixed, 1, 1) * ogain
        return 0

    size = rows // PARTS

    def send(p):
        here = pl.ds(p * size, size)
        return pltpu.make_async_copy(fac_ref.at[here], fac_hbm.at[here], out_sems.at[p])

    def part(p, _):
        for n in range(size):
            body(p * size + n, 0)
        send(p).start()
        return 0

    lax.fori_loop(0, PARTS, part, 0)
    for p in range(PARTS):
        send(p).wait()


def places(n_channels, mine, rows):
    group = BLOCK // rows
    return [
        (slice(c // mine, (c + group) // mine), slice(c, c + group)) for c in range(0, n_channels, group)
    ]


def to_rows(lay, t_ref, ts_ref):
    rows, width, cols = ts_ref.shape
    mine = t_ref.shape[1]
    group = BLOCK // rows
    swap = permutation(rows, group)
    blocks = places(width, mine, rows)
    for n in range(0, len(blocks), 2):
        pair = blocks[n : n + 2]
        for (_to, here), block in zip(pair, swapped(swap, [lay.shares(t_ref, to) for to, _here in pair])):
            ts_ref[:, here] = block.reshape(rows, group, cols)


def tri_back_kernel(lay, t_ref, h_ref, gt_ref, t_hbm, ts_ref, gs_ref, sem):
    rows, width, cols = h_ref.shape
    mine = t_ref.shape[1]
    group = BLOCK // rows
    copy = pltpu.make_async_copy(t_ref, t_hbm, sem)
    copy.start()
    back = permutation(group, rows)
    to_rows(lay, t_ref, ts_ref)

    def body(i, _):
        tri, h = ts_ref[i].astype(F32), h_ref[i]
        shifted = tri - jnp.mean(tri, axis=0, keepdims=True)
        first = jnp.mean(h, axis=0, keepdims=True)
        both = jnp.mean(h * shifted, axis=0, keepdims=True)
        tri_inv = lax.rsqrt(jnp.mean(shifted * shifted, axis=0, keepdims=True) + EPSILON)
        gs_ref[i] = (tri_inv * (h - first - shifted * (both * tri_inv * tri_inv))).astype(BF16)
        return 0

    lax.fori_loop(0, rows, body, 0, unroll=2 * UNROLL)
    blocks = places(width, mine, rows)
    for n in range(0, len(blocks), 2):
        pair = blocks[n : n + 2]
        for (to, _here), block in zip(pair, swapped(back, [gs_ref[:, here] for _to, here in pair])):
            block = block.reshape(group // mine, mine, rows, cols)
            for share in range(to.start, to.stop):
                gt_ref[lay.inside.index(share)] = block[share - to.start]
    copy.wait()


def logit_kernel(lay, *refs):
    (fac_hbm, *sources), refs = refs[:10], refs[10:]
    (gin0_ref, nt0_ref, fac0_ref, gin_hbm, nt_hbm, s_ref), refs = refs[:6], refs[6:]
    (ts_ref, gin_ref, nt_ref, out_sems), targets, sems = refs[:4], refs[4:13], refs[13]
    t_ref, x_ref, cot_ref, gain_ref, bias_ref, w_ref, ogain_ref, obias_ref, ow_ref = targets
    rows, cols, width = x_ref.shape
    first = pl.ds(0, nt0_ref.shape[0])
    fetched([*sources, fac_hbm.at[first]], [*targets, fac0_ref], sems)
    to_rows(lay, t_ref, ts_ref)
    ogain = column(ogain_ref[...], cols)
    obias = column(obias_ref[...], cols)

    def body(i, _):
        normed, scale_inv = normalize(x_ref[i].astype(F32), -1)
        normal_in = (normed * gain_ref[...] + bias_ref[...]).astype(BF16)
        out_gate = sigmoid(dot(normal_in, w_ref[:, 4 * width :], 1, 0))
        tri_hat, _s = normalize(ts_ref[i].astype(F32), 0)
        normal_out = (tri_hat * ogain + obias).astype(BF16)
        mixed = dot(normal_out, ow_ref[...], 0, 0)
        grad_logit = cot_ref[i].astype(F32) * mixed * out_gate * (1.0 - out_gate)
        gin_ref[i] = dot(w_ref[:, 4 * width :], grad_logit.astype(BF16), 1, 1).astype(BF16)
        nt_ref[i] = normed.T.astype(BF16)
        s_ref[pl.ds(i, 1), :] = jnp.broadcast_to(scale_inv, (cols, width)).T[:1]
        return 0

    lax.fori_loop(0, rows, body, 0, unroll=UNROLL)
    gin0_ref[...] = gin_ref[first]
    nt0_ref[...] = nt_ref[first]
    copies = [
        pltpu.make_async_copy(gin_ref, gin_hbm, out_sems.at[0]),
        pltpu.make_async_copy(nt_ref, nt_hbm, out_sems.at[1]),
    ]
    for copy in copies:
        copy.start()
    for copy in copies:
        copy.wait()


def pair_kernel(
    lay, fac_hbm, nt_hbm, gin_hbm, fac0_ref, nt0_ref, gin0_ref, r_ref, s_ref, gain_ref, w_ref, *refs
):
    l_refs, refs = refs[: lay.n_hops], refs[lay.n_hops :]
    out_hbm, l_ref, ls_ref, rs_ref, fac_ref, nt_ref, gin_ref, out_ref, sems, out_sems = refs
    rows, cols, width = out_ref.shape
    mine = width // lay.half
    parts = sems.shape[1]
    size = rows // parts

    def fetch(p):
        here = pl.ds(p * size, size)
        return [
            pltpu.make_async_copy(fac_hbm.at[here], fac_ref.at[here], sems.at[0, p]),
            pltpu.make_async_copy(nt_hbm.at[here], nt_ref.at[here], sems.at[1, p]),
            pltpu.make_async_copy(gin_hbm.at[here], gin_ref.at[here], sems.at[2, p]),
        ]

    def send(n):
        here = pl.ds(2 * n, 2)
        return pltpu.make_async_copy(out_ref.at[here], out_hbm.at[here], out_sems.at[n])

    for p in range(1, parts):
        for copy in fetch(p):
            copy.start()
    gain = column(gain_ref[...], cols)
    eye = identity(cols)
    group = BLOCK // rows
    swap = permutation(rows, group)
    for s, source in lay.received(l_refs):
        l_ref[lay.other(s)] = source[...]
    for to, here in places(width, mine, rows):
        sums = []
        for share in range(to.start, to.stop):
            one, two = (
                r_ref[n]
                for n, device in enumerate(lay.order)
                if device % lay.half == share
            )
            sums.append(one + two)
        left, right = swapped(swap, [l_ref[to], jnp.stack(sums)])
        ls_ref[:, here] = left.reshape(rows, group, cols)
        rs_ref[:, here] = right.reshape(rows, group, cols)

    def part(p, fac_here, nt_here, gin_here):
        for n in range(0, size, 2):
            i = p * size + n
            blocks = []
            for m in range(2):
                left, right, fac = ls_ref[i + m], rs_ref[i + m], fac_here[i + m]
                blocks.append(
                    jnp.concatenate(
                        [
                            left * fac[:width],
                            left * fac[width : 2 * width],
                            right * fac[2 * width : 3 * width],
                            right * fac[3 * width :],
                        ],
                        axis=0,
                    )
                )
            grad_in = dot(w_ref[:, : 4 * width], jnp.concatenate(blocks, axis=1), 1, 0)
            for m in range(2):
                grad = (grad_in[:, m * cols : (m + 1) * cols] + gin_here[i + m].astype(F32)) * gain
                scale_inv = s_ref[pl.ds(i + m, 1), :]
                normed = nt_here[i + m].astype(F32)
                result = norm_back(grad, normed, scale_inv, 0).astype(BF16)
                out_ref[i + m] = dot(eye, result, 1, 1).astype(BF16)
            send(i // 2).start()

    part(0, fac0_ref, nt0_ref, gin0_ref)
    for p in range(1, parts):
        for copy in fetch(p):
            copy.wait()
    for p in range(1, parts):
        part(p, fac_ref, nt_ref, gin_ref)
    for n in range(rows // 2):
        send(n).wait()


class Layout:
    def __init__(self, n_row, n_ch):
        self.n_row, self.n_ch = n_row, n_ch
        self.devices = n_row * n_ch
        self.half = self.devices // 2
        outer = math.isqrt(n_row)
        self.inner = self.devices // outer
        near = [
            2 * n_ch * far + n_ch * core + b
            for b in range(n_ch)
            for far in range(self.inner // (2 * n_ch))
            for core in range(2)
        ]
        self.order = [o * self.inner + n for n in near for o in range(outer)]
        self.inside = [o * self.inner + n for n in near for o in range(outer // 2)]
        self.mate = n_ch
        self.hops = [s for s in range(self.half) if s & self.mate == 0]
        self.hops[3:] = self.hops[:2:-1]
        self.n_hops = len(self.hops) + 1
        self.all_place = self.place(self.order, n_row)
        self.half_place = self.place(self.inside, n_row // 2)
        self.near_place = self.place(list(range(self.half)), n_row // 2)

    def place(self, order, n_row):
        return [[order.index(r * self.n_ch + b) for b in range(self.n_ch)] for r in range(n_row)]

    def shares(self, ref, here):
        return jnp.stack([ref[self.inside.index(share)] for share in range(here.start, here.stop)])

    def other(self, s):
        me = lax.axis_index("row") * self.n_ch + lax.axis_index("ch")
        return jnp.bitwise_xor(lax.rem(me, self.half), s)

    def exchange_all(self, blocks):
        return lax.all_to_all(
            blocks, ("row", "ch"), split_axis=0, concat_axis=0, tiled=True, axis_index_groups=[self.order]
        )

    def exchange_half(self, blocks):
        groups = [[first + n for n in self.inside] for first in (0, self.half)]
        return lax.all_to_all(
            blocks, ("row", "ch"), split_axis=0, concat_axis=0, tiled=True, axis_index_groups=groups
        )

    def swap(self, block, s):
        return lax.ppermute(block, ("row", "ch"), [(n, n ^ s) for n in range(self.devices)])

    def permute(self, mine, mates):
        mates = self.swap(mates, self.mate)
        shape = jax.ShapeDtypeStruct((2,) + mine.shape[1:], mine.dtype)
        pairs = call(merge_kernel, [shape] * (len(self.hops) - 1), [], mine, mates)
        return [mine, mates] + [self.swap(pair, s) for pair, s in zip(pairs, self.hops[1:])]

    def received(self, refs):
        mine, mates, *pairs = refs
        found = [(0, mine.at[0]), (self.mate, mates.at[0])]
        for s, pair in zip(self.hops[1:], pairs):
            found += [(s, pair.at[0]), (s ^ self.mate, pair.at[1])]
        return found


def merge_kernel(mine_ref, mates_ref, *outs):
    for n, out_ref in enumerate(outs, 1):
        out_ref[0] = mine_ref[n]
        out_ref[1] = mates_ref[n]


def plane(ref, place, c):
    return jnp.concatenate(
        [
            jnp.concatenate([ref[n, c] for n in column_of], axis=0)
            for column_of in zip(*place)
        ],
        axis=1,
    )


def store_plane(ref, place, c, value):
    rows, cols = ref.shape[-2:]
    for r, row_of in enumerate(place):
        for b, n in enumerate(row_of):
            ref[n, c] = value[r * rows : (r + 1) * rows, b * cols : (b + 1) * cols]


def tri_kernel(lay, r_ref, *refs):
    l_refs, (t_ref, l_ref) = refs[: lay.n_hops], refs[lay.n_hops :]
    for s, source in lay.received(l_refs):
        l_ref[lay.other(s)] = source[...]
    for c in range(t_ref.shape[1]):
        tri = dot(plane(l_ref, lay.near_place, c), plane(r_ref, lay.all_place, c), 1, 1)
        store_plane(t_ref, lay.half_place, c, tri.astype(BF16))


def factor_back_kernel(lay, gt_ref, l_ref, r_ref, gr_hbm, *refs):
    mine_out, mate_out, gl_ref, gr_ref, sems = refs
    copies = []
    for c in range(gt_ref.shape[1]):
        right = dot(plane(gt_ref, lay.half_place, c), plane(l_ref, lay.near_place, c), 0, 0)
        store_plane(gr_ref, lay.all_place, c, right.astype(BF16))
        here = (slice(None), c)
        copies.append(pltpu.make_async_copy(gr_ref.at[here], gr_hbm.at[here], sems.at[c]))
        copies[-1].start()
    for c in range(gt_ref.shape[1]):
        left = dot(plane(gt_ref, lay.half_place, c), plane(r_ref, lay.all_place, c), 1, 0)
        store_plane(gl_ref, lay.near_place, c, left.astype(BF16))
    for n, s in enumerate(lay.hops):
        mine_out[n] = gl_ref[lay.other(s)]
        mate_out[n] = gl_ref[lay.other(s ^ lay.mate)]
    for copy in copies:
        copy.wait()


def by_channel(
    n_row, n_ch, pair_act, cotangent, in_gain, in_bias, proj_weight, out_gain, out_bias, out_weight
):
    lay = Layout(n_row, n_ch)
    rows, cols, width = pair_act.shape
    mine = width // lay.half
    struct = jax.ShapeDtypeStruct
    half = pltpu.VMEM((rows, width, cols), BF16)
    weight_t = pltpu.VMEM((4 * width, width), BF16)
    in_gain, in_bias, out_gain, out_bias = (
        v.reshape(1, width) for v in (in_gain, in_bias, out_gain, out_bias)
    )

    some = struct((len(lay.hops), mine, rows, cols), BF16)
    one = struct((lay.half, mine, rows, cols), BF16)
    one_here = pltpu.VMEM(one.shape, BF16)
    two_shape = (lay.devices, mine, rows, cols)
    row = pltpu.VMEM((1, width), F32)
    weight = pltpu.VMEM(proj_weight.shape, BF16)
    out_weight_here = pltpu.VMEM((width, width), BF16)
    both_weights = pltpu.VMEM((width, 2 * width), BF16)
    both_turned = pltpu.VMEM((2 * width, width), BF16)
    right, normal_in = call(
        functools.partial(right_kernel, lay),
        [pltpu.HBM(two_shape, BF16), struct((rows // 2, width, 2 * cols), BF16)],
        [
            half,
            row,
            row,
            both_weights,
            both_turned,
            half,
            one_here,
            pltpu.SemaphoreType.DMA((4 + PARTS // 2,)),
            pltpu.SemaphoreType.DMA((lay.devices,)),
        ],
        pair_act,
        in_gain,
        in_bias,
        proj_weight,
        hbm=4,
    )
    left = call(
        functools.partial(left_kernel, lay),
        [some, some],
        [both_weights, both_turned, half, one_here, pltpu.SemaphoreType.DMA((2,))],
        proj_weight,
        normal_in,
        hbm=1,
    )
    right = lay.exchange_all(right)
    left = lay.permute(*left)
    h, fac = call(
        gate_kernel,
        [pltpu.VMEM((rows, width, cols), F32), pltpu.HBM((rows, 4 * width, cols), BF16)],
        [
            pltpu.VMEM((rows, 4 * width, cols), BF16),
            weight_t,
            half,
            half,
            row,
            row,
            weight,
            row,
            out_weight_here,
            pltpu.SemaphoreType.DMA((7,)),
            pltpu.SemaphoreType.DMA((PARTS,)),
        ],
        pair_act,
        cotangent,
        in_gain,
        in_bias,
        proj_weight,
        out_gain,
        out_weight,
        hbm=7,
    )
    right, h, fac = lax.optimization_barrier((right, h, fac))
    tri, left = call(functools.partial(tri_kernel, lay), [one, one], [], right, *left)
    tri = lay.exchange_half(tri)
    grad_tri, tri = call(
        functools.partial(tri_back_kernel, lay),
        [one, pltpu.HBM(one.shape, BF16)],
        [half, half, pltpu.SemaphoreType.DMA(())],
        tri,
        h,
    )
    grad_right, *grad_left = call(
        functools.partial(factor_back_kernel, lay),
        [pltpu.HBM(two_shape, BF16), some, some],
        [one_here, pltpu.VMEM(two_shape, BF16), pltpu.SemaphoreType.DMA((mine,))],
        lay.exchange_half(grad_tri),
        left,
        right,
    )
    grad_right = lay.exchange_all(grad_right)
    grad_left = lay.permute(*grad_left)
    grad_in_first, normed_first, fac_first, grad_in, normed_t, scale = call(
        functools.partial(logit_kernel, lay),
        [
            pltpu.VMEM((rows // PARTS, width, cols), BF16),
            pltpu.VMEM((rows // PARTS, width, cols), BF16),
            pltpu.VMEM((rows // PARTS, 4 * width, cols), BF16),
            pltpu.HBM((rows, width, cols), BF16),
            pltpu.HBM((rows, width, cols), BF16),
            pltpu.VMEM((rows, cols), F32),
        ],
        [
            half,
            half,
            half,
            pltpu.SemaphoreType.DMA((2,)),
            one_here,
            half,
            half,
            row,
            row,
            weight,
            row,
            row,
            out_weight_here,
            pltpu.SemaphoreType.DMA((10,)),
        ],
        fac,
        tri,
        pair_act,
        cotangent,
        in_gain,
        in_bias,
        proj_weight,
        out_gain,
        out_bias,
        out_weight,
        hbm=10,
    )
    return call(
        functools.partial(pair_kernel, lay),
        pltpu.HBM((rows, cols, width), BF16),
        [
            one_here,
            half,
            half,
            pltpu.VMEM((rows, 4 * width, cols), BF16),
            half,
            half,
            half,
            pltpu.SemaphoreType.DMA((3, PARTS)),
            pltpu.SemaphoreType.DMA((rows // 2,)),
        ],
        fac,
        normed_t,
        grad_in,
        fac_first,
        normed_first,
        grad_in_first,
        grad_right,
        scale,
        in_gain,
        proj_weight,
        *grad_left,
        hbm=3,
    )


def by_row(
    pair_act, cotangent, in_gain, in_bias, proj_weight, out_gain, out_bias, out_weight
):
    rows_here, cols_here, width = pair_act.shape
    flat = pair_act.astype(jnp.float32).reshape(rows_here * cols_here, width)
    normed, scale_inv = normalize(flat, -1)
    normal_in = (normed * in_gain + in_bias).astype(jnp.bfloat16)
    projected = jnp.einsum("pd,de->ep", normal_in, proj_weight, preferred_element_type=jnp.float32)
    blocks = jnp.split(projected, 5, axis=0)
    left_sig = jax.nn.sigmoid(blocks[1])
    right_sig = jax.nn.sigmoid(blocks[3])
    left_fac = (left_sig * blocks[0]).astype(jnp.bfloat16).reshape(width, rows_here, cols_here)
    right_fac = (right_sig * blocks[2]).astype(jnp.bfloat16).reshape(width, rows_here, cols_here)
    left_chan, right_chan = (
        lax.all_to_all(left_fac, "ch", split_axis=0, concat_axis=2, tiled=True),
        lax.all_to_all(right_fac, "ch", split_axis=0, concat_axis=2, tiled=True),
    )
    tri_chan = jnp.einsum(
        "cik,cjk->cij",
        left_chan,
        lax.all_gather(right_chan, "row", axis=1, tiled=True),
        preferred_element_type=jnp.float32,
    ).astype(jnp.bfloat16)
    tri_back = lax.all_to_all(tri_chan, "ch", split_axis=2, concat_axis=0, tiled=True)
    tri_hat, tri_inv = normalize(tri_back.astype(jnp.float32).reshape(width, -1), 0)
    normal_out = (tri_hat * out_gain[:, None] + out_bias[:, None]).astype(jnp.bfloat16)
    mixed = jnp.einsum("cp,ce->ep", normal_out, out_weight, preferred_element_type=jnp.float32)
    out_gate = jax.nn.sigmoid(blocks[4])
    grad_out = cotangent.astype(jnp.float32).reshape(rows_here * cols_here, width).T
    grad_mixed = (grad_out * out_gate).astype(jnp.bfloat16)
    grad_logit = grad_out * mixed * out_gate * (1.0 - out_gate)
    grad_normal = jnp.einsum(
        "ep,ce->cp", grad_mixed, out_weight, preferred_element_type=jnp.float32
    )
    grad_tri = norm_back(grad_normal * out_gain[:, None], tri_hat, tri_inv, 0)
    grad_tri = grad_tri.astype(jnp.bfloat16).reshape(width, rows_here, cols_here)
    grad_chan = lax.all_to_all(grad_tri, "ch", split_axis=0, concat_axis=2, tiled=True)
    grad_cols = lax.all_to_all(grad_chan, "row", split_axis=2, concat_axis=1, tiled=True)
    grad_left = jnp.einsum(
        "cij,cjk->cik",
        grad_chan,
        lax.all_gather(right_chan, "row", axis=1, tiled=True),
        preferred_element_type=jnp.float32,
    )
    grad_right = jnp.einsum(
        "cij,cik->cjk",
        grad_cols,
        lax.all_gather(left_chan, "row", axis=1, tiled=True),
        preferred_element_type=jnp.float32,
    )
    left_back, right_back = (
        lax.all_to_all(
            grad_left.astype(jnp.bfloat16), "ch", split_axis=2, concat_axis=0, tiled=True
        ),
        lax.all_to_all(
            grad_right.astype(jnp.bfloat16), "ch", split_axis=2, concat_axis=0, tiled=True
        ),
    )
    left_grad = left_back.astype(jnp.float32).reshape(width, -1)
    right_grad = right_back.astype(jnp.float32).reshape(width, -1)
    grad_proj = jnp.concatenate(
        [
            left_grad * left_sig,
            left_grad * blocks[0] * left_sig * (1.0 - left_sig),
            right_grad * right_sig,
            right_grad * blocks[2] * right_sig * (1.0 - right_sig),
            grad_logit,
        ],
        axis=0,
    ).astype(jnp.bfloat16)
    grad_in = jnp.einsum("ep,de->pd", grad_proj, proj_weight, preferred_element_type=jnp.float32)
    grad_pair = norm_back(grad_in * in_gain, normed, scale_inv, -1)
    return grad_pair.astype(jnp.bfloat16).reshape(rows_here, cols_here, width)


def solution(mesh):
    n_row, n_ch = mesh.shape["row"], mesh.shape["ch"]
    placed = (P("row", "ch", None), P("row", "ch", None), P(), P(), P(), P(), P(), P())

    def on_device(*args):
        rows, cols, width = args[0].shape
        devices, outer, group = n_row * n_ch, math.isqrt(n_row), BLOCK // rows
        if (
            devices & (devices - 1) == 0
            and n_row >= 4
            and n_row % outer == 0
            and (devices // outer) % (2 * n_ch) == 0
            and outer % 2 == 0
            and width % (devices // 2) == 0
            and rows % (2 * PARTS) == 0
            and BLOCK % rows == 0
            and group % (width // (devices // 2)) == 0
            and width % (2 * group) == 0
            and cols % 128 == 0
            and width <= 256
            and width & (width - 1) == 0
        ):
            return by_channel(n_row, n_ch, *args)
        return by_row(*args)

    return jax.shard_map(
        on_device, mesh=mesh, in_specs=placed, out_specs=P("row", "ch", None), check_vma=False
    )
```

```python
import functools
import math

import jax
import jax.numpy as jnp
from jax import lax
from jax.experimental import pallas as pl
from jax.experimental.pallas import tpu as pltpu
from jax.sharding import PartitionSpec as P

EPSILON = 1e-05
F32 = jnp.float32
BF16 = jnp.bfloat16
UNROLL = 4
BLOCK = 256
PARTS = 4


def dot(a, b, da, db):
    return lax.dot_general(a, b, (((da,), (db,)), ((), ())), preferred_element_type=F32)


def sigmoid(values):
    return 0.5 * jnp.tanh(0.5 * values) + 0.5


def normalize(values, axis):
    center = jnp.mean(values, axis=axis, keepdims=True)
    shifted = values - center
    scale_inv = lax.rsqrt(jnp.mean(shifted * shifted, axis=axis, keepdims=True) + EPSILON)
    return (shifted * scale_inv, scale_inv)


def norm_back(grad_hat, normed, scale_inv, axis):
    first = jnp.mean(grad_hat, axis=axis, keepdims=True)
    second = jnp.mean(grad_hat * normed, axis=axis, keepdims=True)
    return scale_inv * (grad_hat - first - normed * second)


def column(row, width):
    return jnp.broadcast_to(row, (width, row.shape[-1])).T


def call(kernel, outs, scratch, *args, hbm=0, limit=16):
    single = not isinstance(outs, (list, tuple))
    args = [pltpu.with_memory_space_constraint(a, pltpu.HBM) if n < hbm else a for n, a in enumerate(args)]
    specs = [pl.BlockSpec(memory_space=pltpu.HBM if n < hbm else pltpu.VMEM) for n in range(len(args))]
    out_specs = [
        pl.BlockSpec(memory_space=getattr(out, "memory_space", pltpu.VMEM))
        for out in ([outs] if single else outs)
    ]
    return pl.pallas_call(
        kernel,
        out_shape=outs if single else tuple(outs),
        in_specs=specs,
        out_specs=out_specs[0] if single else tuple(out_specs),
        scratch_shapes=scratch,
        compiler_params=pltpu.CompilerParams(vmem_limit_bytes=limit * 1024 * 1024),
    )(*args)


def permutation(outer, inner):
    to = lax.broadcasted_iota(jnp.int32, (BLOCK, BLOCK), 0)
    start = lax.broadcasted_iota(jnp.int32, (BLOCK, BLOCK), 1)
    return (start == to % inner * outer + to // inner).astype(F32).astype(BF16)


def identity(size):
    first = lax.broadcasted_iota(jnp.int32, (size, size), 0)
    return (first == lax.broadcasted_iota(jnp.int32, (size, size), 1)).astype(F32).astype(BF16)


def swapped(swap, blocks):
    cols = blocks[0].shape[-1]
    wide = jnp.concatenate([block.reshape(BLOCK, cols) for block in blocks], axis=1)
    wide = dot(swap, wide, 1, 0).astype(BF16)
    return [wide[:, n * cols : (n + 1) * cols] for n in range(len(blocks))]


def fetched(sources, targets, sems):
    copies = [
        pltpu.make_async_copy(source, target, sems.at[n])
        for n, (source, target) in enumerate(zip(sources, targets))
    ]
    for copy in copies:
        copy.start()
    for copy in copies:
        copy.wait()


def weight_copies(w_hbm, w_ref, first, sems):
    width = w_hbm.shape[0]
    return [
        pltpu.make_async_copy(
            w_hbm.at[:, (first + n) * width : (first + n + 1) * width],
            w_ref.at[:, n * width : (n + 1) * width],
            sems.at[n],
        )
        for n in range(2)
    ]


def right_kernel(
    lay, x_hbm, gain_hbm, bias_hbm, w_hbm, r_hbm, n_ref, x_ref, gain_ref, bias_ref, w_ref, wt_ref, r_ref, right_ref, sems, out_sems
):
    rows, cols, width = x_ref.shape
    mine = width // lay.half
    parts = sems.shape[0] - 4
    size = rows // parts

    def fetch(p):
        here = pl.ds(p * size, size)
        return pltpu.make_async_copy(x_hbm.at[here], x_ref.at[here], sems.at[4 + p])

    small = [
        pltpu.make_async_copy(gain_hbm, gain_ref, sems.at[2]),
        pltpu.make_async_copy(bias_hbm, bias_ref, sems.at[3]),
    ]
    weights = weight_copies(w_hbm, w_ref, 2, sems)
    fetch(0).start()
    for copy in small + weights:
        copy.start()
    for p in range(1, parts):
        fetch(p).start()
    group = BLOCK // rows
    swap = permutation(group, rows)

    def normal(p):
        fetch(p).wait()
        for n in range(0, size, 2):
            i = p * size + n
            shifted = dot(center, x_ref[pl.ds(i, 2)].reshape(2 * cols, width), 1, 1)
            scale_inv = lax.rsqrt(jnp.mean(shifted * shifted, axis=0, keepdims=True) + EPSILON)
            n_ref[p * size // 2 + n // 2] = (shifted * scale_inv * gain + bias).astype(BF16)

    def project(p):
        for n in range(0, size, 2):
            i = p * size + n
            proj = dot(wt_ref[...], n_ref[p * size // 2 + n // 2], 1, 0)
            right = (sigmoid(proj[width:]) * proj[:width]).astype(BF16)
            for m in range(2):
                r_ref[i + m] = right[:, m * cols : (m + 1) * cols]

    def body(p, _):
        normal(p)
        project(p - 1)
        return 0

    center = (identity(width).astype(F32) - 1.0 / width).astype(BF16)
    for copy in small:
        copy.wait()
    gain = column(gain_ref[...], 2 * cols)
    bias = column(bias_ref[...], 2 * cols)
    normal(0)
    for copy in weights:
        copy.wait()
    wt_ref[...] = w_ref[...].astype(F32).T.astype(BF16)
    lax.fori_loop(1, parts, body, 0)
    project(parts - 1)
    out = []
    blocks = places(width, mine, rows)
    for k in range(0, len(blocks), 2):
        pair = blocks[k : k + 2]
        for (to, _here), right in zip(pair, swapped(swap, [r_ref[:, here] for _to, here in pair])):
            right_ref[to] = right.reshape(group // mine, mine, rows, cols)
            for share in range(to.start, to.stop):
                for n, device in enumerate(lay.order):
                    if device % lay.half == share:
                        out.append(pltpu.make_async_copy(right_ref.at[share], r_hbm.at[n], out_sems.at[n]))
                        out[-1].start()
    for copy in out:
        copy.wait()


def left_kernel(lay, w_hbm, n_ref, mine_out, mate_out, w_ref, wt_ref, l_ref, left_ref, sems):
    rows, width, cols = l_ref.shape
    mine = width // lay.half
    group = BLOCK // rows
    weights = weight_copies(w_hbm, w_ref, 0, sems)
    for copy in weights:
        copy.start()
    for copy in weights:
        copy.wait()
    wt_ref[...] = w_ref[...].astype(F32).T.astype(BF16)
    swap = permutation(group, rows)

    def body(n, _):
        proj = dot(wt_ref[...], n_ref[n], 1, 0)
        left = (sigmoid(proj[width:]) * proj[:width]).astype(BF16)
        for m in range(2):
            l_ref[2 * n + m] = left[:, m * cols : (m + 1) * cols]
        return 0

    lax.fori_loop(0, rows // 2, body, 0, unroll=2)
    blocks = places(width, mine, rows)
    for k in range(0, len(blocks), 2):
        pair = blocks[k : k + 2]
        for (to, _here), left in zip(pair, swapped(swap, [l_ref[:, here] for _to, here in pair])):
            left_ref[to] = left.reshape(group // mine, mine, rows, cols)
    for n, s in enumerate(lay.hops):
        mine_out[n] = left_ref[lay.other(s)]
        mate_out[n] = left_ref[lay.other(s ^ lay.mate)]


def gate_kernel(*refs):
    sources, (h_ref, fac_hbm, fac_ref, wt_ref), targets, (sems, out_sems) = (
        refs[:7],
        refs[7:11],
        refs[11:18],
        refs[18:],
    )
    x_ref, cot_ref, gain_ref, bias_ref, w_ref, ogain_ref, ow_ref = targets
    rows, cols, width = x_ref.shape
    fetched(sources, targets, sems)
    wt_ref[...] = w_ref[:, : 4 * width].astype(F32).T.astype(BF16)
    ogain = column(ogain_ref[...], cols)

    def body(i, _):
        normed, _s = normalize(x_ref[i].astype(F32), -1)
        normal_in = (normed * gain_ref[...] + bias_ref[...]).astype(BF16)
        proj = dot(wt_ref[...], normal_in, 1, 1)
        for side in range(2):
            val = proj[2 * side * width : (2 * side + 1) * width]
            sig = sigmoid(proj[(2 * side + 1) * width : (2 * side + 2) * width])
            fac_ref[i, 2 * side * width : (2 * side + 1) * width] = sig.astype(BF16)
            fac_ref[i, (2 * side + 1) * width : (2 * side + 2) * width] = (
                val * sig * (1.0 - sig)
            ).astype(BF16)
        out_gate = sigmoid(dot(normal_in, w_ref[:, 4 * width :], 1, 0))
        grad_mixed = (cot_ref[i].astype(F32) * out_gate).astype(BF16)
        h_ref[i] = dot(ow_ref[...], grad_mixed, 1, 1) * ogain
        return 0

    size = rows // PARTS

    def send(p):
        here = pl.ds(p * size, size)
        return pltpu.make_async_copy(fac_ref.at[here], fac_hbm.at[here], out_sems.at[p])

    def part(p, _):
        for n in range(size):
            body(p * size + n, 0)
        send(p).start()
        return 0

    lax.fori_loop(0, PARTS, part, 0)
    for p in range(PARTS):
        send(p).wait()


def places(n_channels, mine, rows):
    group = BLOCK // rows
    return [
        (slice(c // mine, (c + group) // mine), slice(c, c + group)) for c in range(0, n_channels, group)
    ]


def to_rows(lay, t_ref, ts_ref):
    rows, width, cols = ts_ref.shape
    mine = t_ref.shape[1]
    group = BLOCK // rows
    swap = permutation(rows, group)
    blocks = places(width, mine, rows)
    for n in range(0, len(blocks), 2):
        pair = blocks[n : n + 2]
        for (_to, here), block in zip(pair, swapped(swap, [lay.shares(t_ref, to) for to, _here in pair])):
            ts_ref[:, here] = block.reshape(rows, group, cols)


def tri_back_kernel(lay, t_ref, h_ref, gt_ref, t_hbm, ts_ref, gs_ref, sem):
    rows, width, cols = h_ref.shape
    mine = t_ref.shape[1]
    group = BLOCK // rows
    copy = pltpu.make_async_copy(t_ref, t_hbm, sem)
    copy.start()
    back = permutation(group, rows)
    to_rows(lay, t_ref, ts_ref)

    def body(i, _):
        tri, h = ts_ref[i].astype(F32), h_ref[i]
        shifted = tri - jnp.mean(tri, axis=0, keepdims=True)
        first = jnp.mean(h, axis=0, keepdims=True)
        both = jnp.mean(h * shifted, axis=0, keepdims=True)
        tri_inv = lax.rsqrt(jnp.mean(shifted * shifted, axis=0, keepdims=True) + EPSILON)
        gs_ref[i] = (tri_inv * (h - first - shifted * (both * tri_inv * tri_inv))).astype(BF16)
        return 0

    lax.fori_loop(0, rows, body, 0, unroll=2 * UNROLL)
    blocks = places(width, mine, rows)
    for n in range(0, len(blocks), 2):
        pair = blocks[n : n + 2]
        for (to, _here), block in zip(pair, swapped(back, [gs_ref[:, here] for _to, here in pair])):
            block = block.reshape(group // mine, mine, rows, cols)
            for share in range(to.start, to.stop):
                gt_ref[lay.inside.index(share)] = block[share - to.start]
    copy.wait()


def logit_kernel(lay, *refs):
    (fac_hbm, *sources), refs = refs[:10], refs[10:]
    (gin0_ref, nt0_ref, fac0_ref, gin_hbm, nt_hbm, s_ref), refs = refs[:6], refs[6:]
    (ts_ref, gin_ref, nt_ref, out_sems), targets, sems = refs[:4], refs[4:13], refs[13]
    t_ref, x_ref, cot_ref, gain_ref, bias_ref, w_ref, ogain_ref, obias_ref, ow_ref = targets
    rows, cols, width = x_ref.shape
    first = pl.ds(0, nt0_ref.shape[0])
    fetched([*sources, fac_hbm.at[first]], [*targets, fac0_ref], sems)
    to_rows(lay, t_ref, ts_ref)
    ogain = column(ogain_ref[...], cols)
    obias = column(obias_ref[...], cols)

    def body(i, _):
        normed, scale_inv = normalize(x_ref[i].astype(F32), -1)
        normal_in = (normed * gain_ref[...] + bias_ref[...]).astype(BF16)
        out_gate = sigmoid(dot(normal_in, w_ref[:, 4 * width :], 1, 0))
        tri_hat, _s = normalize(ts_ref[i].astype(F32), 0)
        normal_out = (tri_hat * ogain + obias).astype(BF16)
        mixed = dot(normal_out, ow_ref[...], 0, 0)
        grad_logit = cot_ref[i].astype(F32) * mixed * out_gate * (1.0 - out_gate)
        gin_ref[i] = dot(w_ref[:, 4 * width :], grad_logit.astype(BF16), 1, 1).astype(BF16)
        nt_ref[i] = normed.T.astype(BF16)
        s_ref[pl.ds(i, 1), :] = jnp.broadcast_to(scale_inv, (cols, width)).T[:1]
        return 0

    lax.fori_loop(0, rows, body, 0, unroll=UNROLL)
    gin0_ref[...] = gin_ref[first]
    nt0_ref[...] = nt_ref[first]
    copies = [
        pltpu.make_async_copy(gin_ref, gin_hbm, out_sems.at[0]),
        pltpu.make_async_copy(nt_ref, nt_hbm, out_sems.at[1]),
    ]
    for copy in copies:
        copy.start()
    for copy in copies:
        copy.wait()


def pair_kernel(
    lay, fac_hbm, nt_hbm, gin_hbm, fac0_ref, nt0_ref, gin0_ref, r_ref, s_ref, gain_ref, w_ref, *refs
):
    l_refs, refs = refs[: lay.n_hops], refs[lay.n_hops :]
    out_hbm, l_ref, ls_ref, rs_ref, fac_ref, nt_ref, gin_ref, out_ref, sems, out_sems = refs
    rows, cols, width = out_ref.shape
    mine = width // lay.half
    parts = sems.shape[1]
    size = rows // parts

    def fetch(p):
        here = pl.ds(p * size, size)
        return [
            pltpu.make_async_copy(fac_hbm.at[here], fac_ref.at[here], sems.at[0, p]),
            pltpu.make_async_copy(nt_hbm.at[here], nt_ref.at[here], sems.at[1, p]),
            pltpu.make_async_copy(gin_hbm.at[here], gin_ref.at[here], sems.at[2, p]),
        ]

    def send(n):
        here = pl.ds(2 * n, 2)
        return pltpu.make_async_copy(out_ref.at[here], out_hbm.at[here], out_sems.at[n])

    for p in range(1, parts):
        for copy in fetch(p):
            copy.start()
    gain = column(gain_ref[...], cols)
    eye = identity(cols)
    group = BLOCK // rows
    swap = permutation(rows, group)
    for s, source in lay.received(l_refs):
        l_ref[lay.other(s)] = source[...]
    for to, here in places(width, mine, rows):
        sums = []
        for share in range(to.start, to.stop):
            one, two = (
                r_ref[n]
                for n, device in enumerate(lay.order)
                if device % lay.half == share
            )
            sums.append(one + two)
        left, right = swapped(swap, [l_ref[to], jnp.stack(sums)])
        ls_ref[:, here] = left.reshape(rows, group, cols)
        rs_ref[:, here] = right.reshape(rows, group, cols)

    def part(p, fac_here, nt_here, gin_here):
        for n in range(0, size, 2):
            i = p * size + n
            blocks = []
            for m in range(2):
                left, right, fac = ls_ref[i + m], rs_ref[i + m], fac_here[i + m]
                blocks.append(
                    jnp.concatenate(
                        [
                            left * fac[:width],
                            left * fac[width : 2 * width],
                            right * fac[2 * width : 3 * width],
                            right * fac[3 * width :],
                        ],
                        axis=0,
                    )
                )
            grad_in = dot(w_ref[:, : 4 * width], jnp.concatenate(blocks, axis=1), 1, 0)
            for m in range(2):
                grad = (grad_in[:, m * cols : (m + 1) * cols] + gin_here[i + m].astype(F32)) * gain
                scale_inv = s_ref[pl.ds(i + m, 1), :]
                normed = nt_here[i + m].astype(F32)
                result = norm_back(grad, normed, scale_inv, 0).astype(BF16)
                out_ref[i + m] = dot(eye, result, 1, 1).astype(BF16)
            send(i // 2).start()

    part(0, fac0_ref, nt0_ref, gin0_ref)
    for p in range(1, parts):
        for copy in fetch(p):
            copy.wait()
    for p in range(1, parts):
        part(p, fac_ref, nt_ref, gin_ref)
    for n in range(rows // 2):
        send(n).wait()


class Layout:
    def __init__(self, n_row, n_ch):
        self.n_row, self.n_ch = n_row, n_ch
        self.devices = n_row * n_ch
        self.half = self.devices // 2
        outer = math.isqrt(n_row)
        self.inner = self.devices // outer
        rest = [
            2 * n_ch * far + b for b in range(n_ch) for far in range(self.inner // (2 * n_ch))
        ]

        def spread(parts):
            return [o * self.inner + n + n_ch * core for n in rest for o in range(parts) for core in range(2)]

        self.order, self.inside = spread(outer), spread(outer // 2)
        self.mate = n_ch
        self.hops = [s for s in range(self.half) if s & self.mate == 0]
        self.hops[3:] = self.hops[:2:-1]
        self.n_hops = len(self.hops) + 1
        self.all_place = self.place(self.order, n_row)
        self.half_place = self.place(self.inside, n_row // 2)
        self.near_place = self.place(list(range(self.half)), n_row // 2)

    def place(self, order, n_row):
        return [[order.index(r * self.n_ch + b) for b in range(self.n_ch)] for r in range(n_row)]

    def shares(self, ref, here):
        return jnp.stack([ref[self.inside.index(share)] for share in range(here.start, here.stop)])

    def other(self, s):
        me = lax.axis_index("row") * self.n_ch + lax.axis_index("ch")
        return jnp.bitwise_xor(lax.rem(me, self.half), s)

    def exchange_all(self, blocks):
        return lax.all_to_all(
            blocks, ("row", "ch"), split_axis=0, concat_axis=0, tiled=True, axis_index_groups=[self.order]
        )

    def exchange_half(self, blocks):
        groups = [[first + n for n in self.inside] for first in (0, self.half)]
        return lax.all_to_all(
            blocks, ("row", "ch"), split_axis=0, concat_axis=0, tiled=True, axis_index_groups=groups
        )

    def swap(self, block, s):
        return lax.ppermute(block, ("row", "ch"), [(n, n ^ s) for n in range(self.devices)])

    def permute(self, mine, mates):
        mates = self.swap(mates, self.mate)
        shape = jax.ShapeDtypeStruct((2,) + mine.shape[1:], mine.dtype)
        pairs = call(merge_kernel, [shape] * (len(self.hops) - 1), [], mine, mates)
        return [mine, mates] + [self.swap(pair, s) for pair, s in zip(pairs, self.hops[1:])]

    def received(self, refs):
        mine, mates, *pairs = refs
        found = [(0, mine.at[0]), (self.mate, mates.at[0])]
        for s, pair in zip(self.hops[1:], pairs):
            found += [(s, pair.at[0]), (s ^ self.mate, pair.at[1])]
        return found


def merge_kernel(mine_ref, mates_ref, *outs):
    for n, out_ref in enumerate(outs, 1):
        out_ref[0] = mine_ref[n]
        out_ref[1] = mates_ref[n]


def plane(ref, place, c):
    return jnp.concatenate(
        [
            jnp.concatenate([ref[n, c] for n in column_of], axis=0)
            for column_of in zip(*place)
        ],
        axis=1,
    )


def store_plane(ref, place, c, value):
    rows, cols = ref.shape[-2:]
    for r, row_of in enumerate(place):
        for b, n in enumerate(row_of):
            ref[n, c] = value[r * rows : (r + 1) * rows, b * cols : (b + 1) * cols]


def tri_kernel(lay, r_ref, *refs):
    l_refs, (t_ref, l_ref) = refs[: lay.n_hops], refs[lay.n_hops :]
    for s, source in lay.received(l_refs):
        l_ref[lay.other(s)] = source[...]
    for c in range(t_ref.shape[1]):
        tri = dot(plane(l_ref, lay.near_place, c), plane(r_ref, lay.all_place, c), 1, 1)
        store_plane(t_ref, lay.half_place, c, tri.astype(BF16))


def factor_back_kernel(lay, gt_ref, l_ref, r_ref, gr_hbm, *refs):
    mine_out, mate_out, gl_ref, gr_ref, sems = refs
    copies = []
    for c in range(gt_ref.shape[1]):
        right = dot(plane(gt_ref, lay.half_place, c), plane(l_ref, lay.near_place, c), 0, 0)
        store_plane(gr_ref, lay.all_place, c, right.astype(BF16))
        here = (slice(None), c)
        copies.append(pltpu.make_async_copy(gr_ref.at[here], gr_hbm.at[here], sems.at[c]))
        copies[-1].start()
    for c in range(gt_ref.shape[1]):
        left = dot(plane(gt_ref, lay.half_place, c), plane(r_ref, lay.all_place, c), 1, 0)
        store_plane(gl_ref, lay.near_place, c, left.astype(BF16))
    for n, s in enumerate(lay.hops):
        mine_out[n] = gl_ref[lay.other(s)]
        mate_out[n] = gl_ref[lay.other(s ^ lay.mate)]
    for copy in copies:
        copy.wait()


def by_channel(
    n_row, n_ch, pair_act, cotangent, in_gain, in_bias, proj_weight, out_gain, out_bias, out_weight
):
    lay = Layout(n_row, n_ch)
    rows, cols, width = pair_act.shape
    mine = width // lay.half
    struct = jax.ShapeDtypeStruct
    half = pltpu.VMEM((rows, width, cols), BF16)
    weight_t = pltpu.VMEM((4 * width, width), BF16)
    in_gain, in_bias, out_gain, out_bias = (
        v.reshape(1, width) for v in (in_gain, in_bias, out_gain, out_bias)
    )

    some = struct((len(lay.hops), mine, rows, cols), BF16)
    one = struct((lay.half, mine, rows, cols), BF16)
    one_here = pltpu.VMEM(one.shape, BF16)
    two_shape = (lay.devices, mine, rows, cols)
    row = pltpu.VMEM((1, width), F32)
    weight = pltpu.VMEM(proj_weight.shape, BF16)
    out_weight_here = pltpu.VMEM((width, width), BF16)
    both_weights = pltpu.VMEM((width, 2 * width), BF16)
    both_turned = pltpu.VMEM((2 * width, width), BF16)
    right, normal_in = call(
        functools.partial(right_kernel, lay),
        [pltpu.HBM(two_shape, BF16), struct((rows // 2, width, 2 * cols), BF16)],
        [
            half,
            row,
            row,
            both_weights,
            both_turned,
            half,
            one_here,
            pltpu.SemaphoreType.DMA((4 + PARTS // 2,)),
            pltpu.SemaphoreType.DMA((lay.devices,)),
        ],
        pair_act,
        in_gain,
        in_bias,
        proj_weight,
        hbm=4,
    )
    left = call(
        functools.partial(left_kernel, lay),
        [some, some],
        [both_weights, both_turned, half, one_here, pltpu.SemaphoreType.DMA((2,))],
        proj_weight,
        normal_in,
        hbm=1,
    )
    right = lay.exchange_all(right)
    left = lay.permute(*left)
    h, fac = call(
        gate_kernel,
        [pltpu.VMEM((rows, width, cols), F32), pltpu.HBM((rows, 4 * width, cols), BF16)],
        [
            pltpu.VMEM((rows, 4 * width, cols), BF16),
            weight_t,
            half,
            half,
            row,
            row,
            weight,
            row,
            out_weight_here,
            pltpu.SemaphoreType.DMA((7,)),
            pltpu.SemaphoreType.DMA((PARTS,)),
        ],
        pair_act,
        cotangent,
        in_gain,
        in_bias,
        proj_weight,
        out_gain,
        out_weight,
        hbm=7,
    )
    right, h, fac = lax.optimization_barrier((right, h, fac))
    tri, left = call(functools.partial(tri_kernel, lay), [one, one], [], right, *left)
    tri = lay.exchange_half(tri)
    grad_tri, tri = call(
        functools.partial(tri_back_kernel, lay),
        [one, pltpu.HBM(one.shape, BF16)],
        [half, half, pltpu.SemaphoreType.DMA(())],
        tri,
        h,
    )
    grad_right, *grad_left = call(
        functools.partial(factor_back_kernel, lay),
        [pltpu.HBM(two_shape, BF16), some, some],
        [one_here, pltpu.VMEM(two_shape, BF16), pltpu.SemaphoreType.DMA((mine,))],
        lay.exchange_half(grad_tri),
        left,
        right,
    )
    grad_right = lay.exchange_all(grad_right)
    grad_left = lay.permute(*grad_left)
    grad_in_first, normed_first, fac_first, grad_in, normed_t, scale = call(
        functools.partial(logit_kernel, lay),
        [
            pltpu.VMEM((rows // PARTS, width, cols), BF16),
            pltpu.VMEM((rows // PARTS, width, cols), BF16),
            pltpu.VMEM((rows // PARTS, 4 * width, cols), BF16),
            pltpu.HBM((rows, width, cols), BF16),
            pltpu.HBM((rows, width, cols), BF16),
            pltpu.VMEM((rows, cols), F32),
        ],
        [
            half,
            half,
            half,
            pltpu.SemaphoreType.DMA((2,)),
            one_here,
            half,
            half,
            row,
            row,
            weight,
            row,
            row,
            out_weight_here,
            pltpu.SemaphoreType.DMA((10,)),
        ],
        fac,
        tri,
        pair_act,
        cotangent,
        in_gain,
        in_bias,
        proj_weight,
        out_gain,
        out_bias,
        out_weight,
        hbm=10,
    )
    return call(
        functools.partial(pair_kernel, lay),
        pltpu.HBM((rows, cols, width), BF16),
        [
            one_here,
            half,
            half,
            pltpu.VMEM((rows, 4 * width, cols), BF16),
            half,
            half,
            half,
            pltpu.SemaphoreType.DMA((3, PARTS)),
            pltpu.SemaphoreType.DMA((rows // 2,)),
        ],
        fac,
        normed_t,
        grad_in,
        fac_first,
        normed_first,
        grad_in_first,
        grad_right,
        scale,
        in_gain,
        proj_weight,
        *grad_left,
        hbm=3,
    )


def by_row(
    pair_act, cotangent, in_gain, in_bias, proj_weight, out_gain, out_bias, out_weight
):
    rows_here, cols_here, width = pair_act.shape
    flat = pair_act.astype(jnp.float32).reshape(rows_here * cols_here, width)
    normed, scale_inv = normalize(flat, -1)
    normal_in = (normed * in_gain + in_bias).astype(jnp.bfloat16)
    projected = jnp.einsum("pd,de->ep", normal_in, proj_weight, preferred_element_type=jnp.float32)
    blocks = jnp.split(projected, 5, axis=0)
    left_sig = jax.nn.sigmoid(blocks[1])
    right_sig = jax.nn.sigmoid(blocks[3])
    left_fac = (left_sig * blocks[0]).astype(jnp.bfloat16).reshape(width, rows_here, cols_here)
    right_fac = (right_sig * blocks[2]).astype(jnp.bfloat16).reshape(width, rows_here, cols_here)
    left_chan, right_chan = (
        lax.all_to_all(left_fac, "ch", split_axis=0, concat_axis=2, tiled=True),
        lax.all_to_all(right_fac, "ch", split_axis=0, concat_axis=2, tiled=True),
    )
    tri_chan = jnp.einsum(
        "cik,cjk->cij",
        left_chan,
        lax.all_gather(right_chan, "row", axis=1, tiled=True),
        preferred_element_type=jnp.float32,
    ).astype(jnp.bfloat16)
    tri_back = lax.all_to_all(tri_chan, "ch", split_axis=2, concat_axis=0, tiled=True)
    tri_hat, tri_inv = normalize(tri_back.astype(jnp.float32).reshape(width, -1), 0)
    normal_out = (tri_hat * out_gain[:, None] + out_bias[:, None]).astype(jnp.bfloat16)
    mixed = jnp.einsum("cp,ce->ep", normal_out, out_weight, preferred_element_type=jnp.float32)
    out_gate = jax.nn.sigmoid(blocks[4])
    grad_out = cotangent.astype(jnp.float32).reshape(rows_here * cols_here, width).T
    grad_mixed = (grad_out * out_gate).astype(jnp.bfloat16)
    grad_logit = grad_out * mixed * out_gate * (1.0 - out_gate)
    grad_normal = jnp.einsum(
        "ep,ce->cp", grad_mixed, out_weight, preferred_element_type=jnp.float32
    )
    grad_tri = norm_back(grad_normal * out_gain[:, None], tri_hat, tri_inv, 0)
    grad_tri = grad_tri.astype(jnp.bfloat16).reshape(width, rows_here, cols_here)
    grad_chan = lax.all_to_all(grad_tri, "ch", split_axis=0, concat_axis=2, tiled=True)
    grad_cols = lax.all_to_all(grad_chan, "row", split_axis=2, concat_axis=1, tiled=True)
    grad_left = jnp.einsum(
        "cij,cjk->cik",
        grad_chan,
        lax.all_gather(right_chan, "row", axis=1, tiled=True),
        preferred_element_type=jnp.float32,
    )
    grad_right = jnp.einsum(
        "cij,cik->cjk",
        grad_cols,
        lax.all_gather(left_chan, "row", axis=1, tiled=True),
        preferred_element_type=jnp.float32,
    )
    left_back, right_back = (
        lax.all_to_all(
            grad_left.astype(jnp.bfloat16), "ch", split_axis=2, concat_axis=0, tiled=True
        ),
        lax.all_to_all(
            grad_right.astype(jnp.bfloat16), "ch", split_axis=2, concat_axis=0, tiled=True
        ),
    )
    left_grad = left_back.astype(jnp.float32).reshape(width, -1)
    right_grad = right_back.astype(jnp.float32).reshape(width, -1)
    grad_proj = jnp.concatenate(
        [
            left_grad * left_sig,
            left_grad * blocks[0] * left_sig * (1.0 - left_sig),
            right_grad * right_sig,
            right_grad * blocks[2] * right_sig * (1.0 - right_sig),
            grad_logit,
        ],
        axis=0,
    ).astype(jnp.bfloat16)
    grad_in = jnp.einsum("ep,de->pd", grad_proj, proj_weight, preferred_element_type=jnp.float32)
    grad_pair = norm_back(grad_in * in_gain, normed, scale_inv, -1)
    return grad_pair.astype(jnp.bfloat16).reshape(rows_here, cols_here, width)


def solution(mesh):
    n_row, n_ch = mesh.shape["row"], mesh.shape["ch"]
    placed = (P("row", "ch", None), P("row", "ch", None), P(), P(), P(), P(), P(), P())

    def on_device(*args):
        rows, cols, width = args[0].shape
        devices, outer, group = n_row * n_ch, math.isqrt(n_row), BLOCK // rows
        if (
            devices & (devices - 1) == 0
            and n_row >= 4
            and n_row % outer == 0
            and (devices // outer) % (2 * n_ch) == 0
            and outer % 2 == 0
            and width % (devices // 2) == 0
            and rows % (2 * PARTS) == 0
            and BLOCK % rows == 0
            and group % (width // (devices // 2)) == 0
            and width % (2 * group) == 0
            and cols % 128 == 0
            and width <= 256
            and width & (width - 1) == 0
        ):
            return by_channel(n_row, n_ch, *args)
        return by_row(*args)

    return jax.shard_map(
        on_device, mesh=mesh, in_specs=placed, out_specs=P("row", "ch", None), check_vma=False
    )
```

```python
import functools
import math

import jax
import jax.numpy as jnp
from jax import lax
from jax.experimental import pallas as pl
from jax.experimental.pallas import tpu as pltpu
from jax.sharding import PartitionSpec as P

EPSILON = 1e-05
F32 = jnp.float32
BF16 = jnp.bfloat16
UNROLL = 4
BLOCK = 256
PARTS = 4


def dot(a, b, da, db):
    return lax.dot_general(a, b, (((da,), (db,)), ((), ())), preferred_element_type=F32)


def sigmoid(values):
    return 0.5 * jnp.tanh(0.5 * values) + 0.5


def normalize(values, axis):
    center = jnp.mean(values, axis=axis, keepdims=True)
    shifted = values - center
    scale_inv = lax.rsqrt(jnp.mean(shifted * shifted, axis=axis, keepdims=True) + EPSILON)
    return (shifted * scale_inv, scale_inv)


def norm_back(grad_hat, normed, scale_inv, axis):
    first = jnp.mean(grad_hat, axis=axis, keepdims=True)
    second = jnp.mean(grad_hat * normed, axis=axis, keepdims=True)
    return scale_inv * (grad_hat - first - normed * second)


def column(row, width):
    return jnp.broadcast_to(row, (width, row.shape[-1])).T


def call(kernel, outs, scratch, *args, hbm=0, limit=16):
    single = not isinstance(outs, (list, tuple))
    args = [pltpu.with_memory_space_constraint(a, pltpu.HBM) if n < hbm else a for n, a in enumerate(args)]
    specs = [pl.BlockSpec(memory_space=pltpu.HBM if n < hbm else pltpu.VMEM) for n in range(len(args))]
    out_specs = [
        pl.BlockSpec(memory_space=getattr(out, "memory_space", pltpu.VMEM))
        for out in ([outs] if single else outs)
    ]
    return pl.pallas_call(
        kernel,
        out_shape=outs if single else tuple(outs),
        in_specs=specs,
        out_specs=out_specs[0] if single else tuple(out_specs),
        scratch_shapes=scratch,
        compiler_params=pltpu.CompilerParams(vmem_limit_bytes=limit * 1024 * 1024),
    )(*args)


def permutation(outer, inner):
    to = lax.broadcasted_iota(jnp.int32, (BLOCK, BLOCK), 0)
    start = lax.broadcasted_iota(jnp.int32, (BLOCK, BLOCK), 1)
    return (start == to % inner * outer + to // inner).astype(F32).astype(BF16)


def identity(size):
    first = lax.broadcasted_iota(jnp.int32, (size, size), 0)
    return (first == lax.broadcasted_iota(jnp.int32, (size, size), 1)).astype(F32).astype(BF16)


def swapped(swap, blocks):
    cols = blocks[0].shape[-1]
    wide = jnp.concatenate([block.reshape(BLOCK, cols) for block in blocks], axis=1)
    wide = dot(swap, wide, 1, 0).astype(BF16)
    return [wide[:, n * cols : (n + 1) * cols] for n in range(len(blocks))]


def fetched(sources, targets, sems):
    copies = [
        pltpu.make_async_copy(source, target, sems.at[n])
        for n, (source, target) in enumerate(zip(sources, targets))
    ]
    for copy in copies:
        copy.start()
    for copy in copies:
        copy.wait()


def weight_copies(w_hbm, w_ref, first, sems):
    width = w_hbm.shape[0]
    return [
        pltpu.make_async_copy(
            w_hbm.at[:, (first + n) * width : (first + n + 1) * width],
            w_ref.at[:, n * width : (n + 1) * width],
            sems.at[n],
        )
        for n in range(2)
    ]


def right_kernel(
    lay, x_hbm, gain_hbm, bias_hbm, w_hbm, r_hbm, n_ref, x_ref, gain_ref, bias_ref, w_ref, wt_ref, r_ref, right_ref, sems, out_sems
):
    rows, cols, width = x_ref.shape
    mine = width // lay.half
    parts = sems.shape[0] - 4
    size = rows // parts

    def fetch(p):
        here = pl.ds(p * size, size)
        return pltpu.make_async_copy(x_hbm.at[here], x_ref.at[here], sems.at[4 + p])

    small = [
        pltpu.make_async_copy(gain_hbm, gain_ref, sems.at[2]),
        pltpu.make_async_copy(bias_hbm, bias_ref, sems.at[3]),
    ]
    weights = weight_copies(w_hbm, w_ref, 2, sems)
    fetch(0).start()
    for copy in small + weights:
        copy.start()
    for p in range(1, parts):
        fetch(p).start()
    group = BLOCK // rows
    swap = permutation(group, rows)

    def normal(p):
        fetch(p).wait()
        for n in range(0, size, 2):
            i = p * size + n
            shifted = dot(center, x_ref[pl.ds(i, 2)].reshape(2 * cols, width), 1, 1)
            scale_inv = lax.rsqrt(jnp.mean(shifted * shifted, axis=0, keepdims=True) + EPSILON)
            n_ref[p * size // 2 + n // 2] = (shifted * scale_inv * gain + bias).astype(BF16)

    def project(p):
        for n in range(0, size, 2):
            i = p * size + n
            proj = dot(wt_ref[...], n_ref[p * size // 2 + n // 2], 1, 0)
            right = (sigmoid(proj[width:]) * proj[:width]).astype(BF16)
            for m in range(2):
                r_ref[i + m] = right[:, m * cols : (m + 1) * cols]

    def body(p, _):
        normal(p)
        project(p - 1)
        return 0

    center = (identity(width).astype(F32) - 1.0 / width).astype(BF16)
    for copy in small:
        copy.wait()
    gain = column(gain_ref[...], 2 * cols)
    bias = column(bias_ref[...], 2 * cols)
    normal(0)
    for copy in weights:
        copy.wait()
    wt_ref[...] = w_ref[...].astype(F32).T.astype(BF16)
    lax.fori_loop(1, parts, body, 0)
    project(parts - 1)
    out = []
    blocks = places(width, mine, rows)
    for k in range(0, len(blocks), 2):
        pair = blocks[k : k + 2]
        for (to, _here), right in zip(pair, swapped(swap, [r_ref[:, here] for _to, here in pair])):
            right_ref[to] = right.reshape(group // mine, mine, rows, cols)
            for share in range(to.start, to.stop):
                for n, device in enumerate(lay.order):
                    if device % lay.half == share:
                        out.append(pltpu.make_async_copy(right_ref.at[share], r_hbm.at[n], out_sems.at[n]))
                        out[-1].start()
    for copy in out:
        copy.wait()


def left_kernel(lay, w_hbm, n_ref, mine_out, mate_out, w_ref, wt_ref, l_ref, left_ref, sems):
    rows, width, cols = l_ref.shape
    mine = width // lay.half
    group = BLOCK // rows
    weights = weight_copies(w_hbm, w_ref, 0, sems)
    for copy in weights:
        copy.start()
    for copy in weights:
        copy.wait()
    wt_ref[...] = w_ref[...].astype(F32).T.astype(BF16)
    swap = permutation(group, rows)

    def body(n, _):
        proj = dot(wt_ref[...], n_ref[n], 1, 0)
        left = (sigmoid(proj[width:]) * proj[:width]).astype(BF16)
        for m in range(2):
            l_ref[2 * n + m] = left[:, m * cols : (m + 1) * cols]
        return 0

    lax.fori_loop(0, rows // 2, body, 0, unroll=2)
    blocks = places(width, mine, rows)
    for k in range(0, len(blocks), 2):
        pair = blocks[k : k + 2]
        for (to, _here), left in zip(pair, swapped(swap, [l_ref[:, here] for _to, here in pair])):
            left_ref[to] = left.reshape(group // mine, mine, rows, cols)
    for n, s in enumerate(lay.hops):
        mine_out[n] = left_ref[lay.other(s)]
        mate_out[n] = left_ref[lay.other(s ^ lay.mate)]


def gate_kernel(*refs):
    sources, (h_ref, fac_hbm, fac_ref, wt_ref), targets, (sems, out_sems) = (
        refs[:7],
        refs[7:11],
        refs[11:18],
        refs[18:],
    )
    x_ref, cot_ref, gain_ref, bias_ref, w_ref, ogain_ref, ow_ref = targets
    rows, cols, width = x_ref.shape
    fetched(sources, targets, sems)
    wt_ref[...] = w_ref[:, : 4 * width].astype(F32).T.astype(BF16)
    ogain = column(ogain_ref[...], cols)

    def body(i, _):
        normed, _s = normalize(x_ref[i].astype(F32), -1)
        normal_in = (normed * gain_ref[...] + bias_ref[...]).astype(BF16)
        proj = dot(wt_ref[...], normal_in, 1, 1)
        for side in range(2):
            val = proj[2 * side * width : (2 * side + 1) * width]
            sig = sigmoid(proj[(2 * side + 1) * width : (2 * side + 2) * width])
            fac_ref[i, 2 * side * width : (2 * side + 1) * width] = sig.astype(BF16)
            fac_ref[i, (2 * side + 1) * width : (2 * side + 2) * width] = (
                val * sig * (1.0 - sig)
            ).astype(BF16)
        out_gate = sigmoid(dot(normal_in, w_ref[:, 4 * width :], 1, 0))
        grad_mixed = (cot_ref[i].astype(F32) * out_gate).astype(BF16)
        h_ref[i] = dot(ow_ref[...], grad_mixed, 1, 1) * ogain
        return 0

    size = rows // PARTS

    def send(p):
        here = pl.ds(p * size, size)
        return pltpu.make_async_copy(fac_ref.at[here], fac_hbm.at[here], out_sems.at[p])

    def part(p, _):
        for n in range(size):
            body(p * size + n, 0)
        send(p).start()
        return 0

    lax.fori_loop(0, PARTS, part, 0)
    for p in range(PARTS):
        send(p).wait()


def places(n_channels, mine, rows):
    group = BLOCK // rows
    return [
        (slice(c // mine, (c + group) // mine), slice(c, c + group)) for c in range(0, n_channels, group)
    ]


def to_rows(lay, t_ref, ts_ref):
    rows, width, cols = ts_ref.shape
    mine = t_ref.shape[1]
    group = BLOCK // rows
    swap = permutation(rows, group)
    blocks = places(width, mine, rows)
    for n in range(0, len(blocks), 2):
        pair = blocks[n : n + 2]
        for (_to, here), block in zip(pair, swapped(swap, [lay.shares(t_ref, to) for to, _here in pair])):
            ts_ref[:, here] = block.reshape(rows, group, cols)


def tri_back_kernel(lay, t_ref, h_ref, gt_ref, ts_ref, gs_ref):
    rows, width, cols = h_ref.shape
    mine = t_ref.shape[1]
    group = BLOCK // rows
    back = permutation(group, rows)
    to_rows(lay, t_ref, ts_ref)

    def body(i, _):
        tri, h = ts_ref[i].astype(F32), h_ref[i]
        shifted = tri - jnp.mean(tri, axis=0, keepdims=True)
        first = jnp.mean(h, axis=0, keepdims=True)
        both = jnp.mean(h * shifted, axis=0, keepdims=True)
        tri_inv = lax.rsqrt(jnp.mean(shifted * shifted, axis=0, keepdims=True) + EPSILON)
        gs_ref[i] = (tri_inv * (h - first - shifted * (both * tri_inv * tri_inv))).astype(BF16)
        return 0

    lax.fori_loop(0, rows, body, 0, unroll=2 * UNROLL)
    blocks = places(width, mine, rows)
    for n in range(0, len(blocks), 2):
        pair = blocks[n : n + 2]
        for (to, _here), block in zip(pair, swapped(back, [gs_ref[:, here] for _to, here in pair])):
            block = block.reshape(group // mine, mine, rows, cols)
            for share in range(to.start, to.stop):
                gt_ref[lay.inside.index(share)] = block[share - to.start]


def logit_kernel(lay, *refs):
    (fac_hbm, *sources), t_ref, refs = refs[:9], refs[9], refs[10:]
    (gin0_ref, nt0_ref, fac0_ref, gin_hbm, nt_hbm, s_ref), refs = refs[:6], refs[6:]
    (ts_ref, gin_ref, nt_ref, out_sems), targets, sems = refs[:4], refs[4:12], refs[12]
    x_ref, cot_ref, gain_ref, bias_ref, w_ref, ogain_ref, obias_ref, ow_ref = targets
    rows, cols, width = x_ref.shape
    first = pl.ds(0, nt0_ref.shape[0])
    fetched([*sources, fac_hbm.at[first]], [*targets, fac0_ref], sems)
    to_rows(lay, t_ref, ts_ref)
    ogain = column(ogain_ref[...], cols)
    obias = column(obias_ref[...], cols)

    def body(i, _):
        normed, scale_inv = normalize(x_ref[i].astype(F32), -1)
        normal_in = (normed * gain_ref[...] + bias_ref[...]).astype(BF16)
        out_gate = sigmoid(dot(normal_in, w_ref[:, 4 * width :], 1, 0))
        tri_hat, _s = normalize(ts_ref[i].astype(F32), 0)
        normal_out = (tri_hat * ogain + obias).astype(BF16)
        mixed = dot(normal_out, ow_ref[...], 0, 0)
        grad_logit = cot_ref[i].astype(F32) * mixed * out_gate * (1.0 - out_gate)
        gin_ref[i] = dot(w_ref[:, 4 * width :], grad_logit.astype(BF16), 1, 1).astype(BF16)
        nt_ref[i] = normed.T.astype(BF16)
        s_ref[pl.ds(i, 1), :] = jnp.broadcast_to(scale_inv, (cols, width)).T[:1]
        return 0

    lax.fori_loop(0, rows, body, 0, unroll=UNROLL)
    gin0_ref[...] = gin_ref[first]
    nt0_ref[...] = nt_ref[first]
    copies = [
        pltpu.make_async_copy(gin_ref, gin_hbm, out_sems.at[0]),
        pltpu.make_async_copy(nt_ref, nt_hbm, out_sems.at[1]),
    ]
    for copy in copies:
        copy.start()
    for copy in copies:
        copy.wait()


def pair_kernel(
    lay, fac_hbm, nt_hbm, gin_hbm, fac0_ref, nt0_ref, gin0_ref, r_ref, s_ref, gain_ref, w_ref, *refs
):
    l_refs, refs = refs[: lay.n_hops], refs[lay.n_hops :]
    out_hbm, l_ref, ls_ref, rs_ref, fac_ref, nt_ref, gin_ref, out_ref, sems, out_sems = refs
    rows, cols, width = out_ref.shape
    mine = width // lay.half
    parts = sems.shape[1]
    size = rows // parts

    def fetch(p):
        here = pl.ds(p * size, size)
        return [
            pltpu.make_async_copy(fac_hbm.at[here], fac_ref.at[here], sems.at[0, p]),
            pltpu.make_async_copy(nt_hbm.at[here], nt_ref.at[here], sems.at[1, p]),
            pltpu.make_async_copy(gin_hbm.at[here], gin_ref.at[here], sems.at[2, p]),
        ]

    def send(n):
        here = pl.ds(2 * n, 2)
        return pltpu.make_async_copy(out_ref.at[here], out_hbm.at[here], out_sems.at[n])

    for p in range(1, parts):
        for copy in fetch(p):
            copy.start()
    gain = column(gain_ref[...], cols)
    eye = identity(cols)
    group = BLOCK // rows
    swap = permutation(rows, group)
    for s, source in lay.received(l_refs):
        l_ref[lay.other(s)] = source[...]
    for to, here in places(width, mine, rows):
        sums = []
        for share in range(to.start, to.stop):
            one, two = (
                r_ref[n]
                for n, device in enumerate(lay.order)
                if device % lay.half == share
            )
            sums.append(one + two)
        left, right = swapped(swap, [l_ref[to], jnp.stack(sums)])
        ls_ref[:, here] = left.reshape(rows, group, cols)
        rs_ref[:, here] = right.reshape(rows, group, cols)

    def part(p, fac_here, nt_here, gin_here):
        for n in range(0, size, 2):
            i = p * size + n
            blocks = []
            for m in range(2):
                left, right, fac = ls_ref[i + m], rs_ref[i + m], fac_here[i + m]
                blocks.append(
                    jnp.concatenate(
                        [
                            left * fac[:width],
                            left * fac[width : 2 * width],
                            right * fac[2 * width : 3 * width],
                            right * fac[3 * width :],
                        ],
                        axis=0,
                    )
                )
            grad_in = dot(w_ref[:, : 4 * width], jnp.concatenate(blocks, axis=1), 1, 0)
            for m in range(2):
                grad = (grad_in[:, m * cols : (m + 1) * cols] + gin_here[i + m].astype(F32)) * gain
                scale_inv = s_ref[pl.ds(i + m, 1), :]
                normed = nt_here[i + m].astype(F32)
                result = norm_back(grad, normed, scale_inv, 0).astype(BF16)
                out_ref[i + m] = dot(eye, result, 1, 1).astype(BF16)
            send(i // 2).start()

    part(0, fac0_ref, nt0_ref, gin0_ref)
    for p in range(1, parts):
        for copy in fetch(p):
            copy.wait()
    for p in range(1, parts):
        part(p, fac_ref, nt_ref, gin_ref)
    for n in range(rows // 2):
        send(n).wait()


class Layout:
    def __init__(self, n_row, n_ch):
        self.n_row, self.n_ch = n_row, n_ch
        self.devices = n_row * n_ch
        self.half = self.devices // 2
        outer = math.isqrt(n_row)
        self.inner = self.devices // outer
        near = [
            2 * n_ch * far + n_ch * core + b
            for b in range(n_ch)
            for far in range(self.inner // (2 * n_ch))
            for core in range(2)
        ]
        self.order = [o * self.inner + n for n in near for o in range(outer)]
        self.inside = [o * self.inner + n for n in near for o in range(outer // 2)]
        self.mate = n_ch
        self.hops = [s for s in range(self.half) if s & self.mate == 0]
        self.hops[3:] = self.hops[:2:-1]
        self.n_hops = len(self.hops) + 1
        self.all_place = self.place(self.order, n_row)
        self.half_place = self.place(self.inside, n_row // 2)
        self.near_place = self.place(list(range(self.half)), n_row // 2)

    def place(self, order, n_row):
        return [[order.index(r * self.n_ch + b) for b in range(self.n_ch)] for r in range(n_row)]

    def shares(self, ref, here):
        return jnp.stack([ref[self.inside.index(share)] for share in range(here.start, here.stop)])

    def other(self, s):
        me = lax.axis_index("row") * self.n_ch + lax.axis_index("ch")
        return jnp.bitwise_xor(lax.rem(me, self.half), s)

    def exchange_all(self, blocks):
        return lax.all_to_all(
            blocks, ("row", "ch"), split_axis=0, concat_axis=0, tiled=True, axis_index_groups=[self.order]
        )

    def exchange_half(self, blocks):
        groups = [[first + n for n in self.inside] for first in (0, self.half)]
        return lax.all_to_all(
            blocks, ("row", "ch"), split_axis=0, concat_axis=0, tiled=True, axis_index_groups=groups
        )

    def swap(self, block, s):
        return lax.ppermute(block, ("row", "ch"), [(n, n ^ s) for n in range(self.devices)])

    def permute(self, mine, mates):
        mates = self.swap(mates, self.mate)
        shape = jax.ShapeDtypeStruct((2,) + mine.shape[1:], mine.dtype)
        pairs = call(merge_kernel, [shape] * (len(self.hops) - 1), [], mine, mates)
        return [mine, mates] + [self.swap(pair, s) for pair, s in zip(pairs, self.hops[1:])]

    def received(self, refs):
        mine, mates, *pairs = refs
        found = [(0, mine.at[0]), (self.mate, mates.at[0])]
        for s, pair in zip(self.hops[1:], pairs):
            found += [(s, pair.at[0]), (s ^ self.mate, pair.at[1])]
        return found


def merge_kernel(mine_ref, mates_ref, *outs):
    for n, out_ref in enumerate(outs, 1):
        out_ref[0] = mine_ref[n]
        out_ref[1] = mates_ref[n]


def plane(ref, place, c):
    return jnp.concatenate(
        [
            jnp.concatenate([ref[n, c] for n in column_of], axis=0)
            for column_of in zip(*place)
        ],
        axis=1,
    )


def store_plane(ref, place, c, value):
    rows, cols = ref.shape[-2:]
    for r, row_of in enumerate(place):
        for b, n in enumerate(row_of):
            ref[n, c] = value[r * rows : (r + 1) * rows, b * cols : (b + 1) * cols]


def tri_kernel(lay, r_ref, *refs):
    l_refs, (t_ref, l_ref) = refs[: lay.n_hops], refs[lay.n_hops :]
    for s, source in lay.received(l_refs):
        l_ref[lay.other(s)] = source[...]
    for c in range(t_ref.shape[1]):
        tri = dot(plane(l_ref, lay.near_place, c), plane(r_ref, lay.all_place, c), 1, 1)
        store_plane(t_ref, lay.half_place, c, tri.astype(BF16))


def factor_back_kernel(lay, gt_ref, l_ref, r_ref, gr_hbm, *refs):
    mine_out, mate_out, gl_ref, gr_ref, sems = refs
    copies = []
    for c in range(gt_ref.shape[1]):
        right = dot(plane(gt_ref, lay.half_place, c), plane(l_ref, lay.near_place, c), 0, 0)
        store_plane(gr_ref, lay.all_place, c, right.astype(BF16))
        here = (slice(None), c)
        copies.append(pltpu.make_async_copy(gr_ref.at[here], gr_hbm.at[here], sems.at[c]))
        copies[-1].start()
    for c in range(gt_ref.shape[1]):
        left = dot(plane(gt_ref, lay.half_place, c), plane(r_ref, lay.all_place, c), 1, 0)
        store_plane(gl_ref, lay.near_place, c, left.astype(BF16))
    for n, s in enumerate(lay.hops):
        mine_out[n] = gl_ref[lay.other(s)]
        mate_out[n] = gl_ref[lay.other(s ^ lay.mate)]
    for copy in copies:
        copy.wait()


def by_channel(
    n_row, n_ch, pair_act, cotangent, in_gain, in_bias, proj_weight, out_gain, out_bias, out_weight
):
    lay = Layout(n_row, n_ch)
    rows, cols, width = pair_act.shape
    mine = width // lay.half
    struct = jax.ShapeDtypeStruct
    half = pltpu.VMEM((rows, width, cols), BF16)
    weight_t = pltpu.VMEM((4 * width, width), BF16)
    in_gain, in_bias, out_gain, out_bias = (
        v.reshape(1, width) for v in (in_gain, in_bias, out_gain, out_bias)
    )

    some = struct((len(lay.hops), mine, rows, cols), BF16)
    one = struct((lay.half, mine, rows, cols), BF16)
    one_here = pltpu.VMEM(one.shape, BF16)
    two_shape = (lay.devices, mine, rows, cols)
    row = pltpu.VMEM((1, width), F32)
    weight = pltpu.VMEM(proj_weight.shape, BF16)
    out_weight_here = pltpu.VMEM((width, width), BF16)
    both_weights = pltpu.VMEM((width, 2 * width), BF16)
    both_turned = pltpu.VMEM((2 * width, width), BF16)
    right, normal_in = call(
        functools.partial(right_kernel, lay),
        [pltpu.HBM(two_shape, BF16), struct((rows // 2, width, 2 * cols), BF16)],
        [
            half,
            row,
            row,
            both_weights,
            both_turned,
            half,
            one_here,
            pltpu.SemaphoreType.DMA((4 + PARTS // 2,)),
            pltpu.SemaphoreType.DMA((lay.devices,)),
        ],
        pair_act,
        in_gain,
        in_bias,
        proj_weight,
        hbm=4,
    )
    left = call(
        functools.partial(left_kernel, lay),
        [some, some],
        [both_weights, both_turned, half, one_here, pltpu.SemaphoreType.DMA((2,))],
        proj_weight,
        normal_in,
        hbm=1,
    )
    right = lay.exchange_all(right)
    left = lay.permute(*left)
    h, fac = call(
        gate_kernel,
        [pltpu.VMEM((rows, width, cols), F32), pltpu.HBM((rows, 4 * width, cols), BF16)],
        [
            pltpu.VMEM((rows, 4 * width, cols), BF16),
            weight_t,
            half,
            half,
            row,
            row,
            weight,
            row,
            out_weight_here,
            pltpu.SemaphoreType.DMA((7,)),
            pltpu.SemaphoreType.DMA((PARTS,)),
        ],
        pair_act,
        cotangent,
        in_gain,
        in_bias,
        proj_weight,
        out_gain,
        out_weight,
        hbm=7,
    )
    right, h, fac = lax.optimization_barrier((right, h, fac))
    tri, left = call(functools.partial(tri_kernel, lay), [one, one], [], right, *left)
    tri = lay.exchange_half(tri)
    grad_tri = call(functools.partial(tri_back_kernel, lay), one, [half, half], tri, h)
    grad_right, *grad_left = call(
        functools.partial(factor_back_kernel, lay),
        [pltpu.HBM(two_shape, BF16), some, some],
        [one_here, pltpu.VMEM(two_shape, BF16), pltpu.SemaphoreType.DMA((mine,))],
        lay.exchange_half(grad_tri),
        left,
        right,
    )
    grad_right = lay.exchange_all(grad_right)
    grad_left = lay.permute(*grad_left)
    grad_in_first, normed_first, fac_first, grad_in, normed_t, scale = call(
        functools.partial(logit_kernel, lay),
        [
            pltpu.VMEM((rows // PARTS, width, cols), BF16),
            pltpu.VMEM((rows // PARTS, width, cols), BF16),
            pltpu.VMEM((rows // PARTS, 4 * width, cols), BF16),
            pltpu.HBM((rows, width, cols), BF16),
            pltpu.HBM((rows, width, cols), BF16),
            pltpu.VMEM((rows, cols), F32),
        ],
        [
            half,
            half,
            half,
            pltpu.SemaphoreType.DMA((2,)),
            half,
            half,
            row,
            row,
            weight,
            row,
            row,
            out_weight_here,
            pltpu.SemaphoreType.DMA((9,)),
        ],
        fac,
        pair_act,
        cotangent,
        in_gain,
        in_bias,
        proj_weight,
        out_gain,
        out_bias,
        out_weight,
        tri,
        hbm=9,
    )
    return call(
        functools.partial(pair_kernel, lay),
        pltpu.HBM((rows, cols, width), BF16),
        [
            one_here,
            half,
            half,
            pltpu.VMEM((rows, 4 * width, cols), BF16),
            half,
            half,
            half,
            pltpu.SemaphoreType.DMA((3, PARTS)),
            pltpu.SemaphoreType.DMA((rows // 2,)),
        ],
        fac,
        normed_t,
        grad_in,
        fac_first,
        normed_first,
        grad_in_first,
        grad_right,
        scale,
        in_gain,
        proj_weight,
        *grad_left,
        hbm=3,
    )


def by_row(
    pair_act, cotangent, in_gain, in_bias, proj_weight, out_gain, out_bias, out_weight
):
    rows_here, cols_here, width = pair_act.shape
    flat = pair_act.astype(jnp.float32).reshape(rows_here * cols_here, width)
    normed, scale_inv = normalize(flat, -1)
    normal_in = (normed * in_gain + in_bias).astype(jnp.bfloat16)
    projected = jnp.einsum("pd,de->ep", normal_in, proj_weight, preferred_element_type=jnp.float32)
    blocks = jnp.split(projected, 5, axis=0)
    left_sig = jax.nn.sigmoid(blocks[1])
    right_sig = jax.nn.sigmoid(blocks[3])
    left_fac = (left_sig * blocks[0]).astype(jnp.bfloat16).reshape(width, rows_here, cols_here)
    right_fac = (right_sig * blocks[2]).astype(jnp.bfloat16).reshape(width, rows_here, cols_here)
    left_chan, right_chan = (
        lax.all_to_all(left_fac, "ch", split_axis=0, concat_axis=2, tiled=True),
        lax.all_to_all(right_fac, "ch", split_axis=0, concat_axis=2, tiled=True),
    )
    tri_chan = jnp.einsum(
        "cik,cjk->cij",
        left_chan,
        lax.all_gather(right_chan, "row", axis=1, tiled=True),
        preferred_element_type=jnp.float32,
    ).astype(jnp.bfloat16)
    tri_back = lax.all_to_all(tri_chan, "ch", split_axis=2, concat_axis=0, tiled=True)
    tri_hat, tri_inv = normalize(tri_back.astype(jnp.float32).reshape(width, -1), 0)
    normal_out = (tri_hat * out_gain[:, None] + out_bias[:, None]).astype(jnp.bfloat16)
    mixed = jnp.einsum("cp,ce->ep", normal_out, out_weight, preferred_element_type=jnp.float32)
    out_gate = jax.nn.sigmoid(blocks[4])
    grad_out = cotangent.astype(jnp.float32).reshape(rows_here * cols_here, width).T
    grad_mixed = (grad_out * out_gate).astype(jnp.bfloat16)
    grad_logit = grad_out * mixed * out_gate * (1.0 - out_gate)
    grad_normal = jnp.einsum(
        "ep,ce->cp", grad_mixed, out_weight, preferred_element_type=jnp.float32
    )
    grad_tri = norm_back(grad_normal * out_gain[:, None], tri_hat, tri_inv, 0)
    grad_tri = grad_tri.astype(jnp.bfloat16).reshape(width, rows_here, cols_here)
    grad_chan = lax.all_to_all(grad_tri, "ch", split_axis=0, concat_axis=2, tiled=True)
    grad_cols = lax.all_to_all(grad_chan, "row", split_axis=2, concat_axis=1, tiled=True)
    grad_left = jnp.einsum(
        "cij,cjk->cik",
        grad_chan,
        lax.all_gather(right_chan, "row", axis=1, tiled=True),
        preferred_element_type=jnp.float32,
    )
    grad_right = jnp.einsum(
        "cij,cik->cjk",
        grad_cols,
        lax.all_gather(left_chan, "row", axis=1, tiled=True),
        preferred_element_type=jnp.float32,
    )
    left_back, right_back = (
        lax.all_to_all(
            grad_left.astype(jnp.bfloat16), "ch", split_axis=2, concat_axis=0, tiled=True
        ),
        lax.all_to_all(
            grad_right.astype(jnp.bfloat16), "ch", split_axis=2, concat_axis=0, tiled=True
        ),
    )
    left_grad = left_back.astype(jnp.float32).reshape(width, -1)
    right_grad = right_back.astype(jnp.float32).reshape(width, -1)
    grad_proj = jnp.concatenate(
        [
            left_grad * left_sig,
            left_grad * blocks[0] * left_sig * (1.0 - left_sig),
            right_grad * right_sig,
            right_grad * blocks[2] * right_sig * (1.0 - right_sig),
            grad_logit,
        ],
        axis=0,
    ).astype(jnp.bfloat16)
    grad_in = jnp.einsum("ep,de->pd", grad_proj, proj_weight, preferred_element_type=jnp.float32)
    grad_pair = norm_back(grad_in * in_gain, normed, scale_inv, -1)
    return grad_pair.astype(jnp.bfloat16).reshape(rows_here, cols_here, width)


def solution(mesh):
    n_row, n_ch = mesh.shape["row"], mesh.shape["ch"]
    placed = (P("row", "ch", None), P("row", "ch", None), P(), P(), P(), P(), P(), P())

    def on_device(*args):
        rows, cols, width = args[0].shape
        devices, outer, group = n_row * n_ch, math.isqrt(n_row), BLOCK // rows
        if (
            devices & (devices - 1) == 0
            and n_row >= 4
            and n_row % outer == 0
            and (devices // outer) % (2 * n_ch) == 0
            and outer % 2 == 0
            and width % (devices // 2) == 0
            and rows % (2 * PARTS) == 0
            and BLOCK % rows == 0
            and group % (width // (devices // 2)) == 0
            and width % (2 * group) == 0
            and cols % 128 == 0
            and width <= 256
            and width & (width - 1) == 0
        ):
            return by_channel(n_row, n_ch, *args)
        return by_row(*args)

    return jax.shard_map(
        on_device, mesh=mesh, in_specs=placed, out_specs=P("row", "ch", None), check_vma=False
    )
```

```python
import functools
import math

import jax
import jax.numpy as jnp
from jax import lax
from jax.experimental import pallas as pl
from jax.experimental.pallas import tpu as pltpu
from jax.sharding import PartitionSpec as P

EPSILON = 1e-05
F32 = jnp.float32
BF16 = jnp.bfloat16
UNROLL = 4
BLOCK = 256
PARTS = 4


def dot(a, b, da, db):
    return lax.dot_general(a, b, (((da,), (db,)), ((), ())), preferred_element_type=F32)


def sigmoid(values):
    return 0.5 * jnp.tanh(0.5 * values) + 0.5


def normalize(values, axis):
    center = jnp.mean(values, axis=axis, keepdims=True)
    shifted = values - center
    scale_inv = lax.rsqrt(jnp.mean(shifted * shifted, axis=axis, keepdims=True) + EPSILON)
    return (shifted * scale_inv, scale_inv)


def norm_back(grad_hat, normed, scale_inv, axis):
    first = jnp.mean(grad_hat, axis=axis, keepdims=True)
    second = jnp.mean(grad_hat * normed, axis=axis, keepdims=True)
    return scale_inv * (grad_hat - first - normed * second)


def column(row, width):
    return jnp.broadcast_to(row, (width, row.shape[-1])).T


def call(kernel, outs, scratch, *args, hbm=0, limit=16):
    single = not isinstance(outs, (list, tuple))
    args = [pltpu.with_memory_space_constraint(a, pltpu.HBM) if n < hbm else a for n, a in enumerate(args)]
    specs = [pl.BlockSpec(memory_space=pltpu.HBM if n < hbm else pltpu.VMEM) for n in range(len(args))]
    out_specs = [
        pl.BlockSpec(memory_space=getattr(out, "memory_space", pltpu.VMEM))
        for out in ([outs] if single else outs)
    ]
    return pl.pallas_call(
        kernel,
        out_shape=outs if single else tuple(outs),
        in_specs=specs,
        out_specs=out_specs[0] if single else tuple(out_specs),
        scratch_shapes=scratch,
        compiler_params=pltpu.CompilerParams(vmem_limit_bytes=limit * 1024 * 1024),
    )(*args)


def permutation(outer, inner):
    to = lax.broadcasted_iota(jnp.int32, (BLOCK, BLOCK), 0)
    start = lax.broadcasted_iota(jnp.int32, (BLOCK, BLOCK), 1)
    return (start == to % inner * outer + to // inner).astype(F32).astype(BF16)


def identity(size):
    first = lax.broadcasted_iota(jnp.int32, (size, size), 0)
    return (first == lax.broadcasted_iota(jnp.int32, (size, size), 1)).astype(F32).astype(BF16)


def swapped(swap, blocks):
    cols = blocks[0].shape[-1]
    wide = jnp.concatenate([block.reshape(BLOCK, cols) for block in blocks], axis=1)
    wide = dot(swap, wide, 1, 0).astype(BF16)
    return [wide[:, n * cols : (n + 1) * cols] for n in range(len(blocks))]


def fetched(sources, targets, sems):
    copies = [
        pltpu.make_async_copy(source, target, sems.at[n])
        for n, (source, target) in enumerate(zip(sources, targets))
    ]
    for copy in copies:
        copy.start()
    for copy in copies:
        copy.wait()


def weight_copies(w_hbm, w_ref, first, sems):
    width = w_hbm.shape[0]
    return [
        pltpu.make_async_copy(
            w_hbm.at[:, (first + n) * width : (first + n + 1) * width],
            w_ref.at[:, n * width : (n + 1) * width],
            sems.at[n],
        )
        for n in range(2)
    ]


def right_kernel(
    lay, x_hbm, gain_hbm, bias_hbm, w_hbm, r_hbm, n_ref, x_ref, gain_ref, bias_ref, w_ref, wt_ref, r_ref, right_ref, sems, out_sems
):
    rows, cols, width = x_ref.shape
    mine = width // lay.half
    parts = sems.shape[0] - 4
    size = rows // parts

    def fetch(p):
        here = pl.ds(p * size, size)
        return pltpu.make_async_copy(x_hbm.at[here], x_ref.at[here], sems.at[4 + p])

    small = [
        pltpu.make_async_copy(gain_hbm, gain_ref, sems.at[2]),
        pltpu.make_async_copy(bias_hbm, bias_ref, sems.at[3]),
    ]
    weights = weight_copies(w_hbm, w_ref, 2, sems)
    fetch(0).start()
    for copy in small + weights:
        copy.start()
    for p in range(1, parts):
        fetch(p).start()
    group = BLOCK // rows
    swap = permutation(group, rows)

    def normal(p):
        fetch(p).wait()
        for n in range(0, size, 2):
            i = p * size + n
            shifted = dot(center, x_ref[pl.ds(i, 2)].reshape(2 * cols, width), 1, 1)
            scale_inv = lax.rsqrt(jnp.mean(shifted * shifted, axis=0, keepdims=True) + EPSILON)
            n_ref[p * size // 2 + n // 2] = (shifted * scale_inv * gain + bias).astype(BF16)

    def project(p):
        for n in range(0, size, 2):
            i = p * size + n
            proj = dot(wt_ref[...], n_ref[p * size // 2 + n // 2], 1, 0)
            right = (sigmoid(proj[width:]) * proj[:width]).astype(BF16)
            for m in range(2):
                r_ref[i + m] = right[:, m * cols : (m + 1) * cols]

    def body(p, _):
        normal(p)
        project(p - 1)
        return 0

    center = (identity(width).astype(F32) - 1.0 / width).astype(BF16)
    for copy in small:
        copy.wait()
    gain = column(gain_ref[...], 2 * cols)
    bias = column(bias_ref[...], 2 * cols)
    normal(0)
    for copy in weights:
        copy.wait()
    wt_ref[...] = w_ref[...].astype(F32).T.astype(BF16)
    lax.fori_loop(1, parts, body, 0)
    project(parts - 1)
    out = []
    blocks = places(width, mine, rows)
    for k in range(0, len(blocks), 2):
        pair = blocks[k : k + 2]
        for (to, _here), right in zip(pair, swapped(swap, [r_ref[:, here] for _to, here in pair])):
            right_ref[to] = right.reshape(group // mine, mine, rows, cols)
            for share in range(to.start, to.stop):
                for n, device in enumerate(lay.order):
                    if device % lay.half == share:
                        out.append(pltpu.make_async_copy(right_ref.at[share], r_hbm.at[n], out_sems.at[n]))
                        out[-1].start()
    for copy in out:
        copy.wait()


def left_kernel(lay, w_hbm, n_ref, mine_out, mate_out, w_ref, wt_ref, l_ref, left_ref, sems):
    rows, width, cols = l_ref.shape
    mine = width // lay.half
    group = BLOCK // rows
    weights = weight_copies(w_hbm, w_ref, 0, sems)
    for copy in weights:
        copy.start()
    for copy in weights:
        copy.wait()
    wt_ref[...] = w_ref[...].astype(F32).T.astype(BF16)
    swap = permutation(group, rows)

    def body(n, _):
        proj = dot(wt_ref[...], n_ref[n], 1, 0)
        left = (sigmoid(proj[width:]) * proj[:width]).astype(BF16)
        for m in range(2):
            l_ref[2 * n + m] = left[:, m * cols : (m + 1) * cols]
        return 0

    lax.fori_loop(0, rows // 2, body, 0, unroll=2)
    blocks = places(width, mine, rows)
    for k in range(0, len(blocks), 2):
        pair = blocks[k : k + 2]
        for (to, _here), left in zip(pair, swapped(swap, [l_ref[:, here] for _to, here in pair])):
            left_ref[to] = left.reshape(group // mine, mine, rows, cols)
    for n, s in enumerate(lay.hops):
        mine_out[n] = left_ref[lay.other(s)]
        mate_out[n] = left_ref[lay.other(s ^ lay.mate)]


def gate_kernel(*refs):
    sources, (h_ref, fac_hbm, fac_ref, wt_ref), targets, (sems, out_sems) = (
        refs[:7],
        refs[7:11],
        refs[11:18],
        refs[18:],
    )
    x_ref, cot_ref, gain_ref, bias_ref, w_ref, ogain_ref, ow_ref = targets
    rows, cols, width = x_ref.shape
    fetched(sources, targets, sems)
    wt_ref[...] = w_ref[:, : 4 * width].astype(F32).T.astype(BF16)
    ogain = column(ogain_ref[...], cols)

    def body(i, _):
        normed, _s = normalize(x_ref[i].astype(F32), -1)
        normal_in = (normed * gain_ref[...] + bias_ref[...]).astype(BF16)
        proj = dot(wt_ref[...], normal_in, 1, 1)
        for side in range(2):
            val = proj[2 * side * width : (2 * side + 1) * width]
            sig = sigmoid(proj[(2 * side + 1) * width : (2 * side + 2) * width])
            fac_ref[i, 2 * side * width : (2 * side + 1) * width] = sig.astype(BF16)
            fac_ref[i, (2 * side + 1) * width : (2 * side + 2) * width] = (
                val * sig * (1.0 - sig)
            ).astype(BF16)
        out_gate = sigmoid(dot(normal_in, w_ref[:, 4 * width :], 1, 0))
        grad_mixed = (cot_ref[i].astype(F32) * out_gate).astype(BF16)
        h_ref[i] = dot(ow_ref[...], grad_mixed, 1, 1) * ogain
        return 0

    size = rows // PARTS

    def send(p):
        here = pl.ds(p * size, size)
        return pltpu.make_async_copy(fac_ref.at[here], fac_hbm.at[here], out_sems.at[p])

    def part(p, _):
        for n in range(size):
            body(p * size + n, 0)
        send(p).start()
        return 0

    lax.fori_loop(0, PARTS, part, 0)
    for p in range(PARTS):
        send(p).wait()


def places(n_channels, mine, rows):
    group = BLOCK // rows
    return [
        (slice(c // mine, (c + group) // mine), slice(c, c + group)) for c in range(0, n_channels, group)
    ]


def to_rows(lay, t_ref, ts_ref):
    rows, width, cols = ts_ref.shape
    mine = t_ref.shape[1]
    group = BLOCK // rows
    swap = permutation(rows, group)
    blocks = places(width, mine, rows)
    for n in range(0, len(blocks), 2):
        pair = blocks[n : n + 2]
        for (_to, here), block in zip(pair, swapped(swap, [lay.shares(t_ref, to) for to, _here in pair])):
            ts_ref[:, here] = block.reshape(rows, group, cols)


def tri_back_kernel(lay, t_ref, h_ref, gt_ref, ts_ref, gs_ref):
    rows, width, cols = h_ref.shape
    mine = t_ref.shape[1]
    group = BLOCK // rows
    back = permutation(group, rows)
    to_rows(lay, t_ref, ts_ref)

    def body(i, _):
        tri, h = ts_ref[i].astype(F32), h_ref[i]
        shifted = tri - jnp.mean(tri, axis=0, keepdims=True)
        first = jnp.mean(h, axis=0, keepdims=True)
        both = jnp.mean(h * shifted, axis=0, keepdims=True)
        tri_inv = lax.rsqrt(jnp.mean(shifted * shifted, axis=0, keepdims=True) + EPSILON)
        gs_ref[i] = (tri_inv * (h - first - shifted * (both * tri_inv * tri_inv))).astype(BF16)
        return 0

    lax.fori_loop(0, rows, body, 0, unroll=2 * UNROLL)
    blocks = places(width, mine, rows)
    for n in range(0, len(blocks), 2):
        pair = blocks[n : n + 2]
        for (to, _here), block in zip(pair, swapped(back, [gs_ref[:, here] for _to, here in pair])):
            block = block.reshape(group // mine, mine, rows, cols)
            for share in range(to.start, to.stop):
                gt_ref[lay.inside.index(share)] = block[share - to.start]


def logit_kernel(lay, *refs):
    (fac_hbm, *sources), t_ref, refs = refs[:9], refs[9], refs[10:]
    (gin0_ref, nt0_ref, fac0_ref, gin_hbm, nt_hbm, s_ref), refs = refs[:6], refs[6:]
    (ts_ref, gin_ref, nt_ref, out_sems), targets, sems = refs[:4], refs[4:12], refs[12]
    x_ref, cot_ref, gain_ref, bias_ref, w_ref, ogain_ref, obias_ref, ow_ref = targets
    rows, cols, width = x_ref.shape
    first = pl.ds(0, nt0_ref.shape[0])
    fetched([*sources, fac_hbm.at[first]], [*targets, fac0_ref], sems)
    to_rows(lay, t_ref, ts_ref)
    ogain = column(ogain_ref[...], cols)
    obias = column(obias_ref[...], cols)

    def body(i, _):
        normed, scale_inv = normalize(x_ref[i].astype(F32), -1)
        normal_in = (normed * gain_ref[...] + bias_ref[...]).astype(BF16)
        out_gate = sigmoid(dot(normal_in, w_ref[:, 4 * width :], 1, 0))
        tri_hat, _s = normalize(ts_ref[i].astype(F32), 0)
        normal_out = (tri_hat * ogain + obias).astype(BF16)
        mixed = dot(normal_out, ow_ref[...], 0, 0)
        grad_logit = cot_ref[i].astype(F32) * mixed * out_gate * (1.0 - out_gate)
        gin_ref[i] = dot(w_ref[:, 4 * width :], grad_logit.astype(BF16), 1, 1).astype(BF16)
        nt_ref[i] = normed.T.astype(BF16)
        s_ref[pl.ds(i, 1), :] = jnp.broadcast_to(scale_inv, (cols, width)).T[:1]
        return 0

    lax.fori_loop(0, rows, body, 0, unroll=UNROLL)
    gin0_ref[...] = gin_ref[first]
    nt0_ref[...] = nt_ref[first]
    copies = [
        pltpu.make_async_copy(gin_ref, gin_hbm, out_sems.at[0]),
        pltpu.make_async_copy(nt_ref, nt_hbm, out_sems.at[1]),
    ]
    for copy in copies:
        copy.start()
    for copy in copies:
        copy.wait()


def pair_kernel(
    lay, fac_hbm, nt_hbm, gin_hbm, fac0_ref, nt0_ref, gin0_ref, r_ref, s_ref, gain_ref, w_ref, *refs
):
    l_refs, refs = refs[: lay.n_hops], refs[lay.n_hops :]
    out_hbm, l_ref, ls_ref, rs_ref, fac_ref, nt_ref, gin_ref, out_ref, sems, out_sems = refs
    rows, cols, width = out_ref.shape
    mine = width // lay.half
    parts = sems.shape[1]
    size = rows // parts

    def fetch(p):
        here = pl.ds(p * size, size)
        return [
            pltpu.make_async_copy(fac_hbm.at[here], fac_ref.at[here], sems.at[0, p]),
            pltpu.make_async_copy(nt_hbm.at[here], nt_ref.at[here], sems.at[1, p]),
            pltpu.make_async_copy(gin_hbm.at[here], gin_ref.at[here], sems.at[2, p]),
        ]

    def send(n):
        here = pl.ds(2 * n, 2)
        return pltpu.make_async_copy(out_ref.at[here], out_hbm.at[here], out_sems.at[n])

    for p in range(1, parts):
        for copy in fetch(p):
            copy.start()
    gain = column(gain_ref[...], cols)
    eye = identity(cols)
    group = BLOCK // rows
    swap = permutation(rows, group)
    for s, source in lay.received(l_refs):
        l_ref[lay.other(s)] = source[...]
    for to, here in places(width, mine, rows):
        sums = []
        for share in range(to.start, to.stop):
            one, two = (
                r_ref[n]
                for n, device in enumerate(lay.order)
                if device % lay.half == share
            )
            sums.append(one + two)
        left, right = swapped(swap, [l_ref[to], jnp.stack(sums)])
        ls_ref[:, here] = left.reshape(rows, group, cols)
        rs_ref[:, here] = right.reshape(rows, group, cols)

    def part(p, fac_here, nt_here, gin_here):
        for n in range(0, size, 2):
            i = p * size + n
            blocks = []
            for m in range(2):
                left, right, fac = ls_ref[i + m], rs_ref[i + m], fac_here[i + m]
                blocks.append(
                    jnp.concatenate(
                        [
                            left * fac[:width],
                            left * fac[width : 2 * width],
                            right * fac[2 * width : 3 * width],
                            right * fac[3 * width :],
                        ],
                        axis=0,
                    )
                )
            grad_in = dot(w_ref[:, : 4 * width], jnp.concatenate(blocks, axis=1), 1, 0)
            for m in range(2):
                grad = (grad_in[:, m * cols : (m + 1) * cols] + gin_here[i + m].astype(F32)) * gain
                scale_inv = s_ref[pl.ds(i + m, 1), :]
                normed = nt_here[i + m].astype(F32)
                result = norm_back(grad, normed, scale_inv, 0).astype(BF16)
                out_ref[i + m] = dot(eye, result, 1, 1).astype(BF16)
            send(i // 2).start()

    part(0, fac0_ref, nt0_ref, gin0_ref)
    for p in range(1, parts):
        for copy in fetch(p):
            copy.wait()
    for p in range(1, parts):
        part(p, fac_ref, nt_ref, gin_ref)
    for n in range(rows // 2):
        send(n).wait()


class Layout:
    def __init__(self, n_row, n_ch):
        self.n_row, self.n_ch = n_row, n_ch
        self.devices = n_row * n_ch
        self.half = self.devices // 2
        outer = math.isqrt(n_row)
        self.inner = self.devices // outer
        near = [
            2 * n_ch * far + n_ch * core + b
            for b in range(n_ch)
            for far in range(self.inner // (2 * n_ch))
            for core in range(2)
        ]
        self.order = [o * self.inner + n for n in near for o in range(outer)]
        self.inside = [o * self.inner + n for n in near for o in range(outer // 2)]
        self.mate = n_ch
        self.hops = [s for s in range(self.half) if s & self.mate == 0]
        self.hops[3:] = sorted(self.hops[3:], key=lambda s: (s < self.inner, s % n_ch == 0, -s))
        self.n_hops = len(self.hops) + 1
        self.all_place = self.place(self.order, n_row)
        self.half_place = self.place(self.inside, n_row // 2)
        self.near_place = self.place(list(range(self.half)), n_row // 2)

    def place(self, order, n_row):
        return [[order.index(r * self.n_ch + b) for b in range(self.n_ch)] for r in range(n_row)]

    def shares(self, ref, here):
        return jnp.stack([ref[self.inside.index(share)] for share in range(here.start, here.stop)])

    def other(self, s):
        me = lax.axis_index("row") * self.n_ch + lax.axis_index("ch")
        return jnp.bitwise_xor(lax.rem(me, self.half), s)

    def exchange_all(self, blocks):
        return lax.all_to_all(
            blocks, ("row", "ch"), split_axis=0, concat_axis=0, tiled=True, axis_index_groups=[self.order]
        )

    def exchange_half(self, blocks):
        groups = [[first + n for n in self.inside] for first in (0, self.half)]
        return lax.all_to_all(
            blocks, ("row", "ch"), split_axis=0, concat_axis=0, tiled=True, axis_index_groups=groups
        )

    def swap(self, block, s):
        return lax.ppermute(block, ("row", "ch"), [(n, n ^ s) for n in range(self.devices)])

    def permute(self, mine, mates):
        mates = self.swap(mates, self.mate)
        shape = jax.ShapeDtypeStruct((2,) + mine.shape[1:], mine.dtype)
        pairs = call(merge_kernel, [shape] * (len(self.hops) - 1), [], mine, mates)
        return [mine, mates] + [self.swap(pair, s) for pair, s in zip(pairs, self.hops[1:])]

    def received(self, refs):
        mine, mates, *pairs = refs
        found = [(0, mine.at[0]), (self.mate, mates.at[0])]
        for s, pair in zip(self.hops[1:], pairs):
            found += [(s, pair.at[0]), (s ^ self.mate, pair.at[1])]
        return found


def merge_kernel(mine_ref, mates_ref, *outs):
    for n, out_ref in enumerate(outs, 1):
        out_ref[0] = mine_ref[n]
        out_ref[1] = mates_ref[n]


def plane(ref, place, c):
    return jnp.concatenate(
        [
            jnp.concatenate([ref[n, c] for n in column_of], axis=0)
            for column_of in zip(*place)
        ],
        axis=1,
    )


def store_plane(ref, place, c, value):
    rows, cols = ref.shape[-2:]
    for r, row_of in enumerate(place):
        for b, n in enumerate(row_of):
            ref[n, c] = value[r * rows : (r + 1) * rows, b * cols : (b + 1) * cols]


def tri_kernel(lay, r_ref, *refs):
    l_refs, (t_ref, l_ref) = refs[: lay.n_hops], refs[lay.n_hops :]
    for s, source in lay.received(l_refs):
        l_ref[lay.other(s)] = source[...]
    for c in range(t_ref.shape[1]):
        tri = dot(plane(l_ref, lay.near_place, c), plane(r_ref, lay.all_place, c), 1, 1)
        store_plane(t_ref, lay.half_place, c, tri.astype(BF16))


def factor_back_kernel(lay, gt_ref, l_ref, r_ref, gr_hbm, *refs):
    mine_out, mate_out, gl_ref, gr_ref, sems = refs
    copies = []
    for c in range(gt_ref.shape[1]):
        right = dot(plane(gt_ref, lay.half_place, c), plane(l_ref, lay.near_place, c), 0, 0)
        store_plane(gr_ref, lay.all_place, c, right.astype(BF16))
        here = (slice(None), c)
        copies.append(pltpu.make_async_copy(gr_ref.at[here], gr_hbm.at[here], sems.at[c]))
        copies[-1].start()
    for c in range(gt_ref.shape[1]):
        left = dot(plane(gt_ref, lay.half_place, c), plane(r_ref, lay.all_place, c), 1, 0)
        store_plane(gl_ref, lay.near_place, c, left.astype(BF16))
    for n, s in enumerate(lay.hops):
        mine_out[n] = gl_ref[lay.other(s)]
        mate_out[n] = gl_ref[lay.other(s ^ lay.mate)]
    for copy in copies:
        copy.wait()


def by_channel(
    n_row, n_ch, pair_act, cotangent, in_gain, in_bias, proj_weight, out_gain, out_bias, out_weight
):
    lay = Layout(n_row, n_ch)
    rows, cols, width = pair_act.shape
    mine = width // lay.half
    struct = jax.ShapeDtypeStruct
    half = pltpu.VMEM((rows, width, cols), BF16)
    weight_t = pltpu.VMEM((4 * width, width), BF16)
    in_gain, in_bias, out_gain, out_bias = (
        v.reshape(1, width) for v in (in_gain, in_bias, out_gain, out_bias)
    )

    some = struct((len(lay.hops), mine, rows, cols), BF16)
    one = struct((lay.half, mine, rows, cols), BF16)
    one_here = pltpu.VMEM(one.shape, BF16)
    two_shape = (lay.devices, mine, rows, cols)
    row = pltpu.VMEM((1, width), F32)
    weight = pltpu.VMEM(proj_weight.shape, BF16)
    out_weight_here = pltpu.VMEM((width, width), BF16)
    both_weights = pltpu.VMEM((width, 2 * width), BF16)
    both_turned = pltpu.VMEM((2 * width, width), BF16)
    right, normal_in = call(
        functools.partial(right_kernel, lay),
        [pltpu.HBM(two_shape, BF16), struct((rows // 2, width, 2 * cols), BF16)],
        [
            half,
            row,
            row,
            both_weights,
            both_turned,
            half,
            one_here,
            pltpu.SemaphoreType.DMA((4 + PARTS // 2,)),
            pltpu.SemaphoreType.DMA((lay.devices,)),
        ],
        pair_act,
        in_gain,
        in_bias,
        proj_weight,
        hbm=4,
    )
    left = call(
        functools.partial(left_kernel, lay),
        [some, some],
        [both_weights, both_turned, half, one_here, pltpu.SemaphoreType.DMA((2,))],
        proj_weight,
        normal_in,
        hbm=1,
    )
    right = lay.exchange_all(right)
    left = lay.permute(*left)
    h, fac = call(
        gate_kernel,
        [pltpu.VMEM((rows, width, cols), F32), pltpu.HBM((rows, 4 * width, cols), BF16)],
        [
            pltpu.VMEM((rows, 4 * width, cols), BF16),
            weight_t,
            half,
            half,
            row,
            row,
            weight,
            row,
            out_weight_here,
            pltpu.SemaphoreType.DMA((7,)),
            pltpu.SemaphoreType.DMA((PARTS,)),
        ],
        pair_act,
        cotangent,
        in_gain,
        in_bias,
        proj_weight,
        out_gain,
        out_weight,
        hbm=7,
    )
    right, h, fac = lax.optimization_barrier((right, h, fac))
    tri, left = call(functools.partial(tri_kernel, lay), [one, one], [], right, *left)
    tri = lay.exchange_half(tri)
    grad_tri = call(functools.partial(tri_back_kernel, lay), one, [half, half], tri, h)
    grad_right, *grad_left = call(
        functools.partial(factor_back_kernel, lay),
        [pltpu.HBM(two_shape, BF16), some, some],
        [one_here, pltpu.VMEM(two_shape, BF16), pltpu.SemaphoreType.DMA((mine,))],
        lay.exchange_half(grad_tri),
        left,
        right,
    )
    grad_right = lay.exchange_all(grad_right)
    grad_left = lay.permute(*grad_left)
    grad_in_first, normed_first, fac_first, grad_in, normed_t, scale = call(
        functools.partial(logit_kernel, lay),
        [
            pltpu.VMEM((rows // PARTS, width, cols), BF16),
            pltpu.VMEM((rows // PARTS, width, cols), BF16),
            pltpu.VMEM((rows // PARTS, 4 * width, cols), BF16),
            pltpu.HBM((rows, width, cols), BF16),
            pltpu.HBM((rows, width, cols), BF16),
            pltpu.VMEM((rows, cols), F32),
        ],
        [
            half,
            half,
            half,
            pltpu.SemaphoreType.DMA((2,)),
            half,
            half,
            row,
            row,
            weight,
            row,
            row,
            out_weight_here,
            pltpu.SemaphoreType.DMA((9,)),
        ],
        fac,
        pair_act,
        cotangent,
        in_gain,
        in_bias,
        proj_weight,
        out_gain,
        out_bias,
        out_weight,
        tri,
        hbm=9,
    )
    return call(
        functools.partial(pair_kernel, lay),
        pltpu.HBM((rows, cols, width), BF16),
        [
            one_here,
            half,
            half,
            pltpu.VMEM((rows, 4 * width, cols), BF16),
            half,
            half,
            half,
            pltpu.SemaphoreType.DMA((3, PARTS)),
            pltpu.SemaphoreType.DMA((rows // 2,)),
        ],
        fac,
        normed_t,
        grad_in,
        fac_first,
        normed_first,
        grad_in_first,
        grad_right,
        scale,
        in_gain,
        proj_weight,
        *grad_left,
        hbm=3,
    )


def by_row(
    pair_act, cotangent, in_gain, in_bias, proj_weight, out_gain, out_bias, out_weight
):
    rows_here, cols_here, width = pair_act.shape
    flat = pair_act.astype(jnp.float32).reshape(rows_here * cols_here, width)
    normed, scale_inv = normalize(flat, -1)
    normal_in = (normed * in_gain + in_bias).astype(jnp.bfloat16)
    projected = jnp.einsum("pd,de->ep", normal_in, proj_weight, preferred_element_type=jnp.float32)
    blocks = jnp.split(projected, 5, axis=0)
    left_sig = jax.nn.sigmoid(blocks[1])
    right_sig = jax.nn.sigmoid(blocks[3])
    left_fac = (left_sig * blocks[0]).astype(jnp.bfloat16).reshape(width, rows_here, cols_here)
    right_fac = (right_sig * blocks[2]).astype(jnp.bfloat16).reshape(width, rows_here, cols_here)
    left_chan, right_chan = (
        lax.all_to_all(left_fac, "ch", split_axis=0, concat_axis=2, tiled=True),
        lax.all_to_all(right_fac, "ch", split_axis=0, concat_axis=2, tiled=True),
    )
    tri_chan = jnp.einsum(
        "cik,cjk->cij",
        left_chan,
        lax.all_gather(right_chan, "row", axis=1, tiled=True),
        preferred_element_type=jnp.float32,
    ).astype(jnp.bfloat16)
    tri_back = lax.all_to_all(tri_chan, "ch", split_axis=2, concat_axis=0, tiled=True)
    tri_hat, tri_inv = normalize(tri_back.astype(jnp.float32).reshape(width, -1), 0)
    normal_out = (tri_hat * out_gain[:, None] + out_bias[:, None]).astype(jnp.bfloat16)
    mixed = jnp.einsum("cp,ce->ep", normal_out, out_weight, preferred_element_type=jnp.float32)
    out_gate = jax.nn.sigmoid(blocks[4])
    grad_out = cotangent.astype(jnp.float32).reshape(rows_here * cols_here, width).T
    grad_mixed = (grad_out * out_gate).astype(jnp.bfloat16)
    grad_logit = grad_out * mixed * out_gate * (1.0 - out_gate)
    grad_normal = jnp.einsum(
        "ep,ce->cp", grad_mixed, out_weight, preferred_element_type=jnp.float32
    )
    grad_tri = norm_back(grad_normal * out_gain[:, None], tri_hat, tri_inv, 0)
    grad_tri = grad_tri.astype(jnp.bfloat16).reshape(width, rows_here, cols_here)
    grad_chan = lax.all_to_all(grad_tri, "ch", split_axis=0, concat_axis=2, tiled=True)
    grad_cols = lax.all_to_all(grad_chan, "row", split_axis=2, concat_axis=1, tiled=True)
    grad_left = jnp.einsum(
        "cij,cjk->cik",
        grad_chan,
        lax.all_gather(right_chan, "row", axis=1, tiled=True),
        preferred_element_type=jnp.float32,
    )
    grad_right = jnp.einsum(
        "cij,cik->cjk",
        grad_cols,
        lax.all_gather(left_chan, "row", axis=1, tiled=True),
        preferred_element_type=jnp.float32,
    )
    left_back, right_back = (
        lax.all_to_all(
            grad_left.astype(jnp.bfloat16), "ch", split_axis=2, concat_axis=0, tiled=True
        ),
        lax.all_to_all(
            grad_right.astype(jnp.bfloat16), "ch", split_axis=2, concat_axis=0, tiled=True
        ),
    )
    left_grad = left_back.astype(jnp.float32).reshape(width, -1)
    right_grad = right_back.astype(jnp.float32).reshape(width, -1)
    grad_proj = jnp.concatenate(
        [
            left_grad * left_sig,
            left_grad * blocks[0] * left_sig * (1.0 - left_sig),
            right_grad * right_sig,
            right_grad * blocks[2] * right_sig * (1.0 - right_sig),
            grad_logit,
        ],
        axis=0,
    ).astype(jnp.bfloat16)
    grad_in = jnp.einsum("ep,de->pd", grad_proj, proj_weight, preferred_element_type=jnp.float32)
    grad_pair = norm_back(grad_in * in_gain, normed, scale_inv, -1)
    return grad_pair.astype(jnp.bfloat16).reshape(rows_here, cols_here, width)


def solution(mesh):
    n_row, n_ch = mesh.shape["row"], mesh.shape["ch"]
    placed = (P("row", "ch", None), P("row", "ch", None), P(), P(), P(), P(), P(), P())

    def on_device(*args):
        rows, cols, width = args[0].shape
        devices, outer, group = n_row * n_ch, math.isqrt(n_row), BLOCK // rows
        if (
            devices & (devices - 1) == 0
            and n_row >= 4
            and n_row % outer == 0
            and (devices // outer) % (2 * n_ch) == 0
            and outer % 2 == 0
            and width % (devices // 2) == 0
            and rows % (2 * PARTS) == 0
            and BLOCK % rows == 0
            and group % (width // (devices // 2)) == 0
            and width % (2 * group) == 0
            and cols % 128 == 0
            and width <= 256
            and width & (width - 1) == 0
        ):
            return by_channel(n_row, n_ch, *args)
        return by_row(*args)

    return jax.shard_map(
        on_device, mesh=mesh, in_specs=placed, out_specs=P("row", "ch", None), check_vma=False
    )
```

```python
import functools
import math

import jax
import jax.numpy as jnp
from jax import lax
from jax.experimental import pallas as pl
from jax.experimental.pallas import tpu as pltpu
from jax.sharding import PartitionSpec as P

EPSILON = 1e-05
F32 = jnp.float32
BF16 = jnp.bfloat16
UNROLL = 4
BLOCK = 256
PARTS = 4


def dot(a, b, da, db):
    return lax.dot_general(a, b, (((da,), (db,)), ((), ())), preferred_element_type=F32)


def sigmoid(values):
    return 0.5 * jnp.tanh(0.5 * values) + 0.5


def normalize(values, axis):
    center = jnp.mean(values, axis=axis, keepdims=True)
    shifted = values - center
    scale_inv = lax.rsqrt(jnp.mean(shifted * shifted, axis=axis, keepdims=True) + EPSILON)
    return (shifted * scale_inv, scale_inv)


def norm_back(grad_hat, normed, scale_inv, axis):
    first = jnp.mean(grad_hat, axis=axis, keepdims=True)
    second = jnp.mean(grad_hat * normed, axis=axis, keepdims=True)
    return scale_inv * (grad_hat - first - normed * second)


def column(row, width):
    return jnp.broadcast_to(row, (width, row.shape[-1])).T


def call(kernel, outs, scratch, *args, hbm=0, limit=16):
    single = not isinstance(outs, (list, tuple))
    args = [pltpu.with_memory_space_constraint(a, pltpu.HBM) if n < hbm else a for n, a in enumerate(args)]
    specs = [pl.BlockSpec(memory_space=pltpu.HBM if n < hbm else pltpu.VMEM) for n in range(len(args))]
    out_specs = [
        pl.BlockSpec(memory_space=getattr(out, "memory_space", pltpu.VMEM))
        for out in ([outs] if single else outs)
    ]
    return pl.pallas_call(
        kernel,
        out_shape=outs if single else tuple(outs),
        in_specs=specs,
        out_specs=out_specs[0] if single else tuple(out_specs),
        scratch_shapes=scratch,
        compiler_params=pltpu.CompilerParams(vmem_limit_bytes=limit * 1024 * 1024),
    )(*args)


def permutation(outer, inner):
    to = lax.broadcasted_iota(jnp.int32, (BLOCK, BLOCK), 0)
    start = lax.broadcasted_iota(jnp.int32, (BLOCK, BLOCK), 1)
    return (start == to % inner * outer + to // inner).astype(F32).astype(BF16)


def identity(size):
    first = lax.broadcasted_iota(jnp.int32, (size, size), 0)
    return (first == lax.broadcasted_iota(jnp.int32, (size, size), 1)).astype(F32).astype(BF16)


def swapped(swap, blocks):
    cols = blocks[0].shape[-1]
    wide = jnp.concatenate([block.reshape(BLOCK, cols) for block in blocks], axis=1)
    wide = dot(swap, wide, 1, 0).astype(BF16)
    return [wide[:, n * cols : (n + 1) * cols] for n in range(len(blocks))]


def fetched(sources, targets, sems):
    copies = [
        pltpu.make_async_copy(source, target, sems.at[n])
        for n, (source, target) in enumerate(zip(sources, targets))
    ]
    for copy in copies:
        copy.start()
    for copy in copies:
        copy.wait()


def weight_copies(w_hbm, w_ref, first, sems):
    width = w_hbm.shape[0]
    return [
        pltpu.make_async_copy(
            w_hbm.at[:, (first + n) * width : (first + n + 1) * width],
            w_ref.at[:, n * width : (n + 1) * width],
            sems.at[n],
        )
        for n in range(2)
    ]


def right_kernel(
    lay, x_hbm, gain_hbm, bias_hbm, w_hbm, r_hbm, n_ref, x_ref, gain_ref, bias_ref, w_ref, wt_ref, r_ref, right_ref, sems, out_sems
):
    rows, cols, width = x_ref.shape
    mine = width // lay.half
    parts = sems.shape[0] - 4
    size = rows // parts

    def fetch(p):
        here = pl.ds(p * size, size)
        return pltpu.make_async_copy(x_hbm.at[here], x_ref.at[here], sems.at[4 + p])

    small = [
        pltpu.make_async_copy(gain_hbm, gain_ref, sems.at[2]),
        pltpu.make_async_copy(bias_hbm, bias_ref, sems.at[3]),
    ]
    weights = weight_copies(w_hbm, w_ref, 2, sems)
    fetch(0).start()
    for copy in small + weights:
        copy.start()
    for p in range(1, parts):
        fetch(p).start()
    group = BLOCK // rows
    swap = permutation(group, rows)

    def normal(p):
        fetch(p).wait()
        for n in range(0, size, 2):
            i = p * size + n
            shifted = dot(center, x_ref[pl.ds(i, 2)].reshape(2 * cols, width), 1, 1)
            scale_inv = lax.rsqrt(jnp.mean(shifted * shifted, axis=0, keepdims=True) + EPSILON)
            n_ref[p * size // 2 + n // 2] = (shifted * scale_inv * gain + bias).astype(BF16)

    def project(p):
        for n in range(0, size, 2):
            i = p * size + n
            proj = dot(wt_ref[...], n_ref[p * size // 2 + n // 2], 1, 0)
            right = (sigmoid(proj[width:]) * proj[:width]).astype(BF16)
            for m in range(2):
                r_ref[i + m] = right[:, m * cols : (m + 1) * cols]

    def body(p, _):
        normal(p)
        project(p - 1)
        return 0

    center = (identity(width).astype(F32) - 1.0 / width).astype(BF16)
    for copy in small:
        copy.wait()
    gain = column(gain_ref[...], 2 * cols)
    bias = column(bias_ref[...], 2 * cols)
    normal(0)
    for copy in weights:
        copy.wait()
    wt_ref[...] = w_ref[...].astype(F32).T.astype(BF16)
    lax.fori_loop(1, parts, body, 0)
    project(parts - 1)
    out = []
    blocks = places(width, mine, rows)
    for k in range(0, len(blocks), 2):
        pair = blocks[k : k + 2]
        for (to, _here), right in zip(pair, swapped(swap, [r_ref[:, here] for _to, here in pair])):
            right_ref[to] = right.reshape(group // mine, mine, rows, cols)
            for share in range(to.start, to.stop):
                for n, device in enumerate(lay.order):
                    if device % lay.half == share:
                        out.append(pltpu.make_async_copy(right_ref.at[share], r_hbm.at[n], out_sems.at[n]))
                        out[-1].start()
    for copy in out:
        copy.wait()


def left_kernel(lay, w_hbm, n_ref, mine_out, mate_out, w_ref, wt_ref, l_ref, left_ref, sems):
    rows, width, cols = l_ref.shape
    mine = width // lay.half
    group = BLOCK // rows
    weights = weight_copies(w_hbm, w_ref, 0, sems)
    for copy in weights:
        copy.start()
    for copy in weights:
        copy.wait()
    wt_ref[...] = w_ref[...].astype(F32).T.astype(BF16)
    swap = permutation(group, rows)

    def body(n, _):
        proj = dot(wt_ref[...], n_ref[n], 1, 0)
        left = (sigmoid(proj[width:]) * proj[:width]).astype(BF16)
        for m in range(2):
            l_ref[2 * n + m] = left[:, m * cols : (m + 1) * cols]
        return 0

    lax.fori_loop(0, rows // 2, body, 0, unroll=2)
    blocks = places(width, mine, rows)
    for k in range(0, len(blocks), 2):
        pair = blocks[k : k + 2]
        for (to, _here), left in zip(pair, swapped(swap, [l_ref[:, here] for _to, here in pair])):
            left_ref[to] = left.reshape(group // mine, mine, rows, cols)
    for n, s in enumerate(lay.hops):
        mine_out[n] = left_ref[lay.other(s)]
        mate_out[n] = left_ref[lay.other(s ^ lay.mate)]


def gate_kernel(*refs):
    sources, (h_ref, fac_hbm, fac_ref, wt_ref), targets, (sems, out_sems) = (
        refs[:7],
        refs[7:11],
        refs[11:18],
        refs[18:],
    )
    x_ref, cot_ref, gain_ref, bias_ref, w_ref, ogain_ref, ow_ref = targets
    rows, cols, width = x_ref.shape
    fetched(sources, targets, sems)
    wt_ref[...] = w_ref[:, : 4 * width].astype(F32).T.astype(BF16)
    ogain = column(ogain_ref[...], cols)

    def body(i, _):
        normed, _s = normalize(x_ref[i].astype(F32), -1)
        normal_in = (normed * gain_ref[...] + bias_ref[...]).astype(BF16)
        proj = dot(wt_ref[...], normal_in, 1, 1)
        for side in range(2):
            val = proj[2 * side * width : (2 * side + 1) * width]
            sig = sigmoid(proj[(2 * side + 1) * width : (2 * side + 2) * width])
            fac_ref[i, 2 * side * width : (2 * side + 1) * width] = sig.astype(BF16)
            fac_ref[i, (2 * side + 1) * width : (2 * side + 2) * width] = (
                val * sig * (1.0 - sig)
            ).astype(BF16)
        out_gate = sigmoid(dot(normal_in, w_ref[:, 4 * width :], 1, 0))
        grad_mixed = (cot_ref[i].astype(F32) * out_gate).astype(BF16)
        h_ref[i] = dot(ow_ref[...], grad_mixed, 1, 1) * ogain
        return 0

    size = rows // PARTS

    def send(p):
        here = pl.ds(p * size, size)
        return pltpu.make_async_copy(fac_ref.at[here], fac_hbm.at[here], out_sems.at[p])

    def part(p, _):
        for n in range(size):
            body(p * size + n, 0)
        send(p).start()
        return 0

    lax.fori_loop(0, PARTS, part, 0)
    for p in range(PARTS):
        send(p).wait()


def places(n_channels, mine, rows):
    group = BLOCK // rows
    return [
        (slice(c // mine, (c + group) // mine), slice(c, c + group)) for c in range(0, n_channels, group)
    ]


def to_rows(lay, t_ref, ts_ref):
    rows, width, cols = ts_ref.shape
    mine = t_ref.shape[1]
    group = BLOCK // rows
    swap = permutation(rows, group)
    blocks = places(width, mine, rows)
    for n in range(0, len(blocks), 2):
        pair = blocks[n : n + 2]
        for (_to, here), block in zip(pair, swapped(swap, [lay.shares(t_ref, to) for to, _here in pair])):
            ts_ref[:, here] = block.reshape(rows, group, cols)


def tri_back_kernel(lay, t_ref, h_ref, gt_ref, ts_ref, gs_ref):
    rows, width, cols = h_ref.shape
    mine = t_ref.shape[1]
    group = BLOCK // rows
    back = permutation(group, rows)
    to_rows(lay, t_ref, ts_ref)

    def body(i, _):
        tri, h = ts_ref[i].astype(F32), h_ref[i]
        shifted = tri - jnp.mean(tri, axis=0, keepdims=True)
        first = jnp.mean(h, axis=0, keepdims=True)
        both = jnp.mean(h * shifted, axis=0, keepdims=True)
        tri_inv = lax.rsqrt(jnp.mean(shifted * shifted, axis=0, keepdims=True) + EPSILON)
        gs_ref[i] = (tri_inv * (h - first - shifted * (both * tri_inv * tri_inv))).astype(BF16)
        return 0

    lax.fori_loop(0, rows, body, 0, unroll=4 * UNROLL)
    blocks = places(width, mine, rows)
    for n in range(0, len(blocks), 2):
        pair = blocks[n : n + 2]
        for (to, _here), block in zip(pair, swapped(back, [gs_ref[:, here] for _to, here in pair])):
            block = block.reshape(group // mine, mine, rows, cols)
            for share in range(to.start, to.stop):
                gt_ref[lay.inside.index(share)] = block[share - to.start]


def logit_kernel(lay, *refs):
    (fac_hbm, *sources), t_ref, refs = refs[:9], refs[9], refs[10:]
    (gin0_ref, nt0_ref, fac0_ref, gin_hbm, nt_hbm, s_ref), refs = refs[:6], refs[6:]
    (ts_ref, gin_ref, nt_ref, out_sems), targets, sems = refs[:4], refs[4:12], refs[12]
    x_ref, cot_ref, gain_ref, bias_ref, w_ref, ogain_ref, obias_ref, ow_ref = targets
    rows, cols, width = x_ref.shape
    first = pl.ds(0, nt0_ref.shape[0])
    fetched([*sources, fac_hbm.at[first]], [*targets, fac0_ref], sems)
    to_rows(lay, t_ref, ts_ref)
    ogain = column(ogain_ref[...], cols)
    obias = column(obias_ref[...], cols)

    def body(i, _):
        normed, scale_inv = normalize(x_ref[i].astype(F32), -1)
        normal_in = (normed * gain_ref[...] + bias_ref[...]).astype(BF16)
        out_gate = sigmoid(dot(normal_in, w_ref[:, 4 * width :], 1, 0))
        tri_hat, _s = normalize(ts_ref[i].astype(F32), 0)
        normal_out = (tri_hat * ogain + obias).astype(BF16)
        mixed = dot(normal_out, ow_ref[...], 0, 0)
        grad_logit = cot_ref[i].astype(F32) * mixed * out_gate * (1.0 - out_gate)
        gin_ref[i] = dot(w_ref[:, 4 * width :], grad_logit.astype(BF16), 1, 1).astype(BF16)
        nt_ref[i] = normed.T.astype(BF16)
        s_ref[pl.ds(i, 1), :] = jnp.broadcast_to(scale_inv, (cols, width)).T[:1]
        return 0

    lax.fori_loop(0, rows, body, 0, unroll=UNROLL)
    gin0_ref[...] = gin_ref[first]
    nt0_ref[...] = nt_ref[first]
    copies = [
        pltpu.make_async_copy(gin_ref, gin_hbm, out_sems.at[0]),
        pltpu.make_async_copy(nt_ref, nt_hbm, out_sems.at[1]),
    ]
    for copy in copies:
        copy.start()
    for copy in copies:
        copy.wait()


def pair_kernel(
    lay, fac_hbm, nt_hbm, gin_hbm, fac0_ref, nt0_ref, gin0_ref, r_ref, s_ref, gain_ref, w_ref, *refs
):
    l_refs, refs = refs[: lay.n_hops], refs[lay.n_hops :]
    out_hbm, l_ref, ls_ref, rs_ref, fac_ref, nt_ref, gin_ref, out_ref, sems, out_sems = refs
    rows, cols, width = out_ref.shape
    mine = width // lay.half
    parts = sems.shape[1]
    size = rows // parts

    def fetch(p):
        here = pl.ds(p * size, size)
        return [
            pltpu.make_async_copy(fac_hbm.at[here], fac_ref.at[here], sems.at[0, p]),
            pltpu.make_async_copy(nt_hbm.at[here], nt_ref.at[here], sems.at[1, p]),
            pltpu.make_async_copy(gin_hbm.at[here], gin_ref.at[here], sems.at[2, p]),
        ]

    def send(n):
        here = pl.ds(2 * n, 2)
        return pltpu.make_async_copy(out_ref.at[here], out_hbm.at[here], out_sems.at[n])

    for p in range(1, parts):
        for copy in fetch(p):
            copy.start()
    gain = column(gain_ref[...], cols)
    eye = identity(cols)
    group = BLOCK // rows
    swap = permutation(rows, group)
    for s, source in lay.received(l_refs):
        l_ref[lay.other(s)] = source[...]
    for to, here in places(width, mine, rows):
        sums = []
        for share in range(to.start, to.stop):
            one, two = (
                r_ref[n]
                for n, device in enumerate(lay.order)
                if device % lay.half == share
            )
            sums.append(one + two)
        left, right = swapped(swap, [l_ref[to], jnp.stack(sums)])
        ls_ref[:, here] = left.reshape(rows, group, cols)
        rs_ref[:, here] = right.reshape(rows, group, cols)

    def part(p, fac_here, nt_here, gin_here):
        for n in range(0, size, 2):
            i = p * size + n
            blocks = []
            for m in range(2):
                left, right, fac = ls_ref[i + m], rs_ref[i + m], fac_here[i + m]
                blocks.append(
                    jnp.concatenate(
                        [
                            left * fac[:width],
                            left * fac[width : 2 * width],
                            right * fac[2 * width : 3 * width],
                            right * fac[3 * width :],
                        ],
                        axis=0,
                    )
                )
            grad_in = dot(w_ref[:, : 4 * width], jnp.concatenate(blocks, axis=1), 1, 0)
            for m in range(2):
                grad = (grad_in[:, m * cols : (m + 1) * cols] + gin_here[i + m].astype(F32)) * gain
                scale_inv = s_ref[pl.ds(i + m, 1), :]
                normed = nt_here[i + m].astype(F32)
                result = norm_back(grad, normed, scale_inv, 0).astype(BF16)
                out_ref[i + m] = dot(eye, result, 1, 1).astype(BF16)
            send(i // 2).start()

    part(0, fac0_ref, nt0_ref, gin0_ref)
    for p in range(1, parts):
        for copy in fetch(p):
            copy.wait()
    for p in range(1, parts):
        part(p, fac_ref, nt_ref, gin_ref)
    for n in range(rows // 2):
        send(n).wait()


class Layout:
    def __init__(self, n_row, n_ch):
        self.n_row, self.n_ch = n_row, n_ch
        self.devices = n_row * n_ch
        self.half = self.devices // 2
        outer = math.isqrt(n_row)
        self.inner = self.devices // outer
        near = [
            2 * n_ch * far + n_ch * core + b
            for b in range(n_ch)
            for far in range(self.inner // (2 * n_ch))
            for core in range(2)
        ]
        self.order = [o * self.inner + n for n in near for o in range(outer)]
        self.inside = [o * self.inner + n for n in near for o in range(outer // 2)]
        self.mate = n_ch
        self.hops = [s for s in range(self.half) if s & self.mate == 0]
        self.hops[3:] = self.hops[:2:-1]
        self.n_hops = len(self.hops) + 1
        self.all_place = self.place(self.order, n_row)
        self.half_place = self.place(self.inside, n_row // 2)
        self.near_place = self.place(list(range(self.half)), n_row // 2)

    def place(self, order, n_row):
        return [[order.index(r * self.n_ch + b) for b in range(self.n_ch)] for r in range(n_row)]

    def shares(self, ref, here):
        return jnp.stack([ref[self.inside.index(share)] for share in range(here.start, here.stop)])

    def other(self, s):
        me = lax.axis_index("row") * self.n_ch + lax.axis_index("ch")
        return jnp.bitwise_xor(lax.rem(me, self.half), s)

    def exchange_all(self, blocks):
        return lax.all_to_all(
            blocks, ("row", "ch"), split_axis=0, concat_axis=0, tiled=True, axis_index_groups=[self.order]
        )

    def exchange_half(self, blocks):
        groups = [[first + n for n in self.inside] for first in (0, self.half)]
        return lax.all_to_all(
            blocks, ("row", "ch"), split_axis=0, concat_axis=0, tiled=True, axis_index_groups=groups
        )

    def swap(self, block, s):
        return lax.ppermute(block, ("row", "ch"), [(n, n ^ s) for n in range(self.devices)])

    def permute(self, mine, mates):
        mates = self.swap(mates, self.mate)
        shape = jax.ShapeDtypeStruct((2,) + mine.shape[1:], mine.dtype)
        pairs = call(merge_kernel, [shape] * (len(self.hops) - 1), [], mine, mates)
        return [mine, mates] + [self.swap(pair, s) for pair, s in zip(pairs, self.hops[1:])]

    def received(self, refs):
        mine, mates, *pairs = refs
        found = [(0, mine.at[0]), (self.mate, mates.at[0])]
        for s, pair in zip(self.hops[1:], pairs):
            found += [(s, pair.at[0]), (s ^ self.mate, pair.at[1])]
        return found


def merge_kernel(mine_ref, mates_ref, *outs):
    for n, out_ref in enumerate(outs, 1):
        out_ref[0] = mine_ref[n]
        out_ref[1] = mates_ref[n]


def plane(ref, place, c):
    return jnp.concatenate(
        [
            jnp.concatenate([ref[n, c] for n in column_of], axis=0)
            for column_of in zip(*place)
        ],
        axis=1,
    )


def store_plane(ref, place, c, value):
    rows, cols = ref.shape[-2:]
    for r, row_of in enumerate(place):
        for b, n in enumerate(row_of):
            ref[n, c] = value[r * rows : (r + 1) * rows, b * cols : (b + 1) * cols]


def tri_kernel(lay, r_ref, *refs):
    l_refs, (t_ref, l_ref) = refs[: lay.n_hops], refs[lay.n_hops :]
    for s, source in lay.received(l_refs):
        l_ref[lay.other(s)] = source[...]
    for c in range(t_ref.shape[1]):
        tri = dot(plane(l_ref, lay.near_place, c), plane(r_ref, lay.all_place, c), 1, 1)
        store_plane(t_ref, lay.half_place, c, tri.astype(BF16))


def factor_back_kernel(lay, gt_ref, l_ref, r_ref, gr_hbm, *refs):
    mine_out, mate_out, gl_ref, gr_ref, sems = refs
    copies = []
    for c in range(gt_ref.shape[1]):
        right = dot(plane(gt_ref, lay.half_place, c), plane(l_ref, lay.near_place, c), 0, 0)
        store_plane(gr_ref, lay.all_place, c, right.astype(BF16))
        here = (slice(None), c)
        copies.append(pltpu.make_async_copy(gr_ref.at[here], gr_hbm.at[here], sems.at[c]))
        copies[-1].start()
    for c in range(gt_ref.shape[1]):
        left = dot(plane(gt_ref, lay.half_place, c), plane(r_ref, lay.all_place, c), 1, 0)
        store_plane(gl_ref, lay.near_place, c, left.astype(BF16))
    for n, s in enumerate(lay.hops):
        mine_out[n] = gl_ref[lay.other(s)]
        mate_out[n] = gl_ref[lay.other(s ^ lay.mate)]
    for copy in copies:
        copy.wait()


def by_channel(
    n_row, n_ch, pair_act, cotangent, in_gain, in_bias, proj_weight, out_gain, out_bias, out_weight
):
    lay = Layout(n_row, n_ch)
    rows, cols, width = pair_act.shape
    mine = width // lay.half
    struct = jax.ShapeDtypeStruct
    half = pltpu.VMEM((rows, width, cols), BF16)
    weight_t = pltpu.VMEM((4 * width, width), BF16)
    in_gain, in_bias, out_gain, out_bias = (
        v.reshape(1, width) for v in (in_gain, in_bias, out_gain, out_bias)
    )

    some = struct((len(lay.hops), mine, rows, cols), BF16)
    one = struct((lay.half, mine, rows, cols), BF16)
    one_here = pltpu.VMEM(one.shape, BF16)
    two_shape = (lay.devices, mine, rows, cols)
    row = pltpu.VMEM((1, width), F32)
    weight = pltpu.VMEM(proj_weight.shape, BF16)
    out_weight_here = pltpu.VMEM((width, width), BF16)
    both_weights = pltpu.VMEM((width, 2 * width), BF16)
    both_turned = pltpu.VMEM((2 * width, width), BF16)
    right, normal_in = call(
        functools.partial(right_kernel, lay),
        [pltpu.HBM(two_shape, BF16), struct((rows // 2, width, 2 * cols), BF16)],
        [
            half,
            row,
            row,
            both_weights,
            both_turned,
            half,
            one_here,
            pltpu.SemaphoreType.DMA((4 + PARTS // 2,)),
            pltpu.SemaphoreType.DMA((lay.devices,)),
        ],
        pair_act,
        in_gain,
        in_bias,
        proj_weight,
        hbm=4,
    )
    left = call(
        functools.partial(left_kernel, lay),
        [some, some],
        [both_weights, both_turned, half, one_here, pltpu.SemaphoreType.DMA((2,))],
        proj_weight,
        normal_in,
        hbm=1,
    )
    right = lay.exchange_all(right)
    left = lay.permute(*left)
    h, fac = call(
        gate_kernel,
        [pltpu.VMEM((rows, width, cols), F32), pltpu.HBM((rows, 4 * width, cols), BF16)],
        [
            pltpu.VMEM((rows, 4 * width, cols), BF16),
            weight_t,
            half,
            half,
            row,
            row,
            weight,
            row,
            out_weight_here,
            pltpu.SemaphoreType.DMA((7,)),
            pltpu.SemaphoreType.DMA((PARTS,)),
        ],
        pair_act,
        cotangent,
        in_gain,
        in_bias,
        proj_weight,
        out_gain,
        out_weight,
        hbm=7,
    )
    right, h, fac = lax.optimization_barrier((right, h, fac))
    tri, left = call(functools.partial(tri_kernel, lay), [one, one], [], right, *left)
    tri = lay.exchange_half(tri)
    grad_tri = call(functools.partial(tri_back_kernel, lay), one, [half, half], tri, h)
    grad_right, *grad_left = call(
        functools.partial(factor_back_kernel, lay),
        [pltpu.HBM(two_shape, BF16), some, some],
        [one_here, pltpu.VMEM(two_shape, BF16), pltpu.SemaphoreType.DMA((mine,))],
        lay.exchange_half(grad_tri),
        left,
        right,
    )
    grad_right = lay.exchange_all(grad_right)
    grad_left = lay.permute(*grad_left)
    grad_in_first, normed_first, fac_first, grad_in, normed_t, scale = call(
        functools.partial(logit_kernel, lay),
        [
            pltpu.VMEM((rows // PARTS, width, cols), BF16),
            pltpu.VMEM((rows // PARTS, width, cols), BF16),
            pltpu.VMEM((rows // PARTS, 4 * width, cols), BF16),
            pltpu.HBM((rows, width, cols), BF16),
            pltpu.HBM((rows, width, cols), BF16),
            pltpu.VMEM((rows, cols), F32),
        ],
        [
            half,
            half,
            half,
            pltpu.SemaphoreType.DMA((2,)),
            half,
            half,
            row,
            row,
            weight,
            row,
            row,
            out_weight_here,
            pltpu.SemaphoreType.DMA((9,)),
        ],
        fac,
        pair_act,
        cotangent,
        in_gain,
        in_bias,
        proj_weight,
        out_gain,
        out_bias,
        out_weight,
        tri,
        hbm=9,
    )
    return call(
        functools.partial(pair_kernel, lay),
        pltpu.HBM((rows, cols, width), BF16),
        [
            one_here,
            half,
            half,
            pltpu.VMEM((rows, 4 * width, cols), BF16),
            half,
            half,
            half,
            pltpu.SemaphoreType.DMA((3, PARTS)),
            pltpu.SemaphoreType.DMA((rows // 2,)),
        ],
        fac,
        normed_t,
        grad_in,
        fac_first,
        normed_first,
        grad_in_first,
        grad_right,
        scale,
        in_gain,
        proj_weight,
        *grad_left,
        hbm=3,
    )


def by_row(
    pair_act, cotangent, in_gain, in_bias, proj_weight, out_gain, out_bias, out_weight
):
    rows_here, cols_here, width = pair_act.shape
    flat = pair_act.astype(jnp.float32).reshape(rows_here * cols_here, width)
    normed, scale_inv = normalize(flat, -1)
    normal_in = (normed * in_gain + in_bias).astype(jnp.bfloat16)
    projected = jnp.einsum("pd,de->ep", normal_in, proj_weight, preferred_element_type=jnp.float32)
    blocks = jnp.split(projected, 5, axis=0)
    left_sig = jax.nn.sigmoid(blocks[1])
    right_sig = jax.nn.sigmoid(blocks[3])
    left_fac = (left_sig * blocks[0]).astype(jnp.bfloat16).reshape(width, rows_here, cols_here)
    right_fac = (right_sig * blocks[2]).astype(jnp.bfloat16).reshape(width, rows_here, cols_here)
    left_chan, right_chan = (
        lax.all_to_all(left_fac, "ch", split_axis=0, concat_axis=2, tiled=True),
        lax.all_to_all(right_fac, "ch", split_axis=0, concat_axis=2, tiled=True),
    )
    tri_chan = jnp.einsum(
        "cik,cjk->cij",
        left_chan,
        lax.all_gather(right_chan, "row", axis=1, tiled=True),
        preferred_element_type=jnp.float32,
    ).astype(jnp.bfloat16)
    tri_back = lax.all_to_all(tri_chan, "ch", split_axis=2, concat_axis=0, tiled=True)
    tri_hat, tri_inv = normalize(tri_back.astype(jnp.float32).reshape(width, -1), 0)
    normal_out = (tri_hat * out_gain[:, None] + out_bias[:, None]).astype(jnp.bfloat16)
    mixed = jnp.einsum("cp,ce->ep", normal_out, out_weight, preferred_element_type=jnp.float32)
    out_gate = jax.nn.sigmoid(blocks[4])
    grad_out = cotangent.astype(jnp.float32).reshape(rows_here * cols_here, width).T
    grad_mixed = (grad_out * out_gate).astype(jnp.bfloat16)
    grad_logit = grad_out * mixed * out_gate * (1.0 - out_gate)
    grad_normal = jnp.einsum(
        "ep,ce->cp", grad_mixed, out_weight, preferred_element_type=jnp.float32
    )
    grad_tri = norm_back(grad_normal * out_gain[:, None], tri_hat, tri_inv, 0)
    grad_tri = grad_tri.astype(jnp.bfloat16).reshape(width, rows_here, cols_here)
    grad_chan = lax.all_to_all(grad_tri, "ch", split_axis=0, concat_axis=2, tiled=True)
    grad_cols = lax.all_to_all(grad_chan, "row", split_axis=2, concat_axis=1, tiled=True)
    grad_left = jnp.einsum(
        "cij,cjk->cik",
        grad_chan,
        lax.all_gather(right_chan, "row", axis=1, tiled=True),
        preferred_element_type=jnp.float32,
    )
    grad_right = jnp.einsum(
        "cij,cik->cjk",
        grad_cols,
        lax.all_gather(left_chan, "row", axis=1, tiled=True),
        preferred_element_type=jnp.float32,
    )
    left_back, right_back = (
        lax.all_to_all(
            grad_left.astype(jnp.bfloat16), "ch", split_axis=2, concat_axis=0, tiled=True
        ),
        lax.all_to_all(
            grad_right.astype(jnp.bfloat16), "ch", split_axis=2, concat_axis=0, tiled=True
        ),
    )
    left_grad = left_back.astype(jnp.float32).reshape(width, -1)
    right_grad = right_back.astype(jnp.float32).reshape(width, -1)
    grad_proj = jnp.concatenate(
        [
            left_grad * left_sig,
            left_grad * blocks[0] * left_sig * (1.0 - left_sig),
            right_grad * right_sig,
            right_grad * blocks[2] * right_sig * (1.0 - right_sig),
            grad_logit,
        ],
        axis=0,
    ).astype(jnp.bfloat16)
    grad_in = jnp.einsum("ep,de->pd", grad_proj, proj_weight, preferred_element_type=jnp.float32)
    grad_pair = norm_back(grad_in * in_gain, normed, scale_inv, -1)
    return grad_pair.astype(jnp.bfloat16).reshape(rows_here, cols_here, width)


def solution(mesh):
    n_row, n_ch = mesh.shape["row"], mesh.shape["ch"]
    placed = (P("row", "ch", None), P("row", "ch", None), P(), P(), P(), P(), P(), P())

    def on_device(*args):
        rows, cols, width = args[0].shape
        devices, outer, group = n_row * n_ch, math.isqrt(n_row), BLOCK // rows
        if (
            devices & (devices - 1) == 0
            and n_row >= 4
            and n_row % outer == 0
            and (devices // outer) % (2 * n_ch) == 0
            and outer % 2 == 0
            and width % (devices // 2) == 0
            and rows % (2 * PARTS) == 0
            and BLOCK % rows == 0
            and group % (width // (devices // 2)) == 0
            and width % (2 * group) == 0
            and cols % 128 == 0
            and width <= 256
            and width & (width - 1) == 0
        ):
            return by_channel(n_row, n_ch, *args)
        return by_row(*args)

    return jax.shard_map(
        on_device, mesh=mesh, in_specs=placed, out_specs=P("row", "ch", None), check_vma=False
    )
```
